32 devices in a mesh: dp: 2 (over y), seq: 4 (over x, core), heads: 4 (over z).
Axes of the slice: x: 2, y: 2, z: 4, core: 2. Of those that a mesh axis runs over, the one named last changes fastest.
Arguments:
- tokens: bfloat16 [2, 2, 2048, 2048], P(None, 'dp', ('seq', 'heads')), may hold values from -6 to 6
- lengths: int32 [2, 2, 3], P(None, 'dp'), may hold values from 1 to 2046, as said below
- attention_gain: bfloat16 [2048], P(('dp', 'seq', 'heads')), may hold values from 0.5 to 1.5
- query_weight: bfloat16 [2048, 1792], P(('dp', 'seq'), 'heads'), may hold values from -0.125 to 0.125
- key_value_matrix: bfloat16 [2048, 896], P(('dp', 'seq', 'heads')), may hold values from -0.125 to 0.125
- per_head_gains: bfloat16 [128], P(('dp', 'seq', 'heads')), may hold values from 0.5 to 1.5
- output_weight: bfloat16 [1792, 2048], P(None, ('dp', 'seq', 'heads')), may hold values from -2 to 2
- feed_gain: bfloat16 [2048], P(('dp', 'seq', 'heads')), may hold values from 0.5 to 1.5
- gate_weight: bfloat16 [2048, 6400], P(('dp', 'seq'), 'heads'), may hold values from -0.125 to 0.125
- up_weight: bfloat16 [2048, 6400], P(('dp', 'seq'), 'heads'), may hold values from -0.125 to 0.125
- down_weight: bfloat16 [6400, 2048], P('heads', ('dp', 'seq')), may hold values from -0.078125 to 0.078125
- cotangent: bfloat16 [2, 2, 2048, 2048], P(None, 'dp', ('seq', 'heads')), may hold values from -6 to 6
Outputs:
- layer_out: bfloat16 [2, 2, 2048, 2048], P(None, 'dp', ('seq', 'heads'))
- tokens_grad: float32 [2, 2, 2048, 2048], P(None, 'dp', ('seq', 'heads'))
- attention_gain_grad: float32 [2048], P(('dp', 'seq', 'heads'))
- query_weight_grad: float32 [2048, 1792], P(('dp', 'seq'), 'heads')
- key_value_weight_grad: float32 [2048, 896], P(('dp', 'seq', 'heads'))
- head_gains_grad: float32 [128], P(('dp', 'seq', 'heads'))
- output_weight_grad: float32 [1792, 2048], P(None, ('dp', 'seq', 'heads'))
- feed_gain_grad: float32 [2048], P(('dp', 'seq', 'heads'))
- gate_weight_grad: float32 [2048, 6400], P(('dp', 'seq'), 'heads')
- up_weight_grad: float32 [2048, 6400], P(('dp', 'seq'), 'heads')
- down_weight_grad: float32 [6400, 2048], P('heads', ('dp', 'seq'))
The draws below stay inside these ranges and needn't reach their ends.
Inputs may be any that keep to these rules, and one draw needn't show every extreme that they name: In each packed row the 3 lengths sum to 2048; the first and the last are shorter than 512, the middle one holds the rest.
All inputs are finite; a program needn't handle non-finite values.
Results may differ from the reference program's by a relative error of at most 0.019.
Values may be sent and summed in bfloat16 or wider, within the bound.
No kernel may reach another device: no remote copies, remote signals or barrier semaphores. Data moves between devices by JAX's collectives and lax.ppermute only.
A program may use at most 320 MiB of HBM per device.

```python
import math
import jax
import jax.numpy as jnp
from jax import lax

MODEL_WIDTH = 2048
QUERY_HEADS = 28
KEY_VALUE_HEADS = 7
HEAD_SIZE = 64
FF = 6400
MB = 2
DOCS = 3
BLK = 512
PACKED_TOKENS = 2048
PACKS = 2


def draw_lengths(key, part):
    key = jax.random.fold_in(key, 11)
    first_key, last_key, pick_key = jax.random.split(key, 3)
    count = MB * PACKS
    leading = jax.random.randint(first_key, (count,), 1, BLK)
    trailing_start = jax.random.randint(last_key, (count,), PACKED_TOKENS - BLK + 1, PACKED_TOKENS)
    chosen = jax.random.randint(pick_key, (), 0, count)
    row_numbers = jnp.arange(count)
    leading = jnp.where(row_numbers == chosen, 1, leading)
    trailing_start = jnp.where(row_numbers == chosen, PACKED_TOKENS - 1, trailing_start)
    sizes = jnp.stack([leading, trailing_start - leading, PACKED_TOKENS - trailing_start], axis=-1)
    return sizes.reshape(MB, PACKS, DOCS).astype(jnp.int32)


def levels(stream_key, shape, cuts, low, largest):
    def one(position, blocks):
        steps = jax.random.uniform(jax.random.fold_in(jax.random.fold_in(stream_key, 6), position), (blocks,), jnp.float32, low / len(cuts), largest / len(cuts))
        return jnp.repeat(jnp.exp(steps), shape[position] // blocks).reshape((-1,) + (1,) * (len(shape) - position - 1))

    level = one(*cuts[0])
    for cut in cuts[1:]:
        level = level * one(*cut)
    return level


def centred(own_key, extent, width, limit, cuts=(), kind=jnp.bfloat16):
    values = jax.random.normal(own_key, extent, jnp.float32) * width
    if len(cuts) > 0:
        values = levels(own_key, extent, cuts, -0.22, 0.18) * values
    return jnp.clip(values, min=-limit, max=limit).astype(kind)


def setup_inputs(seed: int = 0) -> dict:
    arg_keys = jax.random.split(jax.random.key(seed), 13)
    tokens = centred(arg_keys[0], (MB, PACKS, PACKED_TOKENS, MODEL_WIDTH), 1.0, 6.0, ((1, 2), (2, 16)))
    lengths = draw_lengths(jax.random.fold_in(arg_keys[12], 71), 0)
    attention_gain = jnp.clip(1.0 + 0.1 * jax.random.normal(arg_keys[2], (MODEL_WIDTH,), jnp.float32), 0.5, 1.5).astype(jnp.bfloat16)
    query_weight = centred(arg_keys[3], (MODEL_WIDTH, QUERY_HEADS * HEAD_SIZE), MODEL_WIDTH ** -0.5, 0.125, ((0, 8), (1, 4)))
    key_value_matrix = centred(arg_keys[4], (MODEL_WIDTH, 2 * KEY_VALUE_HEADS * HEAD_SIZE), MODEL_WIDTH ** -0.5, 0.125, ((0, 32),))
    per_head_gains = jnp.clip(1.0 + 0.1 * jax.random.normal(arg_keys[5], (2 * HEAD_SIZE,), jnp.float32), 0.5, 1.5).astype(jnp.bfloat16)
    output_weight = centred(arg_keys[6], (QUERY_HEADS * HEAD_SIZE, MODEL_WIDTH), (QUERY_HEADS * HEAD_SIZE // 256) ** -0.5, 2.0, ((1, 32),))
    feed_gain = jnp.clip(1.0 + 0.1 * jax.random.normal(arg_keys[7], (MODEL_WIDTH,), jnp.float32), 0.5, 1.5).astype(jnp.bfloat16)
    gate_weight = centred(arg_keys[8], (MODEL_WIDTH, FF), MODEL_WIDTH ** -0.5, 0.125, ((0, 8), (1, 4)))
    up_weight = centred(arg_keys[9], (MODEL_WIDTH, FF), MODEL_WIDTH ** -0.5, 0.125, ((0, 8), (1, 4)))
    down_weight = centred(arg_keys[10], (FF, MODEL_WIDTH), FF ** -0.5, 0.078125, ((0, 4), (1, 8)))
    cotangent = centred(arg_keys[11], (MB, PACKS, PACKED_TOKENS, MODEL_WIDTH), 1.0, 6.0, ((1, 2), (2, 16)))
    return dict(tokens=tokens, lengths=lengths, attention_gain=attention_gain, query_weight=query_weight, key_value_matrix=key_value_matrix, per_head_gains=per_head_gains, output_weight=output_weight, feed_gain=feed_gain, gate_weight=gate_weight, up_weight=up_weight, down_weight=down_weight, cotangent=cotangent)


EPSILON = 1e-06
SCORE_SCALE = 0.125
MASKED = -1e+30

@jax.custom_vjp
def reduced_precision(v):
    return lax.optimization_barrier(v.astype(jnp.bfloat16)).astype(jnp.float32)

@jax.custom_vjp
def low_back(v):
    return v

def low_keep(v):
    return (reduced_precision(v), None)

def low_pass(kept, grad):
    return (grad,)

def back_keep(v):
    return (v, None)

def back_low(kept, grad):
    return (reduced_precision(grad),)
reduced_precision.defvjp(low_keep, low_pass)
low_back.defvjp(back_keep, back_low)

def matmul(left, right):
    return jnp.dot(left, right, precision=lax.Precision.HIGHEST, preferred_element_type=jnp.float32)

def apply_norm(values, gain):
    return values * lax.rsqrt(lax.optimization_barrier(jnp.mean(values * values, axis=-1, keepdims=True)) + EPSILON) * gain

def rotary_tables(places):
    half_width = HEAD_SIZE // 2
    freqs = jnp.exp(jnp.arange(half_width, dtype=jnp.float32) * (-2.0 * math.log(10000.0) / HEAD_SIZE))
    angles = places.astype(jnp.float32)[:, None] * freqs[None, :]
    cosine_table = jnp.cos(angles)
    sine_table = jnp.sin(angles)
    return (jnp.concatenate([cosine_table, cosine_table], -1)[:, None, :], jnp.concatenate([sine_table, sine_table], -1)[:, None, :])

def apply_rotary(values, cosine_table, sine_table):
    half_width = values.shape[-1] // 2
    turned = jnp.concatenate([-values[..., half_width:], values[..., :half_width]], -1)
    return values * cosine_table + turned * sine_table

def documents(sizes, total):
    finish = jnp.cumsum(sizes).astype(jnp.int32)
    begin = finish - sizes
    places = jnp.arange(total, dtype=jnp.int32)
    segment = lax.optimization_barrier(jnp.sum((places[:, None] >= finish[None, :]).astype(jnp.int32), axis=1))
    member = segment[:, None] == jnp.arange(sizes.shape[0], dtype=jnp.int32)[None, :]
    offset = places - lax.optimization_barrier(jnp.sum(jnp.where(member, begin[None, :], 0), axis=1)).astype(jnp.int32)
    return (segment, offset)

def row_forward(item, params):
    residual_in, segment, offset = item
    attention_gain, query_weight, key_value_matrix, per_head_gains, output_weight, feed_gain, gate_weight, up_weight, down_weight = params
    normed = reduced_precision(apply_norm(residual_in, attention_gain))
    query_raw = low_back(matmul(normed, query_weight))
    key_value_projected = low_back(matmul(normed, key_value_matrix))
    cosine_table, sine_table = rotary_tables(offset)
    key_total_width = KEY_VALUE_HEADS * HEAD_SIZE
    query_rows = reduced_precision(apply_rotary(apply_norm(query_raw.reshape(PACKED_TOKENS, QUERY_HEADS, HEAD_SIZE), per_head_gains[:HEAD_SIZE]), cosine_table, sine_table))
    every_key = reduced_precision(apply_rotary(apply_norm(key_value_projected[:, :key_total_width].reshape(PACKED_TOKENS, KEY_VALUE_HEADS, HEAD_SIZE), per_head_gains[HEAD_SIZE:]), cosine_table, sine_table))
    every_value = reduced_precision(key_value_projected[:, key_total_width:].reshape(PACKED_TOKENS, KEY_VALUE_HEADS, HEAD_SIZE))
    places = jnp.arange(PACKED_TOKENS, dtype=jnp.int32)
    allowed = (segment[:, None] == segment[None, :]) & (places[None, :] <= places[:, None])
    heads_per_group = QUERY_HEADS // KEY_VALUE_HEADS
    grouped_heads = query_rows.reshape(PACKED_TOKENS, KEY_VALUE_HEADS, heads_per_group, HEAD_SIZE).transpose(1, 0, 2, 3)

    def head_block(pieces):
        query_block, key_block, value_block = pieces
        scores = low_back(jnp.einsum('qjh,kh->jqk', query_block, key_block, precision=lax.Precision.HIGHEST) * SCORE_SCALE)
        scores = jnp.where(allowed[None], scores, MASKED)
        peak = lax.optimization_barrier(jnp.max(scores, axis=-1, keepdims=True))
        expo = jnp.exp(scores - peak)
        probs = expo / lax.optimization_barrier(jnp.sum(expo, axis=-1, keepdims=True))
        mixed = jnp.einsum('jqk,kh->qjh', reduced_precision(probs), value_block, precision=lax.Precision.HIGHEST)
        return reduced_precision(low_back(mixed))
    mixed = lax.map(jax.checkpoint(head_block), (grouped_heads, every_key.transpose(1, 0, 2), every_value.transpose(1, 0, 2)))
    mixed = mixed.transpose(1, 0, 2, 3).reshape(PACKED_TOKENS, QUERY_HEADS * HEAD_SIZE)
    hidden_in = residual_in + low_back(matmul(mixed, output_weight))
    feed_normed = reduced_precision(apply_norm(hidden_in, feed_gain))
    gate_pre = low_back(matmul(feed_normed, gate_weight))
    up_pre = low_back(matmul(feed_normed, up_weight))
    activated = reduced_precision(jax.nn.silu(gate_pre) * up_pre)
    return hidden_in + low_back(matmul(activated, down_weight))

def reference(tokens, lengths, attention_gain, query_weight, key_value_matrix, per_head_gains, output_weight, feed_gain, gate_weight, up_weight, down_weight, cotangent):
    params = tuple((weight.astype(jnp.float32) for weight in (attention_gain, query_weight, key_value_matrix, per_head_gains, output_weight, feed_gain, gate_weight, up_weight, down_weight)))
    segments, offsets = jax.vmap(lambda sizes: documents(sizes, PACKED_TOKENS))(lengths.reshape(MB * PACKS, DOCS))

    def forward(inputs, *weights):
        packed = inputs.reshape(MB * PACKS, PACKED_TOKENS, MODEL_WIDTH)
        result = lax.map(jax.checkpoint(lambda item: row_forward(item, weights)), (packed, segments, offsets))
        return result.reshape(inputs.shape)
    outputs, pullback = jax.vjp(forward, tokens.astype(jnp.float32), *params)
    grads = pullback(cotangent.astype(jnp.float32))
    return (outputs.astype(jnp.bfloat16), grads[0], grads[1], grads[2], grads[3], grads[4], grads[5], grads[6], grads[7], grads[8], grads[9])
```

```python
import math

import jax
import jax.numpy as jnp
from jax import lax
from jax.experimental import pallas as pl
from jax.experimental.pallas import tpu as pltpu
from jax.sharding import PartitionSpec as P

QUERY_HEADS = 28
KEY_VALUE_HEADS = 7
HEAD_SIZE = 64
GROUP = QUERY_HEADS // KEY_VALUE_HEADS

EPSILON = 1e-06
SCORE_SCALE = 0.125
MASKED = -1e30
LANES = 128
CHUNK = 256

BF = jnp.bfloat16
F32 = jnp.float32


def dot_nn(left, right):
    return lax.dot_general(left, right, (((1,), (0,)), ((), ())), preferred_element_type=F32)


def dot_nt(left, right):
    return lax.dot_general(left, right, (((1,), (1,)), ((), ())), preferred_element_type=F32)


def dot_tn(left, right):
    return lax.dot_general(left, right, (((0,), (0,)), ((), ())), preferred_element_type=F32)


def pad_heads(tile, low, keep_low):
    rows = tile.shape[0]
    parts = []
    for pair in range(GROUP // 2):
        both = tile[:, pair * LANES : (pair + 1) * LANES].astype(F32)
        turned = pltpu.roll(both, HEAD_SIZE, 1)
        first, second = (both, turned) if keep_low else (turned, both)
        keep = low[:rows] if keep_low else jnp.logical_not(low[:rows])
        parts.append(jnp.where(keep, first, 0.0))
        parts.append(jnp.where(keep, second, 0.0))
    return jnp.concatenate(parts, axis=0).astype(BF)


def four_wide(row):
    return jnp.concatenate([row] * GROUP, axis=1)


def heads_back(stacked, rows):
    parts = []
    for pair in range(GROUP // 2):
        start = 2 * pair * rows
        both = jnp.concatenate(
            [stacked[:, start : start + rows], stacked[:, start + rows : start + 2 * rows]], axis=0
        )
        parts.append(both.T)
    return jnp.concatenate(parts, axis=1)


def attention_forward_kernel(kv0, kv1, query, bias0, bias1, mixed, lse, expo):
    rows = query.shape[0]
    half = kv0.shape[0]
    low = lax.broadcasted_iota(jnp.int32, (half, LANES), 1) < HEAD_SIZE
    padded = pad_heads(query[...], low, True)
    for part, (kv, bias) in enumerate(((kv0, bias0), (kv1, bias1))):
        for step in range(half // CHUNK):
            span = pl.ds(step * CHUNK, CHUNK)
            scores = dot_nt(kv[span, :], padded)
            weight = jnp.exp(scores + four_wide(bias[span, :]))
            expo[pl.ds(part * half + step * CHUNK, CHUNK), :] = weight.astype(BF)
    total = dot_tn(
        jnp.where(low, 1.0, kv0[...].astype(F32)).astype(BF), expo[pl.ds(0, half), :]
    ) + dot_tn(jnp.where(low, 1.0, kv1[...].astype(F32)).astype(BF), expo[pl.ds(half, half), :])
    lse[...] = jnp.log(total[0:1, :])[None]
    mixed[...] = heads_back(total[HEAD_SIZE:, :] / total[:HEAD_SIZE, :], rows).astype(BF)


def attention_backward_kernel(
    kv0, kv1, query, mixed, d_mixed, bias0, bias1, lse, d_query, d_kv0, d_kv1, d_scores
):
    rows = query.shape[0]
    half = kv0.shape[0]
    low = lax.broadcasted_iota(jnp.int32, (rows, LANES), 1) < HEAD_SIZE
    padded = pad_heads(query[...], low, True)
    d_padded = pad_heads(d_mixed[...], low, False)
    product = d_mixed[...].astype(F32) * mixed[...].astype(F32)
    pick = (
        lax.broadcasted_iota(jnp.int32, (8, GROUP * HEAD_SIZE), 1) // HEAD_SIZE
        == lax.broadcasted_iota(jnp.int32, (8, GROUP * HEAD_SIZE), 0)
    ).astype(F32)
    balance = lax.dot_general(
        pick,
        product,
        (((1,), (1,)), ((), ())),
        precision=lax.Precision.HIGHEST,
        preferred_element_type=F32,
    )
    balance = jnp.concatenate([balance[head : head + 1, :] for head in range(GROUP)], axis=1)
    level = lse[0]
    for part, (kv, bias, d_kv) in enumerate(((kv0, bias0, d_kv0), (kv1, bias1, d_kv1))):
        for step in range(half // CHUNK):
            span = pl.ds(step * CHUNK, CHUNK)
            block = kv[span, :]
            scores = dot_nt(block, padded)
            probs = jnp.exp(scores + four_wide(bias[span, :]) - level)
            d_probs = dot_nt(block, d_padded)
            low_scores = (probs * (d_probs - balance)).astype(BF)
            d_scores[pl.ds(part * half + step * CHUNK, CHUNK), :] = low_scores
            d_kv[span, :] = (
                dot_nn(low_scores, padded) + dot_nn(probs.astype(BF), d_padded)
            ).astype(BF)
    total = dot_tn(kv0[...], d_scores[pl.ds(0, half), :]) + dot_tn(
        kv1[...], d_scores[pl.ds(half, half), :]
    )
    d_query[...] = heads_back(total[:HEAD_SIZE, :] * SCORE_SCALE, rows)


def attention_forward(kv0, kv1, query, bias0, bias1):
    half, rows = bias0.shape
    wide = GROUP * rows
    keys = pl.BlockSpec((half, LANES), lambda c: (0, c))
    heads = pl.BlockSpec((rows, GROUP * HEAD_SIZE), lambda c: (0, c))
    fixed = pl.BlockSpec((half, rows), lambda c: (0, 0))
    return pl.pallas_call(
        attention_forward_kernel,
        grid=(KEY_VALUE_HEADS,),
        in_specs=[keys, keys, heads, fixed, fixed],
        out_specs=[heads, pl.BlockSpec((1, 1, wide), lambda c: (c, 0, 0))],
        out_shape=[
            jax.ShapeDtypeStruct(query.shape, BF),
            jax.ShapeDtypeStruct((KEY_VALUE_HEADS, 1, wide), F32),
        ],
        scratch_shapes=[pltpu.VMEM((2 * half, wide), BF)],
        compiler_params=pltpu.CompilerParams(
            dimension_semantics=("arbitrary",), vmem_limit_bytes=48 * 1024 * 1024
        ),
        cost_estimate=pl.CostEstimate(
            flops=KEY_VALUE_HEADS * 2 * half * wide * LANES * 4 * 2,
            bytes_accessed=2 * half * 896 * 2 + rows * 1792 * 4,
            transcendentals=KEY_VALUE_HEADS * 2 * half * wide,
        ),
        name="attention_forward",
    )(kv0, kv1, query, bias0, bias1)


def attention_backward(kv0, kv1, query, mixed, d_mixed, bias0, bias1, lse):
    half, rows = bias0.shape
    wide = GROUP * rows
    keys = pl.BlockSpec((half, LANES), lambda c: (0, c))
    heads = pl.BlockSpec((rows, GROUP * HEAD_SIZE), lambda c: (0, c))
    fixed = pl.BlockSpec((half, rows), lambda c: (0, 0))
    return pl.pallas_call(
        attention_backward_kernel,
        grid=(KEY_VALUE_HEADS,),
        in_specs=[
            keys,
            keys,
            heads,
            heads,
            heads,
            fixed,
            fixed,
            pl.BlockSpec((1, 1, wide), lambda c: (c, 0, 0)),
        ],
        out_specs=[heads, keys, keys],
        out_shape=[
            jax.ShapeDtypeStruct(query.shape, F32),
            jax.ShapeDtypeStruct(kv0.shape, BF),
            jax.ShapeDtypeStruct(kv1.shape, BF),
        ],
        scratch_shapes=[pltpu.VMEM((2 * half, wide), BF)],
        compiler_params=pltpu.CompilerParams(
            dimension_semantics=("arbitrary",), vmem_limit_bytes=48 * 1024 * 1024
        ),
        cost_estimate=pl.CostEstimate(
            flops=KEY_VALUE_HEADS * 2 * half * wide * LANES * 10 * 2,
            bytes_accessed=2 * half * 896 * 4 + rows * 1792 * 10,
            transcendentals=KEY_VALUE_HEADS * 2 * half * wide,
        ),
        name="attention_backward",
    )(kv0, kv1, query, mixed, d_mixed, bias0, bias1, lse)


def norm_scale(values):
    return lax.rsqrt(jnp.mean(values * values, axis=-1, keepdims=True) + EPSILON)


def apply_norm(values, gain):
    return values * norm_scale(values) * gain


def norm_back(values, gain, grad):
    scale = norm_scale(values)
    lifted = grad * gain
    dots = jnp.mean(values * lifted, axis=-1, keepdims=True)
    d_values = scale * lifted - values * (scale * scale * scale) * dots
    return d_values, jnp.sum(grad * values * scale, axis=tuple(range(values.ndim - 1)))


def rotary_tables(places):
    half_width = HEAD_SIZE // 2
    freqs = jnp.exp(
        jnp.arange(half_width, dtype=F32) * (-2.0 * math.log(10000.0) / HEAD_SIZE)
    )
    angles = places.astype(F32)[:, None] * freqs[None, :]
    cosine_table = jnp.cos(angles)
    sine_table = jnp.sin(angles)
    return (
        jnp.concatenate([cosine_table, cosine_table], -1)[:, None, :],
        jnp.concatenate([sine_table, sine_table], -1)[:, None, :],
    )


def apply_rotary(values, cosine_table, sine_table):
    half_width = values.shape[-1] // 2
    turned = jnp.concatenate([-values[..., half_width:], values[..., :half_width]], -1)
    return values * cosine_table + turned * sine_table


def on_device(
    tokens,
    lengths,
    attention_gain,
    query_weight,
    key_value_matrix,
    per_head_gains,
    output_weight,
    feed_gain,
    gate_weight,
    up_weight,
    down_weight,
    cotangent,
):
    batches = tokens.shape[0]
    rows = tokens.shape[2]
    width = tokens.shape[3]
    dp_size = lax.axis_size("dp")
    seq_size = lax.axis_size("seq")
    heads_size = lax.axis_size("heads")
    assert seq_size == 4 and heads_size == 4
    paired = dp_size == 2
    y = lax.axis_index("dp")
    s = lax.axis_index("seq")
    z = lax.axis_index("heads")
    x = s // 2
    core = s % 2
    kv_width = 2 * KEY_VALUE_HEADS * HEAD_SIZE
    q_width = QUERY_HEADS * HEAD_SIZE

    def swap_x(v):
        return lax.ppermute(v, "seq", [(i, i ^ 2) for i in range(4)])

    def swap_core(v):
        return lax.ppermute(v, "seq", [(i, i ^ 1) for i in range(4)])

    def swap_y(v):
        return lax.ppermute(v, "dp", [(0, 1), (1, 0)])

    def line_gather(v):
        up = [(0, 1), (1, 2), (2, 3)]
        down = [(1, 0), (2, 1), (3, 2)]
        u1 = lax.ppermute(v, "heads", up)
        d1 = lax.ppermute(v, "heads", down)
        u2 = lax.ppermute(u1, "heads", up[1:])
        d2 = lax.ppermute(d1, "heads", down[:-1])
        far = lax.ppermute(jnp.where(z == 1, d2, u2), "heads", [(1, 0), (2, 3)])
        table = ((v, u1, u2, far), (d1, v, u1, u2), (d2, d1, v, u1), (far, d2, d1, v))
        return jnp.stack([lax.select_n(z, *row) for row in table], axis=0)

    def gather_yx(v, x_first):
        def along_x(u):
            return jnp.stack([u, swap_x(u)], axis=-3)

        def along_y(u):
            if paired:
                return jnp.stack([u, swap_y(u)], axis=0)
            return lax.all_gather(u, "dp", axis=0)

        return along_y(along_x(v)) if x_first else along_x(along_y(v))

    def scatter_yx(g, x_last):
        def along_x(u):
            return u[..., 0, :, :] + swap_x(u[..., 1, :, :])

        def along_y(u):
            if paired:
                return u[0] + swap_y(u[1])
            return lax.psum_scatter(u, "dp", scatter_dimension=0)

        return along_x(along_y(g)) if x_last else along_y(along_x(g))

    blocks = 2 * dp_size
    piece = width // blocks

    def relative(v):
        cut = [v[..., i * piece : (i + 1) * piece] for i in range(blocks)]
        place = 2 * y + x if paired else x
        ways = 4 if paired else 2
        place = place.astype(jnp.int32)
        return jnp.concatenate(
            [lax.select_n(place, *[cut[i ^ m] for m in range(ways)]) for i in range(blocks)], axis=-1
        )

    def split_core(v):
        u = v.reshape(v.shape[:-1] + (blocks, 2, piece // 2))
        first, second = u[..., 0, :], u[..., 1, :]
        flat = v.shape[:-1] + (width // 2,)
        mine = jnp.where(core == 0, first, second).reshape(flat)
        other = jnp.where(core == 0, second, first).reshape(flat)
        return mine, other

    def merge_core(mine, other):
        shape = mine.shape[:-1] + (blocks, piece // 2)
        mine, other = mine.reshape(shape), other.reshape(shape)
        first = jnp.where(core == 0, mine, other)
        second = jnp.where(core == 0, other, mine)
        return jnp.stack([first, second], axis=-2).reshape(shape[:-2] + (width,))

    small = key_value_matrix.shape[0]
    per_head = per_head_gains.shape[0]
    kv_local = (
        key_value_matrix.reshape(small, 2, KEY_VALUE_HEADS, HEAD_SIZE)
        .transpose(0, 2, 1, 3)
        .reshape(small, kv_width)
    )
    gains_local = jnp.stack(
        [attention_gain, feed_gain, jnp.pad(per_head_gains, (0, small - per_head))], axis=1
    )
    kvg_local = jnp.concatenate(
        [kv_local, jnp.pad(gains_local, ((0, 0), (0, LANES - gains_local.shape[1])))], axis=1
    )
    kvg_rows = line_gather(kvg_local).reshape(4 * small, kv_width + LANES)
    kvg_mine = gather_yx(kvg_rows, True).reshape(width // 2, kv_width + LANES)
    kvg_other = swap_core(kvg_mine)

    q_part = query_weight.shape[1]
    q_rows = (
        line_gather(query_weight).transpose(1, 0, 2).reshape(query_weight.shape[0], q_width)
    )
    q_mine = gather_yx(q_rows, False).reshape(width // 2, q_width)
    q_other = swap_core(q_mine)

    o_rows = line_gather(output_weight.T).reshape(4 * small, q_width)
    o_mine = gather_yx(o_rows, True).reshape(width // 2, q_width)
    o_other = swap_core(o_mine)

    kv_mine, kv_other = kvg_mine[:, :kv_width], kvg_other[:, :kv_width]
    gains = merge_core(kvg_mine[:, kv_width:].T[:3], kvg_other[:, kv_width:].T[:3]).astype(F32)
    attention_scale = gains[0:1]
    feed_scale = gains[1:2]
    head_scale = relative(gains[2:3]).reshape(-1, small)[:, :per_head].reshape(-1)
    query_scale = head_scale[:HEAD_SIZE]
    key_scale = head_scale[HEAD_SIZE:]

    hidden_part = gate_weight.shape[1] // 2

    def unit_half(v, which):
        return jnp.where(which == 0, v[:, :hidden_part], v[:, hidden_part:])

    down_local = down_weight.T
    three = (gate_weight, up_weight, down_local)
    keep = jnp.concatenate([unit_half(v, core) for v in three], axis=1)
    give = jnp.concatenate([unit_half(v, 1 - core) for v in three], axis=1)
    take = swap_core(give)
    ffn_rows = jnp.where(
        core == 0,
        jnp.concatenate([keep, take], axis=0),
        jnp.concatenate([take, keep], axis=0),
    )
    gate_up = gather_yx(ffn_rows[:, : 2 * hidden_part], True).reshape(width, 2 * hidden_part)
    down = gather_yx(ffn_rows[:, 2 * hidden_part :], False).reshape(width, hidden_part)

    row_length = rows * heads_size * seq_size
    block_rows = rows * heads_size
    places = s * block_rows + z * rows + jnp.arange(rows, dtype=jnp.int32)
    inside = jnp.arange(block_rows, dtype=jnp.int32)

    def key_places(first):
        return jnp.concatenate([first * block_rows + inside, (first ^ 2) * block_rows + inside])

    def bias_for(begin, first):
        keys = key_places(first)[:, None]
        return jnp.where((keys <= places[None, :]) & (keys >= begin[None, :]), 0.0, MASKED)

    begins, biases = [], []
    for batch in range(batches):
        sizes = lengths[batch, 0]
        finish = jnp.cumsum(sizes)
        begin = jnp.sum(
            jnp.where(places[:, None] >= finish[None, :], sizes[None, :], 0), axis=1
        ).astype(jnp.int32)
        begins.append(begin)
        biases.append((bias_for(begin, s), bias_for(begin, s ^ 1)))
    offsets = jnp.concatenate([places - begin for begin in begins])
    cosine_table, sine_table = rotary_tables(offsets)

    residual_in = relative(tokens[:, 0].reshape(batches * rows, width)).astype(F32)
    out_cotangent = relative(cotangent[:, 0].reshape(batches * rows, width))
    normed = apply_norm(residual_in, attention_scale).astype(BF)
    normed_mine, normed_other = split_core(normed)
    kv_raw = dot_nn(normed_mine, kv_mine) + dot_nn(normed_other, kv_other)

    def prepare(raw, gain):
        heads = raw.reshape(raw.shape[0], -1, HEAD_SIZE)
        return apply_rotary(apply_norm(heads, gain), cosine_table, sine_table)

    kv_heads = kv_raw.reshape(-1, KEY_VALUE_HEADS, 2, HEAD_SIZE)
    key_raw = kv_heads[:, :, 0]
    keys_float = prepare(key_raw, key_scale)
    kv_low = (
        jnp.stack([keys_float, kv_heads[:, :, 1]], axis=2).reshape(-1, kv_width).astype(BF)
    )
    q_raw = dot_nn(normed_mine, q_mine) + dot_nn(normed_other, q_other)
    queries_float = prepare(q_raw, query_scale)
    queries = (queries_float * SCORE_SCALE).astype(BF).reshape(-1, q_width)

    def every_kv(v):
        pair = jnp.stack([v, swap_x(v)], axis=0).reshape(2 * rows, kv_width)
        lined = lax.all_gather(pair, "heads", axis=0)
        mine = (
            lined.reshape(heads_size, 2, rows, kv_width)
            .transpose(1, 0, 2, 3)
            .reshape(2 * block_rows, kv_width)
        )
        return mine, swap_core(mine)

    feeds, mixeds, lses, kvs, hiddens = [], [], [], [], []
    for batch in range(batches):
        span = slice(batch * rows, (batch + 1) * rows)
        kv0, kv1 = every_kv(kv_low[span])
        mixed, lse = attention_forward(kv0, kv1, queries[span], *biases[batch])
        hidden_in = residual_in[span] + merge_core(dot_nt(mixed, o_mine), dot_nt(mixed, o_other))
        feed_rows = apply_norm(hidden_in, feed_scale).astype(BF)
        feed_mine = lax.all_gather(feed_rows, "heads", axis=0, tiled=True)
        feeds.append((feed_mine, swap_core(feed_mine)))
        mixeds.append(mixed)
        lses.append(lse)
        kvs.append((kv0, kv1))
        hiddens.append(hidden_in)

    def hidden_units(feed):
        both = dot_nn(feed, gate_up)
        return both[:, :hidden_part], both[:, hidden_part:]

    layer_rows, d_feeds, acts, d_gate_ups, cots = [], [], [], [], []
    for batch in range(batches):
        span = slice(batch * rows, (batch + 1) * rows)
        cot_mine = lax.all_gather(out_cotangent[span], "heads", axis=0, tiled=True)
        cot_pair = (cot_mine, swap_core(cot_mine))
        outs = []
        for feed, cot in zip(feeds[batch], cot_pair):
            gate_pre, up_pre = hidden_units(feed)
            sig = jax.nn.sigmoid(gate_pre)
            silu = gate_pre * sig
            act = (silu * up_pre).astype(BF)
            d_act = dot_nn(cot, down)
            d_gate = d_act * up_pre * sig * (1.0 + gate_pre * (1.0 - sig))
            d_up = d_act * silu
            d_gate_up = jnp.concatenate([d_gate, d_up], axis=1).astype(BF)
            out = dot_nt(act, down).astype(BF)
            d_feed = dot_nt(d_gate_up, gate_up).astype(BF)
            acts.append(act)
            d_gate_ups.append(d_gate_up)
            cots.append(cot)
            outs.append((out, d_feed))
        (out_mine, d_feed_mine), (out_other, d_feed_other) = outs
        d_feed = lax.psum_scatter(
            d_feed_mine + swap_core(d_feed_other), "heads", scatter_dimension=0, tiled=True
        )
        feed_out = lax.psum_scatter(
            out_mine + swap_core(out_other), "heads", scatter_dimension=0, tiled=True
        )
        layer_rows.append((hiddens[batch] + feed_out.astype(F32)).astype(BF))
        d_feeds.append(d_feed.astype(F32))

    feed_all = jnp.concatenate([f for pair in feeds for f in pair], axis=0)
    act_all = jnp.concatenate(acts, axis=0)
    d_gate_up_all = jnp.concatenate(d_gate_ups, axis=0)
    cot_all = jnp.concatenate(cots, axis=0)

    def blocked(g):
        return g.astype(BF).reshape(dp_size, 2, -1, g.shape[-1])

    g_gate_up = scatter_yx(blocked(dot_tn(feed_all, d_gate_up_all)), True)
    g_down = scatter_yx(blocked(dot_tn(cot_all, act_all)), False)
    g_ffn = jnp.concatenate([g_gate_up, g_down], axis=1)
    part_rows = g_ffn.shape[0] // 2
    g_keep = jnp.where(core == 0, g_ffn[:part_rows], g_ffn[part_rows:])
    g_give = jnp.where(core == 0, g_ffn[part_rows:], g_ffn[:part_rows])
    g_take = swap_core(g_give)
    grads_ffn = []
    for index in range(3):
        cut = slice(index * hidden_part, (index + 1) * hidden_part)
        own, got = g_keep[:, cut], g_take[:, cut]
        grads_ffn.append(
            jnp.where(
                core == 0,
                jnp.concatenate([own, got], axis=1),
                jnp.concatenate([got, own], axis=1),
            ).astype(F32)
        )
    grad_gate, grad_up, grad_down = grads_ffn
    grad_down = grad_down.T

    d_hiddens, d_attendeds, d_queries, d_pairs = [], [], [], []
    grad_feed_gain = 0.0
    for batch in range(batches):
        span = slice(batch * rows, (batch + 1) * rows)
        d_norm, grad_gain = norm_back(hiddens[batch], feed_scale, d_feeds[batch])
        grad_feed_gain = grad_feed_gain + grad_gain
        d_hidden = out_cotangent[span].astype(F32) + d_norm
        d_attended = d_hidden.astype(BF)
        d_mine, d_other = split_core(d_attended)
        d_mixed = (dot_nn(d_mine, o_mine) + dot_nn(d_other, o_other)).astype(BF)
        d_query, d_kv0, d_kv1 = attention_backward(
            *kvs[batch], queries[span], mixeds[batch], d_mixed, *biases[batch], lses[batch]
        )
        lined = (d_kv0 + swap_core(d_kv1)).reshape(2, heads_size, rows, kv_width)
        lined = lined.transpose(1, 0, 2, 3).reshape(heads_size * 2 * rows, kv_width)
        pair = lax.psum_scatter(lined, "heads", scatter_dimension=0, tiled=True)
        d_pairs.append(pair[:rows] + swap_x(pair[rows:]))
        d_hiddens.append(d_hidden)
        d_attendeds.append((d_mine, d_other))
        d_queries.append(d_query)

    mixed_all = jnp.concatenate(mixeds, axis=0)
    d_mine_all = jnp.concatenate([pair[0] for pair in d_attendeds], axis=0)
    d_other_all = jnp.concatenate([pair[1] for pair in d_attendeds], axis=0)
    d_hidden_all = jnp.concatenate(d_hiddens, axis=0)
    d_query_all = jnp.concatenate(d_queries, axis=0)
    d_pair_all = jnp.concatenate(d_pairs, axis=0)

    def rows_scatter(mine, other, x_last):
        held = mine.astype(BF) + swap_core(other.astype(BF))
        return scatter_yx(held.reshape(dp_size, 2, -1, held.shape[-1]), x_last)

    g_o = rows_scatter(dot_tn(d_mine_all, mixed_all), dot_tn(d_other_all, mixed_all), True)
    grad_output = lax.psum_scatter(g_o, "heads", scatter_dimension=0, tiled=True).astype(F32).T

    def head_norm_back(raw, gain, grad):
        unused, pull = jax.vjp(prepare, raw, gain)
        return pull(grad)

    d_q_raw, grad_query_gain = head_norm_back(
        q_raw, query_scale, d_query_all.reshape(-1, QUERY_HEADS, HEAD_SIZE)
    )
    d_q_raw = d_q_raw.astype(BF)
    g_q = rows_scatter(dot_tn(normed_mine, d_q_raw), dot_tn(normed_other, d_q_raw), False)
    grad_query = lax.psum_scatter(g_q, "heads", scatter_dimension=1, tiled=True).astype(F32)

    d_kv_heads = d_pair_all.astype(F32).reshape(-1, KEY_VALUE_HEADS, 2, HEAD_SIZE)
    d_key_raw, grad_key_gain = head_norm_back(
        key_raw.reshape(key_raw.shape[0], -1), key_scale, d_kv_heads[:, :, 0]
    )
    d_kv_raw = (
        jnp.stack([d_key_raw.reshape(-1, KEY_VALUE_HEADS, HEAD_SIZE), d_kv_heads[:, :, 1]], axis=2)
        .reshape(-1, kv_width)
        .astype(BF)
    )
    d_normed = merge_core(
        dot_nt(d_q_raw, q_mine) + dot_nt(d_kv_raw, kv_mine),
        dot_nt(d_q_raw, q_other) + dot_nt(d_kv_raw, kv_other),
    )
    d_input, grad_attention_gain = norm_back(residual_in, attention_scale, d_normed)
    input_rows = d_hidden_all + d_input

    head_grads = jnp.concatenate([grad_query_gain, grad_key_gain]).reshape(-1, per_head)
    head_column = relative(jnp.pad(head_grads, ((0, 0), (0, small - per_head))).reshape(1, width))
    gain_mine, gain_other = split_core(
        jnp.concatenate([grad_attention_gain[None], grad_feed_gain[None], head_column], axis=0)
    )

    def with_gains(grad, gain):
        return jnp.concatenate([grad, jnp.pad(gain.T, ((0, 0), (0, LANES - 3)))], axis=1)

    g_kv = rows_scatter(
        with_gains(dot_tn(normed_mine, d_kv_raw), gain_mine),
        with_gains(dot_tn(normed_other, d_kv_raw), gain_other),
        True,
    )
    g_kv = lax.psum_scatter(g_kv, "heads", scatter_dimension=0, tiled=True).astype(F32)
    grad_key_value = (
        g_kv[:, :kv_width]
        .reshape(small, KEY_VALUE_HEADS, 2, HEAD_SIZE)
        .transpose(0, 2, 1, 3)
        .reshape(small, kv_width)
    )

    layer_out = relative(jnp.concatenate(layer_rows, axis=0)).reshape(tokens.shape)
    tokens_grad = relative(input_rows).reshape(tokens.shape)
    return (
        layer_out,
        tokens_grad,
        g_kv[:, kv_width],
        grad_query,
        grad_key_value,
        g_kv[:per_head, kv_width + 2],
        grad_output,
        g_kv[:, kv_width + 1],
        grad_gate,
        grad_up,
        grad_down,
    )


def solution(mesh):
    every = ("dp", "seq", "heads")
    token_spec = P(None, "dp", ("seq", "heads"), None)
    return jax.shard_map(
        on_device,
        mesh=mesh,
        in_specs=(
            token_spec,
            P(None, "dp", None),
            P(every),
            P(("dp", "seq"), "heads"),
            P(every, None),
            P(every),
            P(None, every),
            P(every),
            P(("dp", "seq"), "heads"),
            P(("dp", "seq"), "heads"),
            P("heads", ("dp", "seq")),
            token_spec,
        ),
        out_specs=(
            token_spec,
            token_spec,
            P(every),
            P(("dp", "seq"), "heads"),
            P(every, None),
            P(every),
            P(None, every),
            P(every),
            P(("dp", "seq"), "heads"),
            P(("dp", "seq"), "heads"),
            P("heads", ("dp", "seq")),
        ),
        check_vma=False,
    )
```

```python
import functools
import math

import jax
import jax.numpy as jnp
from jax import lax
from jax.experimental import pallas as pl
from jax.experimental.pallas import tpu as pltpu
from jax.sharding import PartitionSpec as P

QUERY_HEADS = 28
KEY_VALUE_HEADS = 7
HEAD_SIZE = 64
GROUP = QUERY_HEADS // KEY_VALUE_HEADS
GROUP_WIDTH = GROUP * HEAD_SIZE
Q_WIDTH = QUERY_HEADS * HEAD_SIZE
KV_WIDTH = 2 * KEY_VALUE_HEADS * HEAD_SIZE

EPSILON = 1e-06
SCORE_SCALE = 0.125
MASKED = -1e30
LANES = 128
CHUNK = 256
BLOCK = 256
FFN_ROWS = 256
ATTENTION_GAIN, FEED_GAIN, HEAD_GAIN = 0, 1, 2

BF = jnp.bfloat16
F32 = jnp.float32


def dot_nn(left, right):
    return lax.dot_general(left, right, (((1,), (0,)), ((), ())), preferred_element_type=F32)


def dot_nt(left, right):
    return lax.dot_general(left, right, (((1,), (1,)), ((), ())), preferred_element_type=F32)


def dot_tn(left, right):
    return lax.dot_general(left, right, (((0,), (0,)), ((), ())), preferred_element_type=F32)


def shape(dims, kind):
    return jax.ShapeDtypeStruct(dims, kind)


def whole(array):
    dims = array.shape
    return pl.BlockSpec(
        dims, lambda *unused: (0,) * len(dims), pipeline_mode=pl.Buffered(1)
    )


def fixed_out(dims):
    return pl.BlockSpec(dims, lambda *unused: (0,) * len(dims))


def kernel_call(body, name, grid, in_specs, out_specs, out_shape, scratch, flops, table=None):
    outs = out_shape if isinstance(out_shape, (list, tuple)) else [out_shape]
    moved = sum(math.prod(o.shape) * jnp.dtype(o.dtype).itemsize for o in outs)
    kwargs = dict(
        out_shape=out_shape,
        compiler_params=pltpu.CompilerParams(
            dimension_semantics=("arbitrary",) * len(grid), vmem_limit_bytes=56 * 1024 * 1024
        ),
        name=name,
    )

    def call(*operands):
        size = moved + sum(math.prod(o.shape) * o.dtype.itemsize for o in operands)
        cost = pl.CostEstimate(
            flops=flops,
            bytes_accessed=size,
            transcendentals=0,
        )
        if table is None:
            return pl.pallas_call(
                body,
                grid=grid,
                in_specs=in_specs,
                out_specs=out_specs,
                scratch_shapes=scratch,
                cost_estimate=cost,
                **kwargs,
            )(*operands)
        return pl.pallas_call(
            body,
            grid_spec=pltpu.PrefetchScalarGridSpec(
                num_scalar_prefetch=1,
                grid=grid,
                in_specs=in_specs,
                out_specs=out_specs,
                scratch_shapes=scratch,
            ),
            cost_estimate=cost,
            **kwargs,
        )(table, *operands)

    return call


def half_lanes(rows):
    return lax.broadcasted_iota(jnp.int32, (rows, LANES), 1) < HEAD_SIZE


def half_means(values, low):
    first = jnp.sum(jnp.where(low, values, 0.0), axis=1, keepdims=True) / HEAD_SIZE
    second = jnp.sum(jnp.where(low, 0.0, values), axis=1, keepdims=True) / HEAD_SIZE
    return jnp.where(low, first, second)


def turn(values):
    lane = lax.broadcasted_iota(jnp.int32, values.shape, 1)
    early = (lane & (HEAD_SIZE // 2)) == 0
    return jnp.where(
        early, pltpu.roll(values, LANES - HEAD_SIZE // 2, 1), pltpu.roll(values, HEAD_SIZE // 2, 1)
    )


def head_norm(tile, gain, cosine, sine, low):
    normed = tile * lax.rsqrt(half_means(tile * tile, low) + EPSILON) * gain
    return normed * cosine + turn(normed) * sine


def head_norm_back(tile, gain, cosine, sine, low, grad):
    grad = grad * cosine - turn(grad) * sine
    scale = lax.rsqrt(half_means(tile * tile, low) + EPSILON)
    lifted = grad * gain
    dots = half_means(tile * lifted, low)
    d_tile = scale * lifted - tile * (scale * scale * scale) * dots
    return d_tile, jnp.sum(grad * tile * scale, axis=0, keepdims=True)


def place(table, j):
    return pl.ds(pl.multiple_of(table[j] * BLOCK, BLOCK), BLOCK)


def span(j, size=BLOCK):
    return slice(j * size, (j + 1) * size)


def over_pieces(left, pieces, columns=None):
    total, start = None, 0
    for piece in pieces:
        size = piece.shape[0]
        right = piece[...] if columns is None else piece[:, columns]
        term = dot_nn(left[:, start : start + size], right)
        total = term if total is None else total + term
        start += size
    return total


def add_back(target, left, pieces, columns=None):
    start = 0
    for piece in pieces:
        size = piece.shape[0]
        right = piece[...] if columns is None else piece[:, columns]
        target[:, start : start + size] += dot_nt(left, right)
        start += size


def key_value_kernel(table, tokens, cosine, sine, gain, *refs):
    kvg = refs[:-4]
    normed, kv_raw, kv_low, gains = refs[-4:]
    rows, width = tokens.shape
    count = width // BLOCK
    columns = jnp.concatenate([part[:, KV_WIDTH:].astype(F32).T for part in kvg], axis=1)
    gains[...] = columns[:8]
    squares = 0.0
    for j in range(count):
        block = tokens[:, place(table, j)].astype(F32)
        squares = squares + jnp.sum(block * block, axis=1, keepdims=True)
    scale = lax.rsqrt(squares / width + EPSILON)
    for j in range(count):
        block = tokens[:, place(table, j)].astype(F32)
        normed[:, span(j)] = (
            block * scale * columns[ATTENTION_GAIN : ATTENTION_GAIN + 1, span(j)]
        ).astype(BF)
    raw = over_pieces(normed, kvg, slice(0, KV_WIDTH))
    kv_raw[...] = raw
    low = half_lanes(rows)
    for c in range(KEY_VALUE_HEADS):
        tile = raw[:, span(c, LANES)]
        key = head_norm(tile, gain[...], cosine[...], sine[...], low)
        kv_low[:, span(c, LANES)] = jnp.where(low, key, tile).astype(BF)


def project_key_value(table, tokens, cosine, sine, gain, kvg):
    rows, width = tokens.shape
    operands = (tokens, cosine, sine, gain, *kvg)
    return kernel_call(
        key_value_kernel,
        "project_key_value",
        (1,),
        [whole(o) for o in operands],
        [
            fixed_out((rows, width)),
            fixed_out((rows, KV_WIDTH)),
            fixed_out((rows, KV_WIDTH)),
            fixed_out((8, width)),
        ],
        [
            shape((rows, width), BF),
            shape((rows, KV_WIDTH), F32),
            shape((rows, KV_WIDTH), BF),
            shape((8, width), F32),
        ],
        [],
        2 * rows * width * KV_WIDTH,
        table,
    )(*operands)


def query_kernel(normed, cosine, sine, gain, *refs):
    q_raw, queries = refs[-2:]
    rows = normed.shape[0]
    raw = over_pieces(normed, refs[:-2])
    q_raw[...] = raw
    low = half_lanes(rows)
    for tile_index in range(GROUP_WIDTH // LANES):
        tile = raw[:, span(tile_index, LANES)]
        turned = head_norm(tile, gain[...], cosine[...], sine[...], low)
        queries[:, span(tile_index, LANES)] = (turned * SCORE_SCALE).astype(BF)


def column_parts(pieces):
    return [pl.BlockSpec((piece.shape[0], GROUP_WIDTH), lambda c, *t: (0, c)) for piece in pieces]


def project_query(normed, cosine, sine, gain, weight):
    rows, width = normed.shape
    out = pl.BlockSpec((rows, GROUP_WIDTH), lambda c: (0, c))
    return kernel_call(
        query_kernel,
        "project_query",
        (KEY_VALUE_HEADS,),
        [whole(normed), whole(cosine), whole(sine), whole(gain), *column_parts(weight)],
        [out, out],
        [shape((rows, Q_WIDTH), F32), shape((rows, Q_WIDTH), BF)],
        [],
        2 * rows * width * Q_WIDTH,
    )(normed, cosine, sine, gain, *weight)


def output_kernel(table, mixed, tokens, gains, *refs):
    hidden, feed = refs[-2:]
    width = hidden.shape[1]
    step = pl.program_id(0)

    @pl.when(step == 0)
    def _():
        for j in range(width // BLOCK):
            hidden[:, span(j)] = tokens[:, place(table, j)].astype(F32)

    add_back(hidden, mixed[...], refs[:-2])

    @pl.when(step == pl.num_programs(0) - 1)
    def _():
        values = hidden[...]
        scale = lax.rsqrt(jnp.mean(values * values, axis=1, keepdims=True) + EPSILON)
        feed[...] = (values * scale * gains[FEED_GAIN : FEED_GAIN + 1, :]).astype(BF)


def project_output(table, mixed, tokens, batch, gains, weight):
    rows = mixed.shape[0]
    width = tokens.shape[1]
    return kernel_call(
        output_kernel,
        "project_output",
        (KEY_VALUE_HEADS,),
        [
            pl.BlockSpec((rows, GROUP_WIDTH), lambda c, t: (0, c)),
            pl.BlockSpec((rows, width), lambda c, t: (batch, 0)),
            whole(gains),
            *column_parts(weight),
        ],
        [fixed_out((rows, width)), fixed_out((rows, width))],
        [shape((rows, width), F32), shape((rows, width), BF)],
        [],
        2 * rows * width * Q_WIDTH,
        table,
    )(mixed, tokens, gains, *weight)


def hidden_back_kernel(table, d_feed, hidden, cot, gains, *refs):
    d_hidden, d_attended, gain_grad, d_mixed = refs[-4:]
    width = hidden.shape[1]

    @pl.when(pl.program_id(0) == 0)
    def _():
        values = hidden[...]
        grad = d_feed[...].astype(F32)
        scale = lax.rsqrt(jnp.mean(values * values, axis=1, keepdims=True) + EPSILON)
        lifted = grad * gains[FEED_GAIN : FEED_GAIN + 1, :]
        dots = jnp.mean(values * lifted, axis=1, keepdims=True)
        d_norm = scale * lifted - values * (scale * scale * scale) * dots
        gain_grad[...] = jnp.broadcast_to(
            jnp.sum(grad * values * scale, axis=0, keepdims=True), gain_grad.shape
        )
        for j in range(width // BLOCK):
            total = cot[:, place(table, j)].astype(F32) + d_norm[:, span(j)]
            d_hidden[:, span(j)] = total
            d_attended[:, span(j)] = total.astype(BF)

    d_mixed[...] = over_pieces(d_attended, refs[:-4]).astype(BF)


def hidden_back(table, d_feed, hidden, cot, batch, gains, weight):
    rows, width = hidden.shape
    return kernel_call(
        hidden_back_kernel,
        "hidden_back",
        (KEY_VALUE_HEADS,),
        [
            whole(d_feed),
            whole(hidden),
            pl.BlockSpec((rows, width), lambda c, t: (batch, 0)),
            whole(gains),
            *column_parts(weight),
        ],
        [
            fixed_out((rows, width)),
            fixed_out((rows, width)),
            fixed_out((8, width)),
            pl.BlockSpec((rows, GROUP_WIDTH), lambda c, t: (0, c)),
        ],
        [
            shape((rows, width), F32),
            shape((rows, width), BF),
            shape((8, width), F32),
            shape((rows, Q_WIDTH), BF),
        ],
        [],
        2 * rows * width * Q_WIDTH,
        table,
    )(d_feed, hidden, cot, gains, *weight)


def query_back_kernel(d_q, *refs):
    out = refs[-1]

    @pl.when(pl.program_id(0) == 0)
    def _():
        out[...] = jnp.zeros_like(out)

    add_back(out, d_q[...], refs[:-1])


def query_back(d_q, weight):
    rows = d_q.shape[0]
    width = sum(piece.shape[0] for piece in weight)
    return kernel_call(
        query_back_kernel,
        "query_back",
        (KEY_VALUE_HEADS,),
        [pl.BlockSpec((rows, GROUP_WIDTH), lambda c: (0, c)), *column_parts(weight)],
        fixed_out((rows, width)),
        shape((rows, width), F32),
        [],
        2 * rows * width * Q_WIDTH,
    )(d_q, *weight)


def input_back_kernel(
    table,
    d_pair,
    kv_raw,
    cosine,
    sine,
    gain,
    d_normed_q,
    d_hidden0,
    d_hidden1,
    tokens,
    gains,
    *refs,
):
    kvg = refs[:-5]
    d_kv_raw, head_grad, tokens_grad, gain_grad, d_normed = refs[-5:]
    rows, width = tokens.shape
    part = d_hidden0.shape[0]
    low = half_lanes(rows)
    total = 0.0
    for c in range(KEY_VALUE_HEADS):
        grad = d_pair[:, span(c, LANES)].astype(F32)
        d_tile, g_tile = head_norm_back(
            kv_raw[:, span(c, LANES)], gain[...], cosine[...], sine[...], low, grad
        )
        total = total + g_tile
        d_kv_raw[:, span(c, LANES)] = jnp.where(low, d_tile, grad).astype(BF)
    head_grad[...] = jnp.broadcast_to(total, head_grad.shape)
    d_kv = d_kv_raw[...]
    d_normed[...] = d_normed_q[...]
    add_back(d_normed, d_kv, kvg, slice(0, KV_WIDTH))
    squares, dots = 0.0, 0.0
    for j in range(width // BLOCK):
        block = tokens[:, place(table, j)].astype(F32)
        lifted = d_normed[:, span(j)] * gains[ATTENTION_GAIN : ATTENTION_GAIN + 1, span(j)]
        squares = squares + jnp.sum(block * block, axis=1, keepdims=True)
        dots = dots + jnp.sum(block * lifted, axis=1, keepdims=True)
    scale = lax.rsqrt(squares / width + EPSILON)
    dots = dots / width * (scale * scale * scale)
    for j in range(width // BLOCK):
        block = tokens[:, place(table, j)].astype(F32)
        grad = d_normed[:, span(j)]
        lifted = grad * gains[ATTENTION_GAIN : ATTENTION_GAIN + 1, span(j)]
        d_input = scale * lifted - block * dots
        for batch, d_hidden in enumerate((d_hidden0, d_hidden1)):
            tokens_grad[span(batch, part), place(table, j)] = (
                d_hidden[:, span(j)] + d_input[span(batch, part), :]
            )
        gain_grad[:, span(j)] = jnp.broadcast_to(
            jnp.sum(grad * block * scale, axis=0, keepdims=True), (8, BLOCK)
        )


def input_back(table, *operands):
    tokens = operands[8]
    rows, width = tokens.shape
    return kernel_call(
        input_back_kernel,
        "input_back",
        (1,),
        [whole(o) for o in operands],
        [
            fixed_out((rows, KV_WIDTH)),
            fixed_out((8, LANES)),
            fixed_out((rows, width)),
            fixed_out((8, width)),
        ],
        [
            shape((rows, KV_WIDTH), BF),
            shape((8, LANES), F32),
            shape((rows, width), F32),
            shape((8, width), F32),
        ],
        [pltpu.VMEM((rows, width), F32)],
        2 * rows * width * KV_WIDTH,
        table,
    )(*operands)


def layer_out_kernel(table, hidden0, hidden1, added0, added1, out):
    part = hidden0.shape[0]
    for batch, (hidden, added) in enumerate(((hidden0, added0), (hidden1, added1))):
        for j in range(hidden.shape[1] // BLOCK):
            out[span(batch, part), place(table, j)] = (
                hidden[:, span(j)] + added[:, span(j)].astype(F32)
            ).astype(BF)


def finish_layer(table, *operands):
    rows, width = operands[0].shape
    return kernel_call(
        layer_out_kernel,
        "finish_layer",
        (1,),
        [whole(o) for o in operands],
        fixed_out((2 * rows, width)),
        shape((2 * rows, width), BF),
        [],
        0,
        table,
    )(*operands)


def key_value_grad_kernel(normed, d_kv_raw, gain_grads, out0, out1):
    half = normed.shape[1] // 2
    for index, out in enumerate((out0, out1)):
        cut = span(index, half)
        out[:, :KV_WIDTH] = dot_tn(normed[:, cut], d_kv_raw[...]).astype(BF)
        rows = gain_grads[:, cut]
        rows = jnp.concatenate([rows, jnp.zeros((LANES - 8, half), F32)], axis=0)
        out[:, KV_WIDTH:] = rows.T.astype(BF)


def key_value_grad(normed, d_kv_raw, gain_grads):
    rows, width = normed.shape
    dims = (width // 2, KV_WIDTH + LANES)
    return kernel_call(
        key_value_grad_kernel,
        "key_value_grad",
        (1,),
        [whole(normed), whole(d_kv_raw), whole(gain_grads)],
        [fixed_out(dims), fixed_out(dims)],
        [shape(dims, BF), shape(dims, BF)],
        [],
        2 * rows * width * KV_WIDTH,
    )(normed, d_kv_raw, gain_grads)


def pad_heads(tile, low, keep_low):
    parts = []
    for pair in range(GROUP // 2):
        both = tile[:, span(pair, LANES)].astype(F32)
        turned = pltpu.roll(both, HEAD_SIZE, 1)
        first, second = (both, turned) if keep_low else (turned, both)
        keep = low if keep_low else jnp.logical_not(low)
        parts.append(jnp.where(keep, first, 0.0))
        parts.append(jnp.where(keep, second, 0.0))
    return jnp.concatenate(parts, axis=0).astype(BF)


def four_wide(row):
    return jnp.concatenate([row] * GROUP, axis=1)


def heads_back(stacked, rows):
    parts = []
    for pair in range(GROUP // 2):
        start = 2 * pair * rows
        both = jnp.concatenate(
            [stacked[:, start : start + rows], stacked[:, start + rows : start + 2 * rows]], axis=0
        )
        parts.append(both.T)
    return jnp.concatenate(parts, axis=1)


def key_rows(kv, cut):
    rows = kv.shape[2]
    block = kv[cut.start // rows : cut.stop // rows, 0]
    return block.reshape(cut.stop - cut.start, kv.shape[3])


def every_row(kv):
    return key_rows(kv, slice(0, kv.shape[0] * kv.shape[2]))


def ones_and_values(kv):
    values = every_row(kv)
    return jnp.where(half_lanes(values.shape[0]), 1.0, values.astype(F32)).astype(BF)


def attention_forward_kernel(kv0, kv1, query, bias0, bias1, mixed, lse, expo):
    rows = query.shape[0]
    half = bias0.shape[0]
    padded = pad_heads(query[...], half_lanes(rows), True)
    for part, (kv, bias) in enumerate(((kv0, bias0), (kv1, bias1))):
        for step in range(half // CHUNK):
            cut = span(step, CHUNK)
            weight = jnp.exp(dot_nt(key_rows(kv, cut), padded) + four_wide(bias[cut, :]))
            expo[part * half + step * CHUNK : part * half + (step + 1) * CHUNK, :] = weight.astype(BF)
    total = dot_tn(ones_and_values(kv0), expo[:half, :]) + dot_tn(
        ones_and_values(kv1), expo[half:, :]
    )
    lse[...] = jnp.log(total[0:1, :])[None]
    mixed[...] = heads_back(total[HEAD_SIZE:, :] / total[:HEAD_SIZE, :], rows).astype(BF)


def attention_forward(kv0, kv1, query, batch, bias0, bias1):
    half, rows = bias0.shape
    wide = GROUP * rows
    keys = pl.BlockSpec((half // rows, 1, rows, LANES), lambda c: (0, batch, 0, c))
    kv0, kv1 = (kv.reshape(half // rows, -1, rows, KV_WIDTH) for kv in (kv0, kv1))
    return kernel_call(
        attention_forward_kernel,
        "attention_forward",
        (KEY_VALUE_HEADS,),
        [
            keys,
            keys,
            pl.BlockSpec((rows, GROUP_WIDTH), lambda c: (batch, c)),
            whole(bias0),
            whole(bias1),
        ],
        [
            pl.BlockSpec((rows, GROUP_WIDTH), lambda c: (0, c)),
            pl.BlockSpec((1, 1, wide), lambda c: (c, 0, 0)),
        ],
        [shape((rows, Q_WIDTH), BF), shape((KEY_VALUE_HEADS, 1, wide), F32)],
        [pltpu.VMEM((2 * half, wide), BF)],
        KEY_VALUE_HEADS * 2 * half * wide * LANES * 12,
    )(kv0, kv1, query, bias0, bias1)


def attention_backward_kernel(
    kv0,
    kv1,
    query,
    mixed,
    d_mixed,
    bias0,
    bias1,
    lse,
    q_raw,
    cosine,
    sine,
    gain,
    d_q_raw,
    d_kv0,
    d_kv1,
    gain_grad,
    d_scores,
):
    rows = query.shape[0]
    half = bias0.shape[0]
    low = half_lanes(rows)
    padded = pad_heads(query[...], low, True)
    d_padded = pad_heads(d_mixed[...], low, False)
    product = d_mixed[...].astype(F32) * mixed[...].astype(F32)
    pick = (
        lax.broadcasted_iota(jnp.int32, (8, GROUP_WIDTH), 1) // HEAD_SIZE
        == lax.broadcasted_iota(jnp.int32, (8, GROUP_WIDTH), 0)
    ).astype(F32)
    balance = lax.dot_general(
        pick,
        product,
        (((1,), (1,)), ((), ())),
        precision=lax.Precision.HIGHEST,
        preferred_element_type=F32,
    )
    balance = jnp.concatenate([balance[head : head + 1, :] for head in range(GROUP)], axis=1)
    level = lse[0]
    for part, (kv, bias, d_kv) in enumerate(((kv0, bias0, d_kv0), (kv1, bias1, d_kv1))):
        for step in range(half // CHUNK):
            cut = span(step, CHUNK)
            block = key_rows(kv, cut)
            probs = jnp.exp(dot_nt(block, padded) + four_wide(bias[cut, :]) - level)
            d_probs = dot_nt(block, d_padded)
            low_scores = (probs * (d_probs - balance)).astype(BF)
            d_scores[part * half + step * CHUNK : part * half + (step + 1) * CHUNK, :] = low_scores
            d_kv[cut, :] = (
                dot_nn(low_scores, padded) + dot_nn(probs.astype(BF), d_padded)
            ).astype(BF)
    total = dot_tn(every_row(kv0), d_scores[:half, :]) + dot_tn(
        every_row(kv1), d_scores[half:, :]
    )
    d_query = heads_back(total[:HEAD_SIZE, :] * SCORE_SCALE, rows)
    grads = 0.0
    for tile_index in range(GROUP_WIDTH // LANES):
        cut = span(tile_index, LANES)
        d_tile, g_tile = head_norm_back(
            q_raw[:, cut], gain[...], cosine[...], sine[...], low, d_query[:, cut]
        )
        d_q_raw[:, cut] = d_tile.astype(BF)
        grads = grads + g_tile

    @pl.when(pl.program_id(0) == 0)
    def _():
        gain_grad[...] = jnp.zeros_like(gain_grad)

    gain_grad[...] += jnp.broadcast_to(grads, gain_grad.shape)


def attention_backward(
    kv0, kv1, query, batch, mixed, d_mixed, bias0, bias1, lse, q_raw, cosine, sine, gain
):
    half, rows = bias0.shape
    wide = GROUP * rows
    keys = pl.BlockSpec((half // rows, 1, rows, LANES), lambda c: (0, batch, 0, c))
    kv0, kv1 = (kv.reshape(half // rows, -1, rows, KV_WIDTH) for kv in (kv0, kv1))
    d_keys = pl.BlockSpec((half, LANES), lambda c: (0, c))
    heads = pl.BlockSpec((rows, GROUP_WIDTH), lambda c: (0, c))
    part = pl.BlockSpec((rows, GROUP_WIDTH), lambda c: (batch, c))
    table = pl.BlockSpec((rows, LANES), lambda c: (batch, 0))
    return kernel_call(
        attention_backward_kernel,
        "attention_backward",
        (KEY_VALUE_HEADS,),
        [
            keys,
            keys,
            part,
            heads,
            heads,
            whole(bias0),
            whole(bias1),
            pl.BlockSpec((1, 1, wide), lambda c: (c, 0, 0)),
            part,
            table,
            table,
            whole(gain),
        ],
        [heads, d_keys, d_keys, fixed_out((8, LANES))],
        [
            shape((rows, Q_WIDTH), BF),
            shape((half, KV_WIDTH), BF),
            shape((half, KV_WIDTH), BF),
            shape((8, LANES), F32),
        ],
        [pltpu.VMEM((2 * half, wide), BF)],
        KEY_VALUE_HEADS * 2 * half * wide * LANES * 28,
    )(kv0, kv1, query, mixed, d_mixed, bias0, bias1, lse, q_raw, cosine, sine, gain)


def swap_halves(values):
    half = values.shape[1] // 2
    return jnp.concatenate([values[:, half:], values[:, :half]], axis=1)


def feed_forward_kernel(count, units, *refs):
    feed0, feed1, cot0, cot1 = refs[:4]
    gate_up = refs[4 : 4 + count]
    down = refs[4 + count : 4 + 2 * count]
    act_out, d_units_out, out0, out1, d_feed0, d_feed1 = refs[4 + 2 * count :]
    first = pl.program_id(0) < pl.num_programs(0) // 2
    rows, width = feed0.shape
    half = width // 2
    size = down[0].shape[0] // 2
    feed = jnp.where(first, swap_halves(feed0[...]), feed1[...])
    cot = jnp.where(first, swap_halves(cot0[...]), cot1[...])

    def over(left, pieces):
        total = None
        for b, piece in enumerate(pieces):
            both = jnp.concatenate(
                [left[:, b * size : (b + 1) * size], left[:, half + b * size : half + (b + 1) * size]],
                axis=1,
            )
            term = dot_nn(both, piece[...])
            total = term if total is None else total + term
        return total

    both = over(feed, gate_up)
    gate_pre, up_pre = both[:, :units], both[:, units : 2 * units]
    sig = 1.0 / (1.0 + jnp.exp(-gate_pre))
    silu = gate_pre * sig
    act = (silu * up_pre).astype(BF)
    act = jnp.concatenate([act, jnp.zeros((rows, down[0].shape[1] - units), BF)], axis=1)
    act_out[...] = act
    d_act = over(cot, down)[:, :units]
    d_gate = d_act * up_pre * (sig * (1.0 + gate_pre * (1.0 - sig)))
    d_units = jnp.concatenate(
        [
            d_gate.astype(BF),
            (d_act * silu).astype(BF),
            jnp.zeros((rows, gate_up[0].shape[1] - 2 * units), BF),
        ],
        axis=1,
    )
    d_units_out[...] = d_units

    def write(target, left, pieces, swapped):
        for b, piece in enumerate(pieces):
            block = dot_nt(left, piece[...]).astype(BF)
            early, late = (half, 0) if swapped else (0, half)
            target[:, early + b * size : early + (b + 1) * size] = block[:, :size]
            target[:, late + b * size : late + (b + 1) * size] = block[:, size:]

    @pl.when(first)
    def _():
        write(d_feed0, d_units, gate_up, True)
        write(out0, act, down, True)

    @pl.when(jnp.logical_not(first))
    def _():
        write(d_feed1, d_units, gate_up, False)
        write(out1, act, down, False)


def feed_forward(feeds, cots, gate_up, down, units):
    tokens, width = feeds[0].shape
    steps = tokens // FFN_ROWS
    early = pl.BlockSpec((FFN_ROWS, width), lambda i: (jnp.minimum(i, steps - 1), 0))
    late = pl.BlockSpec((FFN_ROWS, width), lambda i: (jnp.maximum(i - steps, 0), 0))
    act_width, units_width = down[0].shape[1], gate_up[0].shape[1]
    return kernel_call(
        functools.partial(feed_forward_kernel, len(down), units),
        "feed_forward",
        (2 * steps,),
        [early, late, early, late, *[whole(w) for w in (*gate_up, *down)]],
        [
            pl.BlockSpec((FFN_ROWS, act_width), lambda i: (i, 0)),
            pl.BlockSpec((FFN_ROWS, units_width), lambda i: (i, 0)),
            early,
            late,
            early,
            late,
        ],
        [
            shape((2 * tokens, act_width), BF),
            shape((2 * tokens, units_width), BF),
            *[shape((tokens, width), BF)] * 4,
        ],
        [],
        2 * tokens * 2 * width * units * 6,
    )(*feeds, *cots, *gate_up, *down)


def weight_grad_kernel(count, columns, *refs):
    lefts = refs[: 2 * count]
    rights = refs[2 * count : -1]
    out = refs[-1]
    rows = lefts[0].shape[0]
    each = count // len(rights)
    total = None
    for index in range(count):
        left = jnp.concatenate([lefts[2 * index][...], lefts[2 * index + 1][...]], axis=1)
        right = rights[index // each]
        term = dot_tn(left, right[span(index % each, rows), columns])
        total = term if total is None else total + term
    out[...] = total.astype(BF)


def weight_grad(lefts, rights, columns, steps, stride, offset):
    rows, width = lefts[0].shape
    units = columns.stop - columns.start
    half = width // 2 // BLOCK
    mine = pl.BlockSpec((rows, BLOCK), lambda i: (0, i * stride + offset))
    other = pl.BlockSpec((rows, BLOCK), lambda i: (0, half + i * stride + offset))
    specs, operands = [], []
    for index, left in enumerate(lefts):
        specs += [other, mine] if index % 2 == 0 else [mine, other]
        operands += [left, left]
    return kernel_call(
        functools.partial(weight_grad_kernel, len(lefts), columns),
        "weight_grad",
        (steps,),
        [*specs, *[whole(r) for r in rights]],
        pl.BlockSpec((2 * BLOCK, units), lambda i: (i, 0)),
        shape((2 * BLOCK * steps, units), BF),
        [],
        2 * len(lefts) * rows * 2 * BLOCK * steps * units,
    )(*operands, *rights)


def rotary_tables(places):
    half_width = HEAD_SIZE // 2
    freqs = jnp.exp(jnp.arange(half_width, dtype=F32) * (-2.0 * math.log(10000.0) / HEAD_SIZE))
    angles = places.astype(F32)[:, None] * freqs[None, :]
    cosine, sine = jnp.cos(angles), jnp.sin(angles)
    return (
        jnp.concatenate([cosine] * 4, axis=1),
        jnp.concatenate([-sine, sine, -sine, sine], axis=1),
    )


def padded_columns(values, columns):
    return jnp.pad(values, ((0, 0), (0, columns - values.shape[1])))


def up_to(size):
    return -(-size // LANES) * LANES


def on_device(
    tokens,
    lengths,
    attention_gain,
    query_weight,
    key_value_matrix,
    per_head_gains,
    output_weight,
    feed_gain,
    gate_weight,
    up_weight,
    down_weight,
    cotangent,
):
    batches = tokens.shape[0]
    rows = tokens.shape[2]
    width = tokens.shape[3]
    dp_size = lax.axis_size("dp")
    heads_size = lax.axis_size("heads")
    seq_size = lax.axis_size("seq")
    assert seq_size == 4 and heads_size == 4 and batches == 2
    paired = dp_size == 2
    y = lax.axis_index("dp").astype(jnp.int32)
    s = lax.axis_index("seq").astype(jnp.int32)
    z = lax.axis_index("heads").astype(jnp.int32)
    x = s // 2
    core = s % 2

    def after(v, *others):
        return lax.optimization_barrier((v, others))[0]

    def swap_x(v):
        return lax.ppermute(v, "seq", [(i, i ^ 2) for i in range(4)])

    def swap_core(v):
        return lax.ppermute(v, "seq", [(i, i ^ 1) for i in range(4)])

    def swap_y(v):
        return lax.ppermute(v, "dp", [(0, 1), (1, 0)])

    def pair_scatter(v, axis):
        def step(u, upper, distance):
            low, high = jnp.split(u, 2, axis=axis)
            sent = lax.ppermute(
                jnp.where(upper, low, high), "heads", [(i, i ^ distance) for i in range(4)]
            )
            return jnp.where(upper, high, low) + sent

        return step(step(v, z >= 2, 2), z % 2 == 1, 1)

    def gather_near(v):
        if not paired:
            both = jnp.stack([v, swap_x(v)], axis=0)
            return [lax.all_gather(both, "dp", axis=0).reshape(-1, v.shape[-1])]
        return [v, swap_x(v), swap_y(v)]

    def gather_far(near, x_first):
        if not paired:
            return near
        return [*near, swap_y(near[1]) if x_first else swap_x(near[2])]

    def pair_gather(v, axis):
        def step(u, upper, distance):
            got = lax.ppermute(u, "heads", [(i, i ^ distance) for i in range(4)])
            return jnp.where(
                upper,
                jnp.concatenate([got, u], axis=axis),
                jnp.concatenate([u, got], axis=axis),
            )

        return step(step(v, z % 2 == 1, 1), z >= 2, 2)

    def both_cores(pieces):
        return [*pieces, *[swap_core(v) for v in pieces]]

    def unit_pieces(pieces):
        if paired:
            return pieces
        g = pieces[0].reshape(blocks, 2, -1, pieces[0].shape[-1])
        return [g.transpose(1, 0, 2, 3).reshape(pieces[0].shape)]

    def scatter_yx(g, x_last, first=(), second=()):
        def along_x(u, late):
            return u[..., 0, :, :] + after(swap_x(u[..., 1, :, :]), late)

        def along_y(u, late):
            if paired:
                return u[0] + after(swap_y(u[1]), late)
            return lax.psum_scatter(u, "dp", scatter_dimension=0)

        if x_last:
            return along_x(along_y(g, first), second)
        return along_y(along_x(g, first), second)

    blocks = 2 * dp_size
    piece = width // blocks

    if paired:
        own = (2 * y + x) * 2 + core
        places_of = jnp.array([b * 2 + c for c in range(2) for b in range(4)], jnp.int32)
        table = places_of ^ own

        def to_order(v):
            return v

        from_order = to_order
    else:
        table = jnp.arange(width // BLOCK, dtype=jnp.int32)

        def flip(v):
            u = v.reshape(v.shape[:-1] + (dp_size, 2, 2, piece // 2))
            u = jnp.where(x == 1, u[..., ::-1, :, :], u)
            return jnp.where(core == 1, u[..., ::-1, :], u)

        def to_order(v):
            return jnp.moveaxis(flip(v), -2, -4).reshape(v.shape)

        def from_order(v):
            u = v.reshape(v.shape[:-1] + (2, dp_size, 2, piece // 2))
            return flip(jnp.moveaxis(u, -4, -2).reshape(v.shape)).reshape(v.shape)

    def small_order(v, back):
        if not paired:
            return from_order(v) if back else to_order(v)
        cut = v.reshape(8, -1)
        return jnp.concatenate(
            [
                lax.select_n(own, *[cut[held(i, m, back)] for m in range(8)])
                for i in range(8)
            ]
        ).reshape(v.shape)

    def held(i, m, back):
        if back:
            source = i ^ m
            return (source % 2) * 4 + source // 2
        return ((i % 4) * 2 + i // 4) ^ m

    small = key_value_matrix.shape[0]
    per_head = per_head_gains.shape[0]
    kv_local = (
        key_value_matrix.reshape(small, 2, KEY_VALUE_HEADS, HEAD_SIZE)
        .transpose(0, 2, 1, 3)
        .reshape(small, KV_WIDTH)
    )
    gains_local = jnp.stack(
        [attention_gain, feed_gain, jnp.pad(per_head_gains, (0, small - per_head))], axis=1
    )
    kvg_local = jnp.concatenate([kv_local, padded_columns(gains_local, LANES)], axis=1)
    kvg_rows = pair_gather(kvg_local, 0)
    kvg_near = gather_near(kvg_rows)

    tokens_in = to_order(tokens[:, 0].reshape(batches * rows, width))
    cot_in = to_order(cotangent[:, 0].reshape(batches * rows, width))
    cot_held = order_columns(table, cot_in) if paired else cot_in
    lined = lax.all_gather(
        jnp.concatenate(
            [
                cot_held,
                padded_columns(query_weight.reshape(small, Q_WIDTH), width),
                padded_columns(output_weight.T, width),
            ],
            axis=0,
        ),
        "heads",
        axis=0,
    )
    cots_mine = [
        lined[:, span(batch, rows)].reshape(heads_size * rows, width) for batch in range(batches)
    ]
    q_rows = (
        lined[:, batches * rows : batches * rows + small, :Q_WIDTH]
        .reshape(heads_size, query_weight.shape[0], query_weight.shape[1])
        .transpose(1, 0, 2)
        .reshape(query_weight.shape[0], Q_WIDTH)
    )
    o_rows = lined[:, batches * rows + small :, :Q_WIDTH].reshape(4 * small, Q_WIDTH)
    q_near = gather_near(q_rows)
    q_full = both_cores(gather_far(q_near, False))
    o_near = gather_near(after(o_rows, q_near))
    o_full = both_cores(gather_far(o_near, True))

    units = gate_weight.shape[1] // 2
    act_width, units_width = up_to(units), up_to(2 * units)

    def unit_half(v, which):
        return jnp.where(which == 0, v[:, :units], v[:, units:])

    down_local = down_weight.T

    def halves(which):
        gate_up = jnp.concatenate([unit_half(gate_weight, which), unit_half(up_weight, which)], axis=1)
        return jnp.concatenate(
            [padded_columns(gate_up, units_width), padded_columns(unit_half(down_local, which), act_width)],
            axis=1,
        )

    keep = halves(core)
    take = swap_core(halves(1 - core))
    ffn_rows = jnp.concatenate([keep, take], axis=0)
    down_near = gather_near(ffn_rows[:, units_width:])
    gate_up_near = gather_near(after(ffn_rows[:, :units_width], kvg_near))
    gate_up = unit_pieces(gather_far(gate_up_near, True))
    down = unit_pieces(gather_far(down_near, False))
    kvg = both_cores(gather_far(after(kvg_near, down_near), True))

    head_column = jnp.concatenate([part[:, KV_WIDTH + HEAD_GAIN] for part in kvg])
    head_scale = small_order(head_column.astype(F32)[None], True)
    head_scale = head_scale.reshape(-1, small)[:, :per_head].reshape(1, -1)
    query_gain = jnp.concatenate([head_scale[:, :HEAD_SIZE]] * 2, axis=1)
    key_gain = jnp.concatenate([head_scale[:, HEAD_SIZE:]] * 2, axis=1)

    block_rows = rows * heads_size
    spots = s * block_rows + z * rows + jnp.arange(rows, dtype=jnp.int32)
    inside = jnp.arange(rows, dtype=jnp.int32)

    def key_spots(first):
        lines = jnp.arange(heads_size, dtype=jnp.int32)[:, None, None] * rows
        fronts = jnp.stack([first, first ^ 2])[None, :, None] * block_rows
        return (lines + fronts + inside[None, None, :]).reshape(-1)

    def bias_for(begin, first):
        keys = key_spots(first)[:, None]
        return jnp.where((keys <= spots[None, :]) & (keys >= begin[None, :]), 0.0, MASKED)

    begins, biases = [], []
    for batch in range(batches):
        sizes = lengths[batch, 0]
        finish = jnp.cumsum(sizes)
        begin = jnp.sum(
            jnp.where(spots[:, None] >= finish[None, :], sizes[None, :], 0), axis=1
        ).astype(jnp.int32)
        begins.append(begin)
        biases.append((bias_for(begin, s), bias_for(begin, s ^ 1)))
    cosine, sine = rotary_tables(jnp.concatenate([spots - begin for begin in begins]))

    normed, kv_raw, kv_low, gains = project_key_value(
        table, after(tokens_in, down_near), cosine, sine, key_gain, kvg
    )
    q_raw, queries = project_query(normed, cosine, sine, query_gain, q_full)

    kv_lined = lax.all_gather(
        after(jnp.concatenate([kv_low, swap_x(kv_low)], axis=0), gate_up_near), "heads", axis=0, tiled=True
    )
    kv_lined = after(kv_lined, q_full[:4], o_near)
    kv_other = swap_core(kv_lined)
    kvs = (kv_lined, kv_other)
    feeds, mixeds, lses, hiddens = [], [], [], []
    for batch in range(batches):
        query = queries if batch == 0 else after(queries, hiddens[0])
        mixed, lse = attention_forward(*kvs, query, batch, *biases[batch])
        mixed_tied = mixed if batch == 0 else after(mixed, gate_up, down)
        hidden_in, feed_rows = project_output(
            table, mixed_tied, tokens_in, batch, gains, o_full
        )
        feed_mine = lax.all_gather(feed_rows, "heads", axis=0, tiled=True)
        feeds.append((swap_core(feed_mine), feed_mine))
        mixeds.append(mixed)
        lses.append(lse)
        hiddens.append(hidden_in)

    d_feeds, acts, d_units, cots, outs = [], [], [], [], []
    for batch in range(batches):
        cot_pair = (swap_core(cots_mine[batch]), cots_mine[batch])
        act, d_unit, out_other, out_mine, d_feed_other, d_feed_mine = feed_forward(
            feeds[batch], cot_pair, gate_up, down, units
        )
        acts.append(act)
        d_units.append(d_unit)
        cots.append(cot_pair)
        outs.append((out_mine, out_other))
        d_feed = d_feed_mine + swap_core(d_feed_other)
        if batch + 1 < batches:
            d_feed = after(d_feed, feeds[batch + 1])
        d_feeds.append(lax.psum_scatter(d_feed, "heads", scatter_dimension=0, tiled=True))

    feed_all = [f for pair in feeds for f in pair]
    cot_all = [c for pair in cots for c in pair]
    count = width // 2 // BLOCK

    def unit_order(g):
        g = g.reshape(count, 2, BLOCK, -1).transpose(1, 0, 2, 3)
        g = g.reshape(2, blocks, piece // 2, -1).transpose(1, 0, 2, 3)
        return g.reshape(dp_size, 2, piece, -1)

    cut_at = up_to(units)

    def both_grads(left, right):
        return [dot_tn(left[:, span(i, width // 2)], right).astype(BF) for i in range(2)]

    def split_rows(mine, got, along_y=True):
        if not paired:
            return mine + got, None
        size = mine.shape[0] // 4
        far = (2, 3) if along_y else (1, 3)
        near = (0, 1) if along_y else (0, 2)

        def pick(v, blocks_of):
            return jnp.concatenate([v[span(b, size)] for b in blocks_of], axis=0)

        return pick(mine, far) + pick(got, far), pick(mine, near) + pick(got, near)

    def send_parts(v, swap, *rows_of):
        parts, start = [], 0
        for size in rows_of:
            parts.append(swap(v[start : start + size]))
            start += size
        assert start == v.shape[0]
        return parts

    def halved(total):
        near = total.shape[0] // 2
        return total[near:], total[:near]

    def fold(parts, kept, *late):
        return halved(kept + after(jnp.concatenate(parts, axis=0), late))

    def fold_whole(sent):
        g = sent.reshape(dp_size, 2, -1, sent.shape[-1])
        g = lax.psum_scatter(g, "dp", scatter_dimension=0)
        return g[0] + swap_x(g[1])

    d_hiddens, d_attendeds, d_q_raws, d_lined = [], [], [], []
    feed_gain_grads, query_gain_grads = [], []
    mixed_all = jnp.concatenate(mixeds, axis=0)
    first_cut, second_cut = slice(0, cut_at), slice(cut_at, up_to(2 * units))
    if paired:
        first_far = weight_grad(feed_all, d_units, first_cut, 2, 1, 2)
        first_parts = send_parts(first_far, swap_y, 384, 640)
        second_far = weight_grad(feed_all, after(d_units, first_far), second_cut, 2, 2, 1)
        second_parts = send_parts(second_far, swap_x, 384, 640)
        d_feeds[0] = after(d_feeds[0], second_far)
    for batch in range(batches):
        d_feed = d_feeds[batch]
        if batch == 1:
            d_feed = after(d_feed, d_q_raws[0])
            if paired:
                tied = after(acts, d_q_raws[0], first_parts[1], second_parts[1])
                down_far = weight_grad(cot_all, tied, slice(0, act_width), 2, 2, 1)
                down_parts = send_parts(down_far, swap_x, 256, 640, 128)
                d_feed = after(d_feed, down_far, last_kv)
        d_hidden, d_attended, feed_grad, d_mixed = hidden_back(
            table, d_feed, hiddens[batch], cot_in, batch, gains, o_full
        )
        d_hiddens.append(d_hidden)
        d_attendeds.append(d_attended)
        if batch == 0 and paired:
            d_mixed = after(d_mixed, first_parts[0], second_parts[0])
        if batch == 1:
            if paired:
                d_attendeds[1] = after(d_attended, down_parts[0])
            o_grads = both_grads(jnp.concatenate(d_attendeds, axis=0), mixed_all)
            o_send, o_keep = split_rows(o_grads[0], swap_core(o_grads[1]))
            d_mixed = after(d_mixed, o_send)
            if paired:
                o_parts = send_parts(o_send, swap_y, 320, 128, 64)
        d_q_raw, d_kv0, d_kv1, query_grad = attention_backward(
            *kvs,
            queries,
            batch,
            mixeds[batch],
            d_mixed,
            *biases[batch],
            lses[batch],
            q_raw,
            cosine,
            sine,
            query_gain,
        )
        d_kv = d_kv0 + swap_core(d_kv1)
        last_kv = d_kv
        d_lined.append(lax.psum_scatter(d_kv, "heads", scatter_dimension=0, tiled=True))
        d_q_raws.append(d_q_raw)
        feed_gain_grads.append(feed_grad)
        query_gain_grads.append(query_grad)

    d_pairs = [pair[:rows] + swap_x(pair[rows:]) for pair in d_lined]
    d_q_raw_all = jnp.concatenate(d_q_raws, axis=0)
    late = (down_parts[1], o_parts[0]) if paired else ()
    q_grads = both_grads(after(normed, d_q_raws[1], late), d_q_raw_all)
    q_send, q_keep = split_rows(q_grads[0], swap_core(q_grads[1]), False)
    d_normed_q = query_back(after(d_q_raw_all, q_send, d_pairs[0]), q_full)
    if paired:
        q_parts = send_parts(q_send, swap_x, 128, 192, 192)
        tied = after(d_units, d_normed_q, q_parts[0], o_parts[1])
        second_got = jnp.concatenate(second_parts, axis=0)
        second_half = weight_grad(feed_all, tied, second_cut, 2, 2, 0) + second_got
        second_last = send_parts(second_half[2 * BLOCK :], swap_y, 320, 192)
        tied = after(acts, second_half, q_parts[1], o_parts[2])
        down_got = jnp.concatenate(down_parts, axis=0)
        half = weight_grad(cot_all, tied, slice(0, act_width), 2, 2, 0) + down_got
        o_send, o_keep = fold(o_parts, o_keep, half)
        o_parts = send_parts(o_send, swap_x, 128, 128)
        before_input = (half, q_parts[2], second_last[0])
    else:
        every_unit = slice(0, units_width)
        g_gate_up = scatter_yx(
            unit_order(weight_grad(feed_all, d_units, every_unit, count, 1, 0)), True
        )
        g_down = scatter_yx(
            unit_order(weight_grad(cot_all, acts, slice(0, act_width), count, 1, 0)), False
        )
        before_input = ()
    d_pair_all = after(jnp.concatenate(d_pairs, axis=0), before_input)

    d_kv_raw, key_grad, tokens_grad, attention_grad = input_back(
        table,
        d_pair_all,
        kv_raw,
        cosine,
        sine,
        key_gain,
        d_normed_q,
        *d_hiddens,
        tokens_in,
        gains,
        *kvg,
    )
    if paired:
        d_kv_raw = after(d_kv_raw, o_parts[0], second_last[1])
    query_grad = query_gain_grads[0][0] + query_gain_grads[1][0]
    head_grads = jnp.concatenate(
        [query_grad[:HEAD_SIZE] + query_grad[HEAD_SIZE:], key_grad[0, :HEAD_SIZE]]
    ).reshape(-1, per_head)
    head_row = small_order(
        jnp.pad(head_grads, ((0, 0), (0, small - per_head))).reshape(1, width), False
    )
    gain_grads = jnp.concatenate(
        [
            attention_grad[0:1],
            feed_gain_grads[0][0:1] + feed_gain_grads[1][0:1],
            head_row,
            jnp.zeros((5, width), F32),
        ],
        axis=0,
    )
    kv_mine, kv_other = key_value_grad(normed, d_kv_raw, gain_grads)
    kv_send, kv_keep = split_rows(kv_mine, swap_core(kv_other))
    if paired:
        kv_got = swap_y(kv_send)
        tied = after(d_units, kv_send)
        first_got = jnp.concatenate(first_parts, axis=0)
        first_half = weight_grad(feed_all, tied, first_cut, 2, 1, 0) + first_got
        first_last = swap_x(first_half[2 * BLOCK :])
        q_send, q_keep = fold(q_parts, q_keep, first_half)
        q_got = swap_y(q_send)
        kv_send, kv_keep = fold([kv_got], kv_keep, first_half)
        g_kv = kv_keep + swap_x(kv_send)
        g_q = q_keep + after(q_got, g_kv)
        g_o = o_keep + after(jnp.concatenate(o_parts, axis=0), first_half)
        down_last = swap_y(half[2 * BLOCK :])
        first_last, second_last, down_last = after((first_last, second_last, down_last), g_q)
        second_got = jnp.concatenate(second_last, axis=0)
        g_gate_up = jnp.concatenate(
            [first_half[: 2 * BLOCK] + first_last, second_half[: 2 * BLOCK] + second_got], axis=1
        )
        g_down = half[: 2 * BLOCK] + down_last
    else:
        g_o, g_q, g_kv = (fold_whole(v) for v in (o_send, q_send, kv_send))
    g_kv = pair_scatter(g_kv, 0).astype(F32)
    grad_output = pair_scatter(g_o, 0).astype(F32).T
    grad_query = pair_scatter(g_q, 1).astype(F32)
    part_rows = g_down.shape[0] // 2
    g_ffn = jnp.concatenate([g_gate_up, g_down], axis=1)
    g_keep = g_ffn[:part_rows]
    g_take = swap_core(g_ffn[part_rows:])
    grads_ffn = []
    for start in (0, units, units_width):
        kept, got = g_keep[:, start : start + units], g_take[:, start : start + units]
        grads_ffn.append(
            jnp.where(
                core == 0,
                jnp.concatenate([kept, got], axis=1),
                jnp.concatenate([got, kept], axis=1),
            ).astype(F32)
        )
    grad_gate, grad_up, grad_down = grads_ffn
    grad_down = grad_down.T

    grad_key_value = (
        g_kv[:, :KV_WIDTH]
        .reshape(small, KEY_VALUE_HEADS, 2, HEAD_SIZE)
        .transpose(0, 2, 1, 3)
        .reshape(small, KV_WIDTH)
    )

    added = []
    for out_mine, out_other in outs:
        out = after(out_mine, before_input) + after(swap_core(out_other), before_input)
        added.append(lax.psum_scatter(out, "heads", scatter_dimension=0, tiled=True))
    layer_out = finish_layer(table, *hiddens, *added)

    return (
        from_order(layer_out).reshape(tokens.shape),
        from_order(tokens_grad).reshape(tokens.shape),
        g_kv[:, KV_WIDTH + ATTENTION_GAIN],
        grad_query,
        grad_key_value,
        g_kv[:per_head, KV_WIDTH + HEAD_GAIN],
        grad_output,
        g_kv[:, KV_WIDTH + FEED_GAIN],
        grad_gate,
        grad_up,
        grad_down,
    )


def order_kernel(table, values, out):
    for j in range(values.shape[1] // BLOCK):
        out[:, span(j)] = values[:, place(table, j)]


def order_columns(table, values):
    return kernel_call(
        order_kernel,
        "order_columns",
        (1,),
        [whole(values)],
        fixed_out(values.shape),
        shape(values.shape, values.dtype),
        [],
        0,
        table,
    )(values)


def solution(mesh):
    every = ("dp", "seq", "heads")
    token_spec = P(None, "dp", ("seq", "heads"), None)
    return jax.shard_map(
        on_device,
        mesh=mesh,
        in_specs=(
            token_spec,
            P(None, "dp", None),
            P(every),
            P(("dp", "seq"), "heads"),
            P(every, None),
            P(every),
            P(None, every),
            P(every),
            P(("dp", "seq"), "heads"),
            P(("dp", "seq"), "heads"),
            P("heads", ("dp", "seq")),
            token_spec,
        ),
        out_specs=(
            token_spec,
            token_spec,
            P(every),
            P(("dp", "seq"), "heads"),
            P(every, None),
            P(every),
            P(None, every),
            P(every),
            P(("dp", "seq"), "heads"),
            P(("dp", "seq"), "heads"),
            P("heads", ("dp", "seq")),
        ),
        check_vma=False,
    )
```

```python
import functools
import math

import jax
import jax.numpy as jnp
from jax import lax
from jax.experimental import pallas as pl
from jax.experimental.pallas import tpu as pltpu
from jax.sharding import PartitionSpec as P

QUERY_HEADS = 28
KEY_VALUE_HEADS = 7
HEAD_SIZE = 64
GROUP = QUERY_HEADS // KEY_VALUE_HEADS
GROUP_WIDTH = GROUP * HEAD_SIZE
Q_WIDTH = QUERY_HEADS * HEAD_SIZE
KV_WIDTH = 2 * KEY_VALUE_HEADS * HEAD_SIZE

EPSILON = 1e-06
SCORE_SCALE = 0.125
MASKED = -1e30
LANES = 128
CHUNK = 256
BLOCK = 256
FFN_ROWS = 256
ATTENTION_GAIN, FEED_GAIN, HEAD_GAIN = 0, 1, 2

BF = jnp.bfloat16
F32 = jnp.float32


def dot_nn(left, right):
    return lax.dot_general(left, right, (((1,), (0,)), ((), ())), preferred_element_type=F32)


def dot_nt(left, right):
    return lax.dot_general(left, right, (((1,), (1,)), ((), ())), preferred_element_type=F32)


def dot_tn(left, right):
    return lax.dot_general(left, right, (((0,), (0,)), ((), ())), preferred_element_type=F32)


def shape(dims, kind):
    return jax.ShapeDtypeStruct(dims, kind)


def whole(array):
    dims = array.shape
    return pl.BlockSpec(
        dims, lambda *unused: (0,) * len(dims), pipeline_mode=pl.Buffered(1)
    )


def fixed_out(dims):
    return pl.BlockSpec(dims, lambda *unused: (0,) * len(dims))


def kernel_call(body, name, grid, in_specs, out_specs, out_shape, scratch, flops, table=None):
    outs = out_shape if isinstance(out_shape, (list, tuple)) else [out_shape]
    moved = sum(math.prod(o.shape) * jnp.dtype(o.dtype).itemsize for o in outs)
    kwargs = dict(
        out_shape=out_shape,
        compiler_params=pltpu.CompilerParams(
            dimension_semantics=("arbitrary",) * len(grid), vmem_limit_bytes=56 * 1024 * 1024
        ),
        name=name,
    )

    def call(*operands):
        size = moved + sum(math.prod(o.shape) * o.dtype.itemsize for o in operands)
        cost = pl.CostEstimate(
            flops=flops,
            bytes_accessed=size,
            transcendentals=0,
        )
        if table is None:
            return pl.pallas_call(
                body,
                grid=grid,
                in_specs=in_specs,
                out_specs=out_specs,
                scratch_shapes=scratch,
                cost_estimate=cost,
                **kwargs,
            )(*operands)
        return pl.pallas_call(
            body,
            grid_spec=pltpu.PrefetchScalarGridSpec(
                num_scalar_prefetch=1,
                grid=grid,
                in_specs=in_specs,
                out_specs=out_specs,
                scratch_shapes=scratch,
            ),
            cost_estimate=cost,
            **kwargs,
        )(table, *operands)

    return call


def half_lanes(rows):
    return lax.broadcasted_iota(jnp.int32, (rows, LANES), 1) < HEAD_SIZE


def half_means(values, low):
    first = jnp.sum(jnp.where(low, values, 0.0), axis=1, keepdims=True) / HEAD_SIZE
    second = jnp.sum(jnp.where(low, 0.0, values), axis=1, keepdims=True) / HEAD_SIZE
    return jnp.where(low, first, second)


def turn(values):
    lane = lax.broadcasted_iota(jnp.int32, values.shape, 1)
    early = (lane & (HEAD_SIZE // 2)) == 0
    return jnp.where(
        early, pltpu.roll(values, LANES - HEAD_SIZE // 2, 1), pltpu.roll(values, HEAD_SIZE // 2, 1)
    )


def head_norm(tile, gain, cosine, sine, low):
    normed = tile * lax.rsqrt(half_means(tile * tile, low) + EPSILON) * gain
    return normed * cosine + turn(normed) * sine


def head_norm_back(tile, gain, cosine, sine, low, grad):
    grad = grad * cosine - turn(grad) * sine
    scale = lax.rsqrt(half_means(tile * tile, low) + EPSILON)
    lifted = grad * gain
    dots = half_means(tile * lifted, low)
    d_tile = scale * lifted - tile * (scale * scale * scale) * dots
    return d_tile, jnp.sum(grad * tile * scale, axis=0, keepdims=True)


def place(table, j):
    return pl.ds(pl.multiple_of(table[j] * BLOCK, BLOCK), BLOCK)


def span(j, size=BLOCK):
    return slice(j * size, (j + 1) * size)


def over_pieces(left, pieces, columns=None):
    total, start = None, 0
    for piece in pieces:
        size = piece.shape[0]
        right = piece[...] if columns is None else piece[:, columns]
        term = dot_nn(left[:, start : start + size], right)
        total = term if total is None else total + term
        start += size
    return total


def add_back(target, left, pieces, columns=None):
    start = 0
    for piece in pieces:
        size = piece.shape[0]
        right = piece[...] if columns is None else piece[:, columns]
        target[:, start : start + size] += dot_nt(left, right)
        start += size


def key_value_kernel(table, tokens, cosine, sine, gain, *refs):
    kvg = refs[:-4]
    normed, kv_raw, kv_low, gains = refs[-4:]
    rows, width = tokens.shape
    count = width // BLOCK
    columns = jnp.concatenate([part[:, KV_WIDTH:].astype(F32).T for part in kvg], axis=1)
    gains[...] = columns[:8]
    squares = 0.0
    for j in range(count):
        block = tokens[:, place(table, j)].astype(F32)
        squares = squares + jnp.sum(block * block, axis=1, keepdims=True)
    scale = lax.rsqrt(squares / width + EPSILON)
    for j in range(count):
        block = tokens[:, place(table, j)].astype(F32)
        normed[:, span(j)] = (
            block * scale * columns[ATTENTION_GAIN : ATTENTION_GAIN + 1, span(j)]
        ).astype(BF)
    raw = over_pieces(normed, kvg, slice(0, KV_WIDTH))
    kv_raw[...] = raw
    low = half_lanes(rows)
    for c in range(KEY_VALUE_HEADS):
        tile = raw[:, span(c, LANES)]
        key = head_norm(tile, gain[...], cosine[...], sine[...], low)
        kv_low[:, span(c, LANES)] = jnp.where(low, key, tile).astype(BF)


def project_key_value(table, tokens, cosine, sine, gain, kvg):
    rows, width = tokens.shape
    operands = (tokens, cosine, sine, gain, *kvg)
    return kernel_call(
        key_value_kernel,
        "project_key_value",
        (1,),
        [whole(o) for o in operands],
        [
            fixed_out((rows, width)),
            fixed_out((rows, KV_WIDTH)),
            fixed_out((rows, KV_WIDTH)),
            fixed_out((8, width)),
        ],
        [
            shape((rows, width), BF),
            shape((rows, KV_WIDTH), F32),
            shape((rows, KV_WIDTH), BF),
            shape((8, width), F32),
        ],
        [],
        2 * rows * width * KV_WIDTH,
        table,
    )(*operands)


def query_kernel(normed, cosine, sine, gain, *refs):
    q_raw, queries = refs[-2:]
    rows = normed.shape[0]
    raw = over_pieces(normed, refs[:-2])
    q_raw[...] = raw
    low = half_lanes(rows)
    for tile_index in range(GROUP_WIDTH // LANES):
        tile = raw[:, span(tile_index, LANES)]
        turned = head_norm(tile, gain[...], cosine[...], sine[...], low)
        queries[:, span(tile_index, LANES)] = (turned * SCORE_SCALE).astype(BF)


def column_parts(pieces):
    return [pl.BlockSpec((piece.shape[0], GROUP_WIDTH), lambda c, *t: (0, c)) for piece in pieces]


def project_query(normed, cosine, sine, gain, weight):
    rows, width = normed.shape
    out = pl.BlockSpec((rows, GROUP_WIDTH), lambda c: (0, c))
    return kernel_call(
        query_kernel,
        "project_query",
        (KEY_VALUE_HEADS,),
        [whole(normed), whole(cosine), whole(sine), whole(gain), *column_parts(weight)],
        [out, out],
        [shape((rows, Q_WIDTH), F32), shape((rows, Q_WIDTH), BF)],
        [],
        2 * rows * width * Q_WIDTH,
    )(normed, cosine, sine, gain, *weight)


def output_kernel(table, mixed, tokens, gains, *refs):
    hidden, feed = refs[-2:]
    width = hidden.shape[1]
    step = pl.program_id(0)

    @pl.when(step == 0)
    def _():
        for j in range(width // BLOCK):
            hidden[:, span(j)] = tokens[:, place(table, j)].astype(F32)

    add_back(hidden, mixed[...], refs[:-2])

    @pl.when(step == pl.num_programs(0) - 1)
    def _():
        values = hidden[...]
        scale = lax.rsqrt(jnp.mean(values * values, axis=1, keepdims=True) + EPSILON)
        feed[...] = (values * scale * gains[FEED_GAIN : FEED_GAIN + 1, :]).astype(BF)


def project_output(table, mixed, tokens, batch, gains, weight):
    rows = mixed.shape[0]
    width = tokens.shape[1]
    return kernel_call(
        output_kernel,
        "project_output",
        (KEY_VALUE_HEADS,),
        [
            pl.BlockSpec((rows, GROUP_WIDTH), lambda c, t: (0, c)),
            pl.BlockSpec((rows, width), lambda c, t: (batch, 0)),
            whole(gains),
            *column_parts(weight),
        ],
        [fixed_out((rows, width)), fixed_out((rows, width))],
        [shape((rows, width), F32), shape((rows, width), BF)],
        [],
        2 * rows * width * Q_WIDTH,
        table,
    )(mixed, tokens, gains, *weight)


def hidden_back_kernel(table, d_feed, hidden, cot, gains, *refs):
    d_hidden, d_attended, gain_grad, d_mixed = refs[-4:]
    width = hidden.shape[1]

    @pl.when(pl.program_id(0) == 0)
    def _():
        values = hidden[...]
        grad = d_feed[...].astype(F32)
        scale = lax.rsqrt(jnp.mean(values * values, axis=1, keepdims=True) + EPSILON)
        lifted = grad * gains[FEED_GAIN : FEED_GAIN + 1, :]
        dots = jnp.mean(values * lifted, axis=1, keepdims=True)
        d_norm = scale * lifted - values * (scale * scale * scale) * dots
        gain_grad[...] = jnp.broadcast_to(
            jnp.sum(grad * values * scale, axis=0, keepdims=True), gain_grad.shape
        )
        for j in range(width // BLOCK):
            total = cot[:, place(table, j)].astype(F32) + d_norm[:, span(j)]
            d_hidden[:, span(j)] = total
            d_attended[:, span(j)] = total.astype(BF)

    d_mixed[...] = over_pieces(d_attended, refs[:-4]).astype(BF)


def hidden_back(table, d_feed, hidden, cot, batch, gains, weight):
    rows, width = hidden.shape
    return kernel_call(
        hidden_back_kernel,
        "hidden_back",
        (KEY_VALUE_HEADS,),
        [
            whole(d_feed),
            whole(hidden),
            pl.BlockSpec((rows, width), lambda c, t: (batch, 0)),
            whole(gains),
            *column_parts(weight),
        ],
        [
            fixed_out((rows, width)),
            fixed_out((rows, width)),
            fixed_out((8, width)),
            pl.BlockSpec((rows, GROUP_WIDTH), lambda c, t: (0, c)),
        ],
        [
            shape((rows, width), F32),
            shape((rows, width), BF),
            shape((8, width), F32),
            shape((rows, Q_WIDTH), BF),
        ],
        [],
        2 * rows * width * Q_WIDTH,
        table,
    )(d_feed, hidden, cot, gains, *weight)


def query_back_kernel(d_q, *refs):
    out = refs[-1]

    @pl.when(pl.program_id(0) == 0)
    def _():
        out[...] = jnp.zeros_like(out)

    add_back(out, d_q[...], refs[:-1])


def query_back(d_q, weight):
    rows = d_q.shape[0]
    width = sum(piece.shape[0] for piece in weight)
    return kernel_call(
        query_back_kernel,
        "query_back",
        (KEY_VALUE_HEADS,),
        [pl.BlockSpec((rows, GROUP_WIDTH), lambda c: (0, c)), *column_parts(weight)],
        fixed_out((rows, width)),
        shape((rows, width), F32),
        [],
        2 * rows * width * Q_WIDTH,
    )(d_q, *weight)


def input_back_kernel(
    table,
    d_pair,
    kv_raw,
    cosine,
    sine,
    gain,
    d_normed_q,
    d_hidden0,
    d_hidden1,
    tokens,
    gains,
    *refs,
):
    kvg = refs[:-5]
    d_kv_raw, head_grad, tokens_grad, gain_grad, d_normed = refs[-5:]
    rows, width = tokens.shape
    part = d_hidden0.shape[0]
    low = half_lanes(rows)
    total = 0.0
    for c in range(KEY_VALUE_HEADS):
        grad = d_pair[:, span(c, LANES)].astype(F32)
        d_tile, g_tile = head_norm_back(
            kv_raw[:, span(c, LANES)], gain[...], cosine[...], sine[...], low, grad
        )
        total = total + g_tile
        d_kv_raw[:, span(c, LANES)] = jnp.where(low, d_tile, grad).astype(BF)
    head_grad[...] = jnp.broadcast_to(total, head_grad.shape)
    d_kv = d_kv_raw[...]
    d_normed[...] = d_normed_q[...]
    add_back(d_normed, d_kv, kvg, slice(0, KV_WIDTH))
    squares, dots = 0.0, 0.0
    for j in range(width // BLOCK):
        block = tokens[:, place(table, j)].astype(F32)
        lifted = d_normed[:, span(j)] * gains[ATTENTION_GAIN : ATTENTION_GAIN + 1, span(j)]
        squares = squares + jnp.sum(block * block, axis=1, keepdims=True)
        dots = dots + jnp.sum(block * lifted, axis=1, keepdims=True)
    scale = lax.rsqrt(squares / width + EPSILON)
    dots = dots / width * (scale * scale * scale)
    for j in range(width // BLOCK):
        block = tokens[:, place(table, j)].astype(F32)
        grad = d_normed[:, span(j)]
        lifted = grad * gains[ATTENTION_GAIN : ATTENTION_GAIN + 1, span(j)]
        d_input = scale * lifted - block * dots
        for batch, d_hidden in enumerate((d_hidden0, d_hidden1)):
            tokens_grad[span(batch, part), place(table, j)] = (
                d_hidden[:, span(j)] + d_input[span(batch, part), :]
            )
        gain_grad[:, span(j)] = jnp.broadcast_to(
            jnp.sum(grad * block * scale, axis=0, keepdims=True), (8, BLOCK)
        )


def input_back(table, *operands):
    tokens = operands[8]
    rows, width = tokens.shape
    return kernel_call(
        input_back_kernel,
        "input_back",
        (1,),
        [whole(o) for o in operands],
        [
            fixed_out((rows, KV_WIDTH)),
            fixed_out((8, LANES)),
            fixed_out((rows, width)),
            fixed_out((8, width)),
        ],
        [
            shape((rows, KV_WIDTH), BF),
            shape((8, LANES), F32),
            shape((rows, width), F32),
            shape((8, width), F32),
        ],
        [pltpu.VMEM((rows, width), F32)],
        2 * rows * width * KV_WIDTH,
        table,
    )(*operands)


def layer_out_kernel(table, hidden0, hidden1, added0, added1, out):
    part = hidden0.shape[0]
    for batch, (hidden, added) in enumerate(((hidden0, added0), (hidden1, added1))):
        for j in range(hidden.shape[1] // BLOCK):
            out[span(batch, part), place(table, j)] = (
                hidden[:, span(j)] + added[:, span(j)].astype(F32)
            ).astype(BF)


def finish_layer(table, *operands):
    rows, width = operands[0].shape
    return kernel_call(
        layer_out_kernel,
        "finish_layer",
        (1,),
        [whole(o) for o in operands],
        fixed_out((2 * rows, width)),
        shape((2 * rows, width), BF),
        [],
        0,
        table,
    )(*operands)


def key_value_grad_kernel(normed, d_kv_raw, gain_grads, out0, out1):
    half = normed.shape[1] // 2
    for index, out in enumerate((out0, out1)):
        cut = span(index, half)
        out[:, :KV_WIDTH] = dot_tn(normed[:, cut], d_kv_raw[...]).astype(BF)
        rows = gain_grads[:, cut]
        rows = jnp.concatenate([rows, jnp.zeros((LANES - 8, half), F32)], axis=0)
        out[:, KV_WIDTH:] = rows.T.astype(BF)


def key_value_grad(normed, d_kv_raw, gain_grads):
    rows, width = normed.shape
    dims = (width // 2, KV_WIDTH + LANES)
    return kernel_call(
        key_value_grad_kernel,
        "key_value_grad",
        (1,),
        [whole(normed), whole(d_kv_raw), whole(gain_grads)],
        [fixed_out(dims), fixed_out(dims)],
        [shape(dims, BF), shape(dims, BF)],
        [],
        2 * rows * width * KV_WIDTH,
    )(normed, d_kv_raw, gain_grads)


def pad_heads(tile, low, keep_low):
    parts = []
    for pair in range(GROUP // 2):
        both = tile[:, span(pair, LANES)].astype(F32)
        turned = pltpu.roll(both, HEAD_SIZE, 1)
        first, second = (both, turned) if keep_low else (turned, both)
        keep = low if keep_low else jnp.logical_not(low)
        parts.append(jnp.where(keep, first, 0.0))
        parts.append(jnp.where(keep, second, 0.0))
    return jnp.concatenate(parts, axis=0).astype(BF)


def four_wide(row):
    return jnp.concatenate([row] * GROUP, axis=1)


def heads_back(stacked, rows):
    parts = []
    for pair in range(GROUP // 2):
        start = 2 * pair * rows
        both = jnp.concatenate(
            [stacked[:, start : start + rows], stacked[:, start + rows : start + 2 * rows]], axis=0
        )
        parts.append(both.T)
    return jnp.concatenate(parts, axis=1)


def key_rows(kv, cut):
    rows = kv.shape[2]
    block = kv[cut.start // rows : cut.stop // rows, 0]
    return block.reshape(cut.stop - cut.start, kv.shape[3])


def every_row(kv):
    return key_rows(kv, slice(0, kv.shape[0] * kv.shape[2]))


def ones_and_values(kv):
    values = every_row(kv)
    return jnp.where(half_lanes(values.shape[0]), 1.0, values.astype(F32)).astype(BF)


def attention_forward_kernel(kv0, kv1, query, bias0, bias1, mixed, lse, expo):
    rows = query.shape[0]
    half = bias0.shape[0]
    padded = pad_heads(query[...], half_lanes(rows), True)
    for part, (kv, bias) in enumerate(((kv0, bias0), (kv1, bias1))):
        for step in range(half // CHUNK):
            cut = span(step, CHUNK)
            weight = jnp.exp(dot_nt(key_rows(kv, cut), padded) + four_wide(bias[cut, :]))
            expo[part * half + step * CHUNK : part * half + (step + 1) * CHUNK, :] = weight.astype(BF)
    total = dot_tn(ones_and_values(kv0), expo[:half, :]) + dot_tn(
        ones_and_values(kv1), expo[half:, :]
    )
    lse[...] = jnp.log(total[0:1, :])[None]
    mixed[...] = heads_back(total[HEAD_SIZE:, :] / total[:HEAD_SIZE, :], rows).astype(BF)


def attention_forward(kv0, kv1, query, batch, bias0, bias1):
    half, rows = bias0.shape
    wide = GROUP * rows
    keys = pl.BlockSpec((half // rows, 1, rows, LANES), lambda c: (0, batch, 0, c))
    kv0, kv1 = (kv.reshape(half // rows, -1, rows, KV_WIDTH) for kv in (kv0, kv1))
    return kernel_call(
        attention_forward_kernel,
        "attention_forward",
        (KEY_VALUE_HEADS,),
        [
            keys,
            keys,
            pl.BlockSpec((rows, GROUP_WIDTH), lambda c: (batch, c)),
            whole(bias0),
            whole(bias1),
        ],
        [
            pl.BlockSpec((rows, GROUP_WIDTH), lambda c: (0, c)),
            pl.BlockSpec((1, 1, wide), lambda c: (c, 0, 0)),
        ],
        [shape((rows, Q_WIDTH), BF), shape((KEY_VALUE_HEADS, 1, wide), F32)],
        [pltpu.VMEM((2 * half, wide), BF)],
        KEY_VALUE_HEADS * 2 * half * wide * LANES * 12,
    )(kv0, kv1, query, bias0, bias1)


def attention_backward_kernel(
    kv0,
    kv1,
    query,
    mixed,
    d_mixed,
    bias0,
    bias1,
    lse,
    q_raw,
    cosine,
    sine,
    gain,
    d_q_raw,
    d_kv0,
    d_kv1,
    gain_grad,
    d_scores,
):
    rows = query.shape[0]
    half = bias0.shape[0]
    low = half_lanes(rows)
    padded = pad_heads(query[...], low, True)
    d_padded = pad_heads(d_mixed[...], low, False)
    product = d_mixed[...].astype(F32) * mixed[...].astype(F32)
    pick = (
        lax.broadcasted_iota(jnp.int32, (8, GROUP_WIDTH), 1) // HEAD_SIZE
        == lax.broadcasted_iota(jnp.int32, (8, GROUP_WIDTH), 0)
    ).astype(F32)
    balance = lax.dot_general(
        pick,
        product,
        (((1,), (1,)), ((), ())),
        precision=lax.Precision.HIGHEST,
        preferred_element_type=F32,
    )
    balance = jnp.concatenate([balance[head : head + 1, :] for head in range(GROUP)], axis=1)
    level = lse[0]
    for part, (kv, bias, d_kv) in enumerate(((kv0, bias0, d_kv0), (kv1, bias1, d_kv1))):
        for step in range(half // CHUNK):
            cut = span(step, CHUNK)
            block = key_rows(kv, cut)
            probs = jnp.exp(dot_nt(block, padded) + four_wide(bias[cut, :]) - level)
            d_probs = dot_nt(block, d_padded)
            low_scores = (probs * (d_probs - balance)).astype(BF)
            d_scores[part * half + step * CHUNK : part * half + (step + 1) * CHUNK, :] = low_scores
            d_kv[cut, :] = (
                dot_nn(low_scores, padded) + dot_nn(probs.astype(BF), d_padded)
            ).astype(BF)
    total = dot_tn(every_row(kv0), d_scores[:half, :]) + dot_tn(
        every_row(kv1), d_scores[half:, :]
    )
    d_query = heads_back(total[:HEAD_SIZE, :] * SCORE_SCALE, rows)
    grads = 0.0
    for tile_index in range(GROUP_WIDTH // LANES):
        cut = span(tile_index, LANES)
        d_tile, g_tile = head_norm_back(
            q_raw[:, cut], gain[...], cosine[...], sine[...], low, d_query[:, cut]
        )
        d_q_raw[:, cut] = d_tile.astype(BF)
        grads = grads + g_tile

    @pl.when(pl.program_id(0) == 0)
    def _():
        gain_grad[...] = jnp.zeros_like(gain_grad)

    gain_grad[...] += jnp.broadcast_to(grads, gain_grad.shape)


def attention_backward(
    kv0, kv1, query, batch, mixed, d_mixed, bias0, bias1, lse, q_raw, cosine, sine, gain
):
    half, rows = bias0.shape
    wide = GROUP * rows
    keys = pl.BlockSpec((half // rows, 1, rows, LANES), lambda c: (0, batch, 0, c))
    kv0, kv1 = (kv.reshape(half // rows, -1, rows, KV_WIDTH) for kv in (kv0, kv1))
    d_keys = pl.BlockSpec((half, LANES), lambda c: (0, c))
    heads = pl.BlockSpec((rows, GROUP_WIDTH), lambda c: (0, c))
    part = pl.BlockSpec((rows, GROUP_WIDTH), lambda c: (batch, c))
    table = pl.BlockSpec((rows, LANES), lambda c: (batch, 0))
    return kernel_call(
        attention_backward_kernel,
        "attention_backward",
        (KEY_VALUE_HEADS,),
        [
            keys,
            keys,
            part,
            heads,
            heads,
            whole(bias0),
            whole(bias1),
            pl.BlockSpec((1, 1, wide), lambda c: (c, 0, 0)),
            part,
            table,
            table,
            whole(gain),
        ],
        [heads, d_keys, d_keys, fixed_out((8, LANES))],
        [
            shape((rows, Q_WIDTH), BF),
            shape((half, KV_WIDTH), BF),
            shape((half, KV_WIDTH), BF),
            shape((8, LANES), F32),
        ],
        [pltpu.VMEM((2 * half, wide), BF)],
        KEY_VALUE_HEADS * 2 * half * wide * LANES * 28,
    )(kv0, kv1, query, mixed, d_mixed, bias0, bias1, lse, q_raw, cosine, sine, gain)


def swap_halves(values):
    half = values.shape[1] // 2
    return jnp.concatenate([values[:, half:], values[:, :half]], axis=1)


def feed_forward_kernel(count, units, *refs):
    feed0, feed1, cot0, cot1 = refs[:4]
    gate_up = refs[4 : 4 + count]
    down = refs[4 + count : 4 + 2 * count]
    act_out, d_units_out, out0, out1, d_feed0, d_feed1 = refs[4 + 2 * count :]
    first = pl.program_id(0) < pl.num_programs(0) // 2
    rows, width = feed0.shape
    half = width // 2
    size = down[0].shape[0] // 2
    feed = jnp.where(first, swap_halves(feed0[...]), feed1[...])
    cot = jnp.where(first, swap_halves(cot0[...]), cot1[...])

    def over(left, pieces):
        total = None
        for b, piece in enumerate(pieces):
            both = jnp.concatenate(
                [left[:, b * size : (b + 1) * size], left[:, half + b * size : half + (b + 1) * size]],
                axis=1,
            )
            term = dot_nn(both, piece[...])
            total = term if total is None else total + term
        return total

    both = over(feed, gate_up)
    gate_pre, up_pre = both[:, :units], both[:, units : 2 * units]
    sig = 1.0 / (1.0 + jnp.exp(-gate_pre))
    silu = gate_pre * sig
    act = (silu * up_pre).astype(BF)
    act = jnp.concatenate([act, jnp.zeros((rows, down[0].shape[1] - units), BF)], axis=1)
    act_out[...] = act
    d_act = over(cot, down)[:, :units]
    d_gate = d_act * up_pre * (sig * (1.0 + gate_pre * (1.0 - sig)))
    d_units = jnp.concatenate(
        [
            d_gate.astype(BF),
            (d_act * silu).astype(BF),
            jnp.zeros((rows, gate_up[0].shape[1] - 2 * units), BF),
        ],
        axis=1,
    )
    d_units_out[...] = d_units

    def write(target, left, pieces, swapped):
        for b, piece in enumerate(pieces):
            block = dot_nt(left, piece[...]).astype(BF)
            early, late = (half, 0) if swapped else (0, half)
            target[:, early + b * size : early + (b + 1) * size] = block[:, :size]
            target[:, late + b * size : late + (b + 1) * size] = block[:, size:]

    @pl.when(first)
    def _():
        write(d_feed0, d_units, gate_up, True)
        write(out0, act, down, True)

    @pl.when(jnp.logical_not(first))
    def _():
        write(d_feed1, d_units, gate_up, False)
        write(out1, act, down, False)


def feed_forward(feeds, cots, gate_up, down, units):
    tokens, width = feeds[0].shape
    steps = tokens // FFN_ROWS
    early = pl.BlockSpec((FFN_ROWS, width), lambda i: (jnp.minimum(i, steps - 1), 0))
    late = pl.BlockSpec((FFN_ROWS, width), lambda i: (jnp.maximum(i - steps, 0), 0))
    act_width, units_width = down[0].shape[1], gate_up[0].shape[1]
    return kernel_call(
        functools.partial(feed_forward_kernel, len(down), units),
        "feed_forward",
        (2 * steps,),
        [early, late, early, late, *[whole(w) for w in (*gate_up, *down)]],
        [
            pl.BlockSpec((FFN_ROWS, act_width), lambda i: (i, 0)),
            pl.BlockSpec((FFN_ROWS, units_width), lambda i: (i, 0)),
            early,
            late,
            early,
            late,
        ],
        [
            shape((2 * tokens, act_width), BF),
            shape((2 * tokens, units_width), BF),
            *[shape((tokens, width), BF)] * 4,
        ],
        [],
        2 * tokens * 2 * width * units * 6,
    )(*feeds, *cots, *gate_up, *down)


def weight_grad_kernel(count, columns, *refs):
    lefts = refs[: 2 * count]
    rights = refs[2 * count : -1]
    out = refs[-1]
    rows = lefts[0].shape[0]
    each = count // len(rights)
    total = None
    for index in range(count):
        left = jnp.concatenate([lefts[2 * index][...], lefts[2 * index + 1][...]], axis=1)
        right = rights[index // each]
        term = dot_tn(left, right[span(index % each, rows), columns])
        total = term if total is None else total + term
    out[...] = total.astype(BF)


def weight_grad(lefts, rights, columns, steps, stride, offset):
    rows, width = lefts[0].shape
    units = columns.stop - columns.start
    half = width // 2 // BLOCK
    mine = pl.BlockSpec((rows, BLOCK), lambda i: (0, i * stride + offset))
    other = pl.BlockSpec((rows, BLOCK), lambda i: (0, half + i * stride + offset))
    specs, operands = [], []
    for index, left in enumerate(lefts):
        specs += [other, mine] if index % 2 == 0 else [mine, other]
        operands += [left, left]
    return kernel_call(
        functools.partial(weight_grad_kernel, len(lefts), columns),
        "weight_grad",
        (steps,),
        [*specs, *[whole(r) for r in rights]],
        pl.BlockSpec((2 * BLOCK, units), lambda i: (i, 0)),
        shape((2 * BLOCK * steps, units), BF),
        [],
        2 * len(lefts) * rows * 2 * BLOCK * steps * units,
    )(*operands, *rights)


def rotary_tables(places):
    half_width = HEAD_SIZE // 2
    freqs = jnp.exp(jnp.arange(half_width, dtype=F32) * (-2.0 * math.log(10000.0) / HEAD_SIZE))
    angles = places.astype(F32)[:, None] * freqs[None, :]
    cosine, sine = jnp.cos(angles), jnp.sin(angles)
    return (
        jnp.concatenate([cosine] * 4, axis=1),
        jnp.concatenate([-sine, sine, -sine, sine], axis=1),
    )


def padded_columns(values, columns):
    return jnp.pad(values, ((0, 0), (0, columns - values.shape[1])))


def up_to(size):
    return -(-size // LANES) * LANES


def on_device(
    tokens,
    lengths,
    attention_gain,
    query_weight,
    key_value_matrix,
    per_head_gains,
    output_weight,
    feed_gain,
    gate_weight,
    up_weight,
    down_weight,
    cotangent,
):
    batches = tokens.shape[0]
    rows = tokens.shape[2]
    width = tokens.shape[3]
    dp_size = lax.axis_size("dp")
    heads_size = lax.axis_size("heads")
    seq_size = lax.axis_size("seq")
    assert seq_size == 4 and heads_size == 4 and batches == 2
    paired = dp_size == 2
    y = lax.axis_index("dp").astype(jnp.int32)
    s = lax.axis_index("seq").astype(jnp.int32)
    z = lax.axis_index("heads").astype(jnp.int32)
    x = s // 2
    core = s % 2

    def after(v, *others):
        return lax.optimization_barrier((v, others))[0]

    def beside(outs, parts):
        return lax.optimization_barrier((outs, parts))

    def swap_x(v):
        return lax.ppermute(v, "seq", [(i, i ^ 2) for i in range(4)])

    def swap_xy(v):
        return lax.ppermute(v, ("dp", "seq"), [(i, i ^ 6) for i in range(8)])

    def swap_core(v):
        return lax.ppermute(v, "seq", [(i, i ^ 1) for i in range(4)])

    def swap_y(v):
        return lax.ppermute(v, "dp", [(0, 1), (1, 0)])

    def line_scatter(v, axis):
        cut = jnp.split(v, 4, axis=axis)
        total = lax.select_n(z, *cut)
        for k in range(1, 4):
            block = lax.select_n(z, *[cut[i ^ k] for i in range(4)])
            total = total + lax.ppermute(block, "heads", [(i, i ^ k) for i in range(4)])
        return total

    def gather_near(v):
        if not paired:
            both = jnp.stack([v, swap_x(v)], axis=0)
            return [lax.all_gather(both, "dp", axis=0).reshape(-1, v.shape[-1])]
        return [v, swap_x(v), swap_y(v)]

    def gather_far(near, x_first):
        if not paired:
            return near
        return [*near, swap_y(near[1]) if x_first else swap_x(near[2])]

    def pair_gather(v, axis):
        def step(u, upper, distance):
            got = lax.ppermute(u, "heads", [(i, i ^ distance) for i in range(4)])
            return jnp.where(
                upper,
                jnp.concatenate([got, u], axis=axis),
                jnp.concatenate([u, got], axis=axis),
            )

        return step(step(v, z % 2 == 1, 1), z >= 2, 2)

    def both_cores(pieces):
        return [*pieces, *[swap_core(v) for v in pieces]]

    def unit_pieces(pieces):
        if paired:
            return pieces
        g = pieces[0].reshape(blocks, 2, -1, pieces[0].shape[-1])
        return [g.transpose(1, 0, 2, 3).reshape(pieces[0].shape)]

    def scatter_yx(g, x_last, first=(), second=()):
        def along_x(u, late):
            return u[..., 0, :, :] + after(swap_x(u[..., 1, :, :]), late)

        def along_y(u, late):
            if paired:
                return u[0] + after(swap_y(u[1]), late)
            return lax.psum_scatter(u, "dp", scatter_dimension=0)

        if x_last:
            return along_x(along_y(g, first), second)
        return along_y(along_x(g, first), second)

    blocks = 2 * dp_size
    piece = width // blocks

    if paired:
        own = (2 * y + x) * 2 + core
        places_of = jnp.array([b * 2 + c for c in range(2) for b in range(4)], jnp.int32)
        table = places_of ^ own

        def to_order(v):
            return v

        from_order = to_order
    else:
        table = jnp.arange(width // BLOCK, dtype=jnp.int32)

        def flip(v):
            u = v.reshape(v.shape[:-1] + (dp_size, 2, 2, piece // 2))
            u = jnp.where(x == 1, u[..., ::-1, :, :], u)
            return jnp.where(core == 1, u[..., ::-1, :], u)

        def to_order(v):
            return jnp.moveaxis(flip(v), -2, -4).reshape(v.shape)

        def from_order(v):
            u = v.reshape(v.shape[:-1] + (2, dp_size, 2, piece // 2))
            return flip(jnp.moveaxis(u, -4, -2).reshape(v.shape)).reshape(v.shape)

    def small_order(v, back):
        if not paired:
            return from_order(v) if back else to_order(v)
        cut = v.reshape(8, -1)
        return jnp.concatenate(
            [
                lax.select_n(own, *[cut[held(i, m, back)] for m in range(8)])
                for i in range(8)
            ]
        ).reshape(v.shape)

    def held(i, m, back):
        if back:
            source = i ^ m
            return (source % 2) * 4 + source // 2
        return ((i % 4) * 2 + i // 4) ^ m

    small = key_value_matrix.shape[0]
    per_head = per_head_gains.shape[0]
    kv_local = (
        key_value_matrix.reshape(small, 2, KEY_VALUE_HEADS, HEAD_SIZE)
        .transpose(0, 2, 1, 3)
        .reshape(small, KV_WIDTH)
    )
    gains_local = jnp.stack(
        [attention_gain, feed_gain, jnp.pad(per_head_gains, (0, small - per_head))], axis=1
    )
    kvg_local = jnp.concatenate([kv_local, padded_columns(gains_local, LANES)], axis=1)
    kvg_rows = pair_gather(kvg_local, 0)
    kvg_near = gather_near(kvg_rows)

    tokens_in = to_order(tokens[:, 0].reshape(batches * rows, width))
    cot_in = to_order(cotangent[:, 0].reshape(batches * rows, width))
    cot_held = order_columns(table, cot_in) if paired else cot_in
    lined = lax.all_gather(
        jnp.concatenate(
            [
                cot_held,
                padded_columns(query_weight.reshape(small, Q_WIDTH), width),
                padded_columns(output_weight.T, width),
            ],
            axis=0,
        ),
        "heads",
        axis=0,
    )
    cots_mine = [
        lined[:, span(batch, rows)].reshape(heads_size * rows, width) for batch in range(batches)
    ]
    q_rows = (
        lined[:, batches * rows : batches * rows + small, :Q_WIDTH]
        .reshape(heads_size, query_weight.shape[0], query_weight.shape[1])
        .transpose(1, 0, 2)
        .reshape(query_weight.shape[0], Q_WIDTH)
    )
    o_rows = lined[:, batches * rows + small :, :Q_WIDTH].reshape(4 * small, Q_WIDTH)
    units = gate_weight.shape[1] // 2
    act_width, units_width = up_to(units), up_to(2 * units)

    def unit_half(v, which):
        return jnp.where(which == 0, v[:, :units], v[:, units:])

    down_local = down_weight.T

    def halves(which):
        gate_up = jnp.concatenate([unit_half(gate_weight, which), unit_half(up_weight, which)], axis=1)
        return jnp.concatenate(
            [padded_columns(gate_up, units_width), padded_columns(unit_half(down_local, which), act_width)],
            axis=1,
        )

    keep = halves(core)
    take = swap_core(halves(1 - core))
    ffn_rows = jnp.concatenate([keep, take], axis=0)
    down_near = gather_near(ffn_rows[:, units_width:])
    gate_up_near = gather_near(after(ffn_rows[:, :units_width], kvg_near))
    gate_up = unit_pieces(gather_far(gate_up_near, True))
    kvg = both_cores(gather_far(after(kvg_near, down_near), True))

    head_column = jnp.concatenate([part[:, KV_WIDTH + HEAD_GAIN] for part in kvg])
    head_scale = small_order(head_column.astype(F32)[None], True)
    head_scale = head_scale.reshape(-1, small)[:, :per_head].reshape(1, -1)
    query_gain = jnp.concatenate([head_scale[:, :HEAD_SIZE]] * 2, axis=1)
    key_gain = jnp.concatenate([head_scale[:, HEAD_SIZE:]] * 2, axis=1)

    block_rows = rows * heads_size
    spots = s * block_rows + z * rows + jnp.arange(rows, dtype=jnp.int32)
    inside = jnp.arange(rows, dtype=jnp.int32)

    def key_spots(first):
        lines = jnp.arange(heads_size, dtype=jnp.int32)[:, None, None] * rows
        fronts = jnp.stack([first, first ^ 2])[None, :, None] * block_rows
        return (lines + fronts + inside[None, None, :]).reshape(-1)

    def bias_for(begin, first):
        keys = key_spots(first)[:, None]
        return jnp.where((keys <= spots[None, :]) & (keys >= begin[None, :]), 0.0, MASKED)

    begins, biases = [], []
    for batch in range(batches):
        sizes = lengths[batch, 0]
        finish = jnp.cumsum(sizes)
        begin = jnp.sum(
            jnp.where(spots[:, None] >= finish[None, :], sizes[None, :], 0), axis=1
        ).astype(jnp.int32)
        begins.append(begin)
        biases.append((bias_for(begin, s), bias_for(begin, s ^ 1)))
    cosine, sine = rotary_tables(jnp.concatenate([spots - begin for begin in begins]))

    normed, kv_raw, kv_low, gains = project_key_value(
        table, after(tokens_in, down_near), cosine, sine, key_gain, kvg
    )
    kv_pair = jnp.concatenate([kv_low, swap_x(kv_low)], axis=0)
    kv_lined = lax.all_gather(after(kv_pair, gate_up_near), "heads", axis=0, tiled=True)
    down = unit_pieces(gather_far(down_near, False))
    q_near = gather_near(q_rows)
    q_full = both_cores(gather_far(q_near, False))
    o_near = gather_near(after(o_rows, q_near))
    q_raw, queries = project_query(after(normed, o_near), cosine, sine, query_gain, q_full)
    o_pieces = gather_far(after(o_near, queries), True)
    kv_lined = after(kv_lined, queries)
    kvs = (kv_lined, swap_core(kv_lined))

    feeds, mixeds, lses, hiddens = [], [], [], []
    for batch in range(batches):
        query = queries if batch == 0 else after(queries, hiddens[0])
        mixed, lse = attention_forward(*kvs, query, batch, *biases[batch])
        if batch == 0:
            o_full = both_cores(after(o_pieces, mixed))
        else:
            (mixed, lse), (gate_up, down) = beside((mixed, lse), (gate_up, down))
        hidden_in, feed_rows = project_output(
            table, mixed, tokens_in, batch, gains, o_full
        )
        feeds.append(lax.all_gather(feed_rows, "heads", axis=0, tiled=True))
        mixeds.append(mixed)
        lses.append(lse)
        hiddens.append(hidden_in)

    feeds[0] = after(feeds[0], feed_rows)
    feeds = [(swap_core(v), v) for v in feeds]

    d_feeds, acts, d_units, cots, outs = [], [], [], [], []
    for batch in range(batches):
        cot_pair = (swap_core(cots_mine[batch]), cots_mine[batch])
        act, d_unit, out_other, out_mine, d_feed_other, d_feed_mine = feed_forward(
            feeds[batch], cot_pair, gate_up, down, units
        )
        acts.append(act)
        d_units.append(d_unit)
        cots.append(cot_pair)
        outs.append((out_mine, out_other))
        d_feed = d_feed_mine + swap_core(d_feed_other)
        if batch + 1 < batches:
            d_feed = after(d_feed, feeds[batch + 1])
        d_feeds.append(lax.psum_scatter(d_feed, "heads", scatter_dimension=0, tiled=True))

    feed_all = [f for pair in feeds for f in pair]
    cot_all = [c for pair in cots for c in pair]
    count = width // 2 // BLOCK

    def unit_order(g):
        g = g.reshape(count, 2, BLOCK, -1).transpose(1, 0, 2, 3)
        g = g.reshape(2, blocks, piece // 2, -1).transpose(1, 0, 2, 3)
        return g.reshape(dp_size, 2, piece, -1)

    cut_at = up_to(units)

    def both_grads(left, right):
        return [dot_tn(left[:, span(i, width // 2)], right).astype(BF) for i in range(2)]

    def split_rows(mine, got, along_y=True):
        if not paired:
            return mine + got, None
        size = mine.shape[0] // 4
        far = (2, 3) if along_y else (1, 3)
        near = (0, 1) if along_y else (0, 2)

        def pick(v, blocks_of):
            return jnp.concatenate([v[span(b, size)] for b in blocks_of], axis=0)

        return pick(mine, far) + pick(got, far), pick(mine, near) + pick(got, near)

    def send_parts(v, swap, *rows_of):
        parts, start = [], 0
        for size in rows_of:
            parts.append(swap(v[start : start + size]))
            start += size
        assert start == v.shape[0]
        return parts

    def halved(total):
        near = total.shape[0] // 2
        return total[near:], total[:near]

    def fold(parts, kept, *late):
        return halved(kept + after(jnp.concatenate(parts, axis=0), late))

    def fold_whole(sent):
        g = sent.reshape(dp_size, 2, -1, sent.shape[-1])
        g = lax.psum_scatter(g, "dp", scatter_dimension=0)
        return g[0] + swap_x(g[1])

    added = [out_mine + swap_core(out_other) for out_mine, out_other in outs]
    d_hiddens, d_attendeds, d_q_raws, d_lined = [], [], [], []
    feed_gain_grads, query_gain_grads = [], []
    mixed_all = jnp.concatenate(mixeds, axis=0)
    first_cut, second_cut = slice(0, cut_at), slice(cut_at, up_to(2 * units))
    if paired:
        first_far = weight_grad(feed_all, d_units, first_cut, 2, 1, 2)
        first_parts = send_parts(first_far, swap_y, 384, 640)
        second_far = weight_grad(feed_all, after(d_units, first_far), second_cut, 2, 2, 1)
        second_parts = send_parts(second_far, swap_x, 384, 640)
        d_feeds[0] = after(d_feeds[0], second_far)
    for batch in range(batches):
        d_feed = d_feeds[batch]
        if batch == 1:
            d_feed = after(d_feed, d_q_raws[0])
            if paired:
                tied = after(acts, d_q_raws[0], added)
                down_far = weight_grad(cot_all, tied, slice(0, act_width), 2, 2, 1)
                down_parts = send_parts(down_far, swap_x, 256, 640, 128)
                d_feed = after(d_feed, down_far, last_kv)
        back = hidden_back(table, d_feed, hiddens[batch], cot_in, batch, gains, o_full)
        if paired and batch == 0:
            back, (first_parts[0], second_parts[0]) = beside(
                back, (first_parts[0], second_parts[0])
            )
        if paired and batch == 1:
            back, down_parts[0] = beside(back, down_parts[0])
        d_hidden, d_attended, feed_grad, d_mixed = back
        d_hiddens.append(d_hidden)
        d_attendeds.append(d_attended)
        if batch == 1:
            o_grads = both_grads(jnp.concatenate(d_attendeds, axis=0), mixed_all)
            o_send, o_keep = split_rows(o_grads[0], swap_core(o_grads[1]))
            d_mixed = after(d_mixed, o_send)
            if paired:
                o_parts = send_parts(o_send, swap_y, 256, 128, 128)
        back = attention_backward(
            *kvs,
            queries,
            batch,
            mixeds[batch],
            d_mixed,
            *biases[batch],
            lses[batch],
            q_raw,
            cosine,
            sine,
            query_gain,
        )
        if paired and batch == 0:
            back, (first_parts[1], second_parts[1]) = beside(
                back, (first_parts[1], second_parts[1])
            )
        if paired and batch == 1:
            back, (down_parts[1], o_parts[0]) = beside(back, (down_parts[1], o_parts[0]))
        d_q_raw, d_kv0, d_kv1, query_grad = back
        d_kv = d_kv0 + swap_core(d_kv1)
        last_kv = d_kv
        d_lined.append(lax.psum_scatter(d_kv, "heads", scatter_dimension=0, tiled=True))
        d_q_raws.append(d_q_raw)
        feed_gain_grads.append(feed_grad)
        query_gain_grads.append(query_grad)

    pairs_got = [swap_x(d_lined[0][rows:])]
    d_q_raw_all = jnp.concatenate(d_q_raws, axis=0)
    q_grads = both_grads(after(normed, last_kv), d_q_raw_all)
    if paired:
        q_grads, (down_parts[2], o_parts[1], pairs_got) = beside(
            q_grads, (down_parts[2], o_parts[1], pairs_got)
        )
    q_send, q_keep = split_rows(q_grads[0], swap_core(q_grads[1]), False)
    d_normed_q = query_back(after(d_q_raw_all, q_send), q_full)
    if paired:
        q_parts = send_parts(q_send[: 2 * LANES], swap_x, 128, 128)
        d_normed_q, (q_parts[0], o_parts[2]) = beside(d_normed_q, (q_parts[0], o_parts[2]))
        tied = after(d_units, d_normed_q)
        second_half = weight_grad(feed_all, tied, second_cut, 2, 2, 0)
        second_half, q_parts[1] = beside(second_half, q_parts[1])
        second_half = second_half + jnp.concatenate(second_parts, axis=0)
        second_last = send_parts(second_half[2 * BLOCK :], swap_y, 320, 192)
        d_lined[1] = after(d_lined[1], second_half)
        pairs_got.append(swap_x(d_lined[1][rows:]))
        q_parts += send_parts(after(q_send[2 * LANES :], pairs_got[1]), swap_x, 128, 128)
    else:
        every_unit = slice(0, units_width)
        g_gate_up = scatter_yx(
            unit_order(weight_grad(feed_all, d_units, every_unit, count, 1, 0)), True
        )
        g_down = scatter_yx(
            unit_order(weight_grad(cot_all, acts, slice(0, act_width), count, 1, 0)), False
        )
        pairs_got.append(swap_x(d_lined[1][rows:]))
    d_pair_all = jnp.concatenate(
        [pair[:rows] + got for pair, got in zip(d_lined, pairs_got)], axis=0
    )

    back = input_back(
        table,
        d_pair_all,
        kv_raw,
        cosine,
        sine,
        key_gain,
        d_normed_q,
        *d_hiddens,
        tokens_in,
        gains,
        *kvg,
    )
    if paired:
        back, (q_parts[2], second_last[0]) = beside(back, (q_parts[2], second_last[0]))
    d_kv_raw, key_grad, tokens_grad, attention_grad = back
    query_grad = query_gain_grads[0][0] + query_gain_grads[1][0]
    head_grads = jnp.concatenate(
        [query_grad[:HEAD_SIZE] + query_grad[HEAD_SIZE:], key_grad[0, :HEAD_SIZE]]
    ).reshape(-1, per_head)
    head_row = small_order(
        jnp.pad(head_grads, ((0, 0), (0, small - per_head))).reshape(1, width), False
    )
    gain_grads = jnp.concatenate(
        [
            attention_grad[0:1],
            feed_gain_grads[0][0:1] + feed_gain_grads[1][0:1],
            head_row,
            jnp.zeros((5, width), F32),
        ],
        axis=0,
    )
    kv_grads = key_value_grad(normed, d_kv_raw, gain_grads)
    if paired:
        kv_grads, second_last[1] = beside(kv_grads, second_last[1])
        o_send, o_keep = fold(o_parts, o_keep, d_kv_raw)
        kv_got = swap_core(kv_grads[1])
        kv_sums = [kv_grads[0][span(b)] + kv_got[span(b)] for b in range(4)]
        kv_parts = [swap_x(kv_sums[1]), swap_y(kv_sums[2]), swap_xy(kv_sums[3])]
        o_got = swap_x(after(o_send, kv_sums))
        tied = after(acts, kv_sums)
        half = weight_grad(cot_all, tied, slice(0, act_width), 2, 2, 0)
        half, q_parts[3] = beside(half, q_parts[3])
        q_send, q_keep = fold(q_parts, q_keep)
        q_got = swap_y(q_send)
        half = half + jnp.concatenate(down_parts, axis=0)
        tied = after(d_units, half, q_send)
        first_half = weight_grad(feed_all, tied, first_cut, 2, 1, 0)
        first_half, kv_parts = beside(first_half, kv_parts)
        g_kv = kv_sums[0] + kv_parts[0] + kv_parts[1] + kv_parts[2]
        first_half = first_half + jnp.concatenate(first_parts, axis=0)
        first_last = swap_x(after(first_half[2 * BLOCK :], g_kv))
        down_last = swap_y(after(half[2 * BLOCK :], q_send))
        g_o = o_keep + after(o_got, first_half)
        g_q = q_keep + after(q_got, first_half)
        first_last, down_last = after((first_last, down_last), g_o, g_q)
        second_got = jnp.concatenate(second_last, axis=0)
        g_gate_up = jnp.concatenate(
            [first_half[: 2 * BLOCK] + first_last, second_half[: 2 * BLOCK] + second_got], axis=1
        )
        g_down = half[: 2 * BLOCK] + down_last
    else:
        kv_send = kv_grads[0] + swap_core(kv_grads[1])
        g_o, g_q, g_kv = (fold_whole(v) for v in (o_send, q_send, kv_send))
    g_kv = line_scatter(g_kv, 0).astype(F32)
    grad_output = line_scatter(g_o, 0).astype(F32).T
    grad_query = line_scatter(g_q, 1).astype(F32)
    part_rows = g_down.shape[0] // 2
    g_ffn = jnp.concatenate([g_gate_up, g_down], axis=1)
    g_keep = g_ffn[:part_rows]
    g_take = swap_core(g_ffn[part_rows:])
    grads_ffn = []
    for start in (0, units, units_width):
        kept, got = g_keep[:, start : start + units], g_take[:, start : start + units]
        grads_ffn.append(
            jnp.where(
                core == 0,
                jnp.concatenate([kept, got], axis=1),
                jnp.concatenate([got, kept], axis=1),
            ).astype(F32)
        )
    grad_gate, grad_up, grad_down = grads_ffn
    grad_down = grad_down.T

    grad_key_value = (
        g_kv[:, :KV_WIDTH]
        .reshape(small, KEY_VALUE_HEADS, 2, HEAD_SIZE)
        .transpose(0, 2, 1, 3)
        .reshape(small, KV_WIDTH)
    )

    added = [
        lax.psum_scatter(after(v, last_kv), "heads", scatter_dimension=0, tiled=True) for v in added
    ]
    added = after(added, (g_kv, grad_output))
    layer_out = finish_layer(table, *hiddens, *added)

    return (
        from_order(layer_out).reshape(tokens.shape),
        from_order(tokens_grad).reshape(tokens.shape),
        g_kv[:, KV_WIDTH + ATTENTION_GAIN],
        grad_query,
        grad_key_value,
        g_kv[:per_head, KV_WIDTH + HEAD_GAIN],
        grad_output,
        g_kv[:, KV_WIDTH + FEED_GAIN],
        grad_gate,
        grad_up,
        grad_down,
    )


def order_kernel(table, values, out):
    for j in range(values.shape[1] // BLOCK):
        out[:, span(j)] = values[:, place(table, j)]


def order_columns(table, values):
    return kernel_call(
        order_kernel,
        "order_columns",
        (1,),
        [whole(values)],
        fixed_out(values.shape),
        shape(values.shape, values.dtype),
        [],
        0,
        table,
    )(values)


def solution(mesh):
    every = ("dp", "seq", "heads")
    token_spec = P(None, "dp", ("seq", "heads"), None)
    return jax.shard_map(
        on_device,
        mesh=mesh,
        in_specs=(
            token_spec,
            P(None, "dp", None),
            P(every),
            P(("dp", "seq"), "heads"),
            P(every, None),
            P(every),
            P(None, every),
            P(every),
            P(("dp", "seq"), "heads"),
            P(("dp", "seq"), "heads"),
            P("heads", ("dp", "seq")),
            token_spec,
        ),
        out_specs=(
            token_spec,
            token_spec,
            P(every),
            P(("dp", "seq"), "heads"),
            P(every, None),
            P(every),
            P(None, every),
            P(every),
            P(("dp", "seq"), "heads"),
            P(("dp", "seq"), "heads"),
            P("heads", ("dp", "seq")),
        ),
        check_vma=False,
    )
```

```python
import functools
import math

import jax
import jax.numpy as jnp
from jax import lax
from jax.experimental import pallas as pl
from jax.experimental.pallas import tpu as pltpu
from jax.sharding import PartitionSpec as P

QUERY_HEADS = 28
KEY_VALUE_HEADS = 7
HEAD_SIZE = 64
GROUP = QUERY_HEADS // KEY_VALUE_HEADS
GROUP_WIDTH = GROUP * HEAD_SIZE
Q_WIDTH = QUERY_HEADS * HEAD_SIZE
KV_WIDTH = 2 * KEY_VALUE_HEADS * HEAD_SIZE

EPSILON = 1e-06
SCORE_SCALE = 0.125
MASKED = -1e30
LANES = 128
CHUNK = 256
BLOCK = 256
FFN_ROWS = 256
ATTENTION_GAIN, FEED_GAIN, HEAD_GAIN = 0, 1, 2

BF = jnp.bfloat16
F32 = jnp.float32


def dot_nn(left, right):
    return lax.dot_general(left, right, (((1,), (0,)), ((), ())), preferred_element_type=F32)


def dot_nt(left, right):
    return lax.dot_general(left, right, (((1,), (1,)), ((), ())), preferred_element_type=F32)


def dot_tn(left, right):
    return lax.dot_general(left, right, (((0,), (0,)), ((), ())), preferred_element_type=F32)


def shape(dims, kind):
    return jax.ShapeDtypeStruct(dims, kind)


def whole(array):
    dims = array.shape
    return pl.BlockSpec(
        dims, lambda *unused: (0,) * len(dims), pipeline_mode=pl.Buffered(1)
    )


def fixed_out(dims):
    return pl.BlockSpec(dims, lambda *unused: (0,) * len(dims))


def kernel_call(body, name, grid, in_specs, out_specs, out_shape, scratch, flops, table=None):
    outs = out_shape if isinstance(out_shape, (list, tuple)) else [out_shape]
    moved = sum(math.prod(o.shape) * jnp.dtype(o.dtype).itemsize for o in outs)
    kwargs = dict(
        out_shape=out_shape,
        compiler_params=pltpu.CompilerParams(
            dimension_semantics=("arbitrary",) * len(grid), vmem_limit_bytes=56 * 1024 * 1024
        ),
        name=name,
    )

    def call(*operands):
        size = moved + sum(math.prod(o.shape) * o.dtype.itemsize for o in operands)
        cost = pl.CostEstimate(
            flops=flops,
            bytes_accessed=size,
            transcendentals=0,
        )
        if table is None:
            return pl.pallas_call(
                body,
                grid=grid,
                in_specs=in_specs,
                out_specs=out_specs,
                scratch_shapes=scratch,
                cost_estimate=cost,
                **kwargs,
            )(*operands)
        return pl.pallas_call(
            body,
            grid_spec=pltpu.PrefetchScalarGridSpec(
                num_scalar_prefetch=1,
                grid=grid,
                in_specs=in_specs,
                out_specs=out_specs,
                scratch_shapes=scratch,
            ),
            cost_estimate=cost,
            **kwargs,
        )(table, *operands)

    return call


def half_lanes(rows):
    return lax.broadcasted_iota(jnp.int32, (rows, LANES), 1) < HEAD_SIZE


def half_means(values, low):
    first = jnp.sum(jnp.where(low, values, 0.0), axis=1, keepdims=True) / HEAD_SIZE
    second = jnp.sum(jnp.where(low, 0.0, values), axis=1, keepdims=True) / HEAD_SIZE
    return jnp.where(low, first, second)


def turn(values):
    lane = lax.broadcasted_iota(jnp.int32, values.shape, 1)
    early = (lane & (HEAD_SIZE // 2)) == 0
    return jnp.where(
        early, pltpu.roll(values, LANES - HEAD_SIZE // 2, 1), pltpu.roll(values, HEAD_SIZE // 2, 1)
    )


def head_norm(tile, gain, cosine, sine, low):
    normed = tile * lax.rsqrt(half_means(tile * tile, low) + EPSILON) * gain
    return normed * cosine + turn(normed) * sine


def head_norm_back(tile, gain, cosine, sine, low, grad):
    grad = grad * cosine - turn(grad) * sine
    scale = lax.rsqrt(half_means(tile * tile, low) + EPSILON)
    lifted = grad * gain
    dots = half_means(tile * lifted, low)
    d_tile = scale * lifted - tile * (scale * scale * scale) * dots
    return d_tile, jnp.sum(grad * tile * scale, axis=0, keepdims=True)


def place(table, j):
    return pl.ds(pl.multiple_of(table[j] * BLOCK, BLOCK), BLOCK)


def span(j, size=BLOCK):
    return slice(j * size, (j + 1) * size)


def over_pieces(left, pieces, columns=None):
    total, start = None, 0
    for piece in pieces:
        size = piece.shape[0]
        right = piece[...] if columns is None else piece[:, columns]
        term = dot_nn(left[:, start : start + size], right)
        total = term if total is None else total + term
        start += size
    return total


def add_back(target, left, pieces, columns=None):
    start = 0
    for piece in pieces:
        size = piece.shape[0]
        right = piece[...] if columns is None else piece[:, columns]
        target[:, start : start + size] += dot_nt(left, right)
        start += size


def key_value_kernel(table, tokens, cosine, sine, gain, *refs):
    kvg = refs[:-4]
    normed, kv_raw, kv_low, gains = refs[-4:]
    rows, width = tokens.shape
    count = width // BLOCK
    columns = jnp.concatenate([part[:, KV_WIDTH:].astype(F32).T for part in kvg], axis=1)
    gains[...] = columns[:8]
    squares = 0.0
    for j in range(count):
        block = tokens[:, place(table, j)].astype(F32)
        squares = squares + jnp.sum(block * block, axis=1, keepdims=True)
    scale = lax.rsqrt(squares / width + EPSILON)
    for j in range(count):
        block = tokens[:, place(table, j)].astype(F32)
        normed[:, span(j)] = (
            block * scale * columns[ATTENTION_GAIN : ATTENTION_GAIN + 1, span(j)]
        ).astype(BF)
    raw = over_pieces(normed, kvg, slice(0, KV_WIDTH))
    kv_raw[...] = raw
    low = half_lanes(rows)
    for c in range(KEY_VALUE_HEADS):
        tile = raw[:, span(c, LANES)]
        key = head_norm(tile, gain[...], cosine[...], sine[...], low)
        kv_low[:, span(c, LANES)] = jnp.where(low, key, tile).astype(BF)


def project_key_value(table, tokens, cosine, sine, gain, kvg):
    rows, width = tokens.shape
    operands = (tokens, cosine, sine, gain, *kvg)
    return kernel_call(
        key_value_kernel,
        "project_key_value",
        (1,),
        [whole(o) for o in operands],
        [
            fixed_out((rows, width)),
            fixed_out((rows, KV_WIDTH)),
            fixed_out((rows, KV_WIDTH)),
            fixed_out((8, width)),
        ],
        [
            shape((rows, width), BF),
            shape((rows, KV_WIDTH), F32),
            shape((rows, KV_WIDTH), BF),
            shape((8, width), F32),
        ],
        [],
        2 * rows * width * KV_WIDTH,
        table,
    )(*operands)


def query_kernel(normed, cosine, sine, gain, *refs):
    q_raw, queries = refs[-2:]
    rows = normed.shape[0]
    raw = over_pieces(normed, refs[:-2])
    q_raw[...] = raw
    low = half_lanes(rows)
    for tile_index in range(GROUP_WIDTH // LANES):
        tile = raw[:, span(tile_index, LANES)]
        turned = head_norm(tile, gain[...], cosine[...], sine[...], low)
        queries[:, span(tile_index, LANES)] = (turned * SCORE_SCALE).astype(BF)


def column_parts(pieces):
    return [pl.BlockSpec((piece.shape[0], GROUP_WIDTH), lambda c, *t: (0, c)) for piece in pieces]


def project_query(normed, cosine, sine, gain, weight):
    rows, width = normed.shape
    out = pl.BlockSpec((rows, GROUP_WIDTH), lambda c: (0, c))
    return kernel_call(
        query_kernel,
        "project_query",
        (KEY_VALUE_HEADS,),
        [whole(normed), whole(cosine), whole(sine), whole(gain), *column_parts(weight)],
        [out, out],
        [shape((rows, Q_WIDTH), F32), shape((rows, Q_WIDTH), BF)],
        [],
        2 * rows * width * Q_WIDTH,
    )(normed, cosine, sine, gain, *weight)


def output_kernel(table, mixed, tokens, gains, *refs):
    hidden, feed = refs[-2:]
    width = hidden.shape[1]
    step = pl.program_id(0)

    @pl.when(step == 0)
    def _():
        for j in range(width // BLOCK):
            hidden[:, span(j)] = tokens[:, place(table, j)].astype(F32)

    add_back(hidden, mixed[...], refs[:-2])

    @pl.when(step == pl.num_programs(0) - 1)
    def _():
        values = hidden[...]
        scale = lax.rsqrt(jnp.mean(values * values, axis=1, keepdims=True) + EPSILON)
        feed[...] = (values * scale * gains[FEED_GAIN : FEED_GAIN + 1, :]).astype(BF)


def project_output(table, mixed, tokens, batch, gains, weight):
    rows = mixed.shape[0]
    width = tokens.shape[1]
    return kernel_call(
        output_kernel,
        "project_output",
        (KEY_VALUE_HEADS,),
        [
            pl.BlockSpec((rows, GROUP_WIDTH), lambda c, t: (0, c)),
            pl.BlockSpec((rows, width), lambda c, t: (batch, 0)),
            whole(gains),
            *column_parts(weight),
        ],
        [fixed_out((rows, width)), fixed_out((rows, width))],
        [shape((rows, width), F32), shape((rows, width), BF)],
        [],
        2 * rows * width * Q_WIDTH,
        table,
    )(mixed, tokens, gains, *weight)


def hidden_back_kernel(table, d_feed, hidden, cot, gains, *refs):
    d_hidden, d_attended, gain_grad, d_mixed = refs[-4:]
    width = hidden.shape[1]

    @pl.when(pl.program_id(0) == 0)
    def _():
        values = hidden[...]
        grad = d_feed[...].astype(F32)
        scale = lax.rsqrt(jnp.mean(values * values, axis=1, keepdims=True) + EPSILON)
        lifted = grad * gains[FEED_GAIN : FEED_GAIN + 1, :]
        dots = jnp.mean(values * lifted, axis=1, keepdims=True)
        d_norm = scale * lifted - values * (scale * scale * scale) * dots
        gain_grad[...] = jnp.broadcast_to(
            jnp.sum(grad * values * scale, axis=0, keepdims=True), gain_grad.shape
        )
        for j in range(width // BLOCK):
            total = cot[:, place(table, j)].astype(F32) + d_norm[:, span(j)]
            d_hidden[:, span(j)] = total
            d_attended[:, span(j)] = total.astype(BF)

    d_mixed[...] = over_pieces(d_attended, refs[:-4]).astype(BF)


def hidden_back(table, d_feed, hidden, cot, batch, gains, weight):
    rows, width = hidden.shape
    return kernel_call(
        hidden_back_kernel,
        "hidden_back",
        (KEY_VALUE_HEADS,),
        [
            whole(d_feed),
            whole(hidden),
            pl.BlockSpec((rows, width), lambda c, t: (batch, 0)),
            whole(gains),
            *column_parts(weight),
        ],
        [
            fixed_out((rows, width)),
            fixed_out((rows, width)),
            fixed_out((8, width)),
            pl.BlockSpec((rows, GROUP_WIDTH), lambda c, t: (0, c)),
        ],
        [
            shape((rows, width), F32),
            shape((rows, width), BF),
            shape((8, width), F32),
            shape((rows, Q_WIDTH), BF),
        ],
        [],
        2 * rows * width * Q_WIDTH,
        table,
    )(d_feed, hidden, cot, gains, *weight)


def query_back_kernel(d_q, *refs):
    out = refs[-1]

    @pl.when(pl.program_id(0) == 0)
    def _():
        out[...] = jnp.zeros_like(out)

    add_back(out, d_q[...], refs[:-1])


def query_back(d_q, weight):
    rows = d_q.shape[0]
    width = sum(piece.shape[0] for piece in weight)
    return kernel_call(
        query_back_kernel,
        "query_back",
        (KEY_VALUE_HEADS,),
        [pl.BlockSpec((rows, GROUP_WIDTH), lambda c: (0, c)), *column_parts(weight)],
        fixed_out((rows, width)),
        shape((rows, width), F32),
        [],
        2 * rows * width * Q_WIDTH,
    )(d_q, *weight)


def input_back_kernel(
    table,
    d_pair,
    kv_raw,
    cosine,
    sine,
    gain,
    d_normed_q,
    d_hidden0,
    d_hidden1,
    tokens,
    gains,
    *refs,
):
    kvg = refs[:-5]
    d_kv_raw, head_grad, tokens_grad, gain_grad, d_normed = refs[-5:]
    rows, width = tokens.shape
    part = d_hidden0.shape[0]
    low = half_lanes(rows)
    total = 0.0
    for c in range(KEY_VALUE_HEADS):
        grad = d_pair[:, span(c, LANES)].astype(F32)
        d_tile, g_tile = head_norm_back(
            kv_raw[:, span(c, LANES)], gain[...], cosine[...], sine[...], low, grad
        )
        total = total + g_tile
        d_kv_raw[:, span(c, LANES)] = jnp.where(low, d_tile, grad).astype(BF)
    head_grad[...] = jnp.broadcast_to(total, head_grad.shape)
    d_kv = d_kv_raw[...]
    d_normed[...] = d_normed_q[...]
    add_back(d_normed, d_kv, kvg, slice(0, KV_WIDTH))
    squares, dots = 0.0, 0.0
    for j in range(width // BLOCK):
        block = tokens[:, place(table, j)].astype(F32)
        lifted = d_normed[:, span(j)] * gains[ATTENTION_GAIN : ATTENTION_GAIN + 1, span(j)]
        squares = squares + jnp.sum(block * block, axis=1, keepdims=True)
        dots = dots + jnp.sum(block * lifted, axis=1, keepdims=True)
    scale = lax.rsqrt(squares / width + EPSILON)
    dots = dots / width * (scale * scale * scale)
    for j in range(width // BLOCK):
        block = tokens[:, place(table, j)].astype(F32)
        grad = d_normed[:, span(j)]
        lifted = grad * gains[ATTENTION_GAIN : ATTENTION_GAIN + 1, span(j)]
        d_input = scale * lifted - block * dots
        for batch, d_hidden in enumerate((d_hidden0, d_hidden1)):
            tokens_grad[span(batch, part), place(table, j)] = (
                d_hidden[:, span(j)] + d_input[span(batch, part), :]
            )
        gain_grad[:, span(j)] = jnp.broadcast_to(
            jnp.sum(grad * block * scale, axis=0, keepdims=True), (8, BLOCK)
        )


def input_back(table, *operands):
    tokens = operands[8]
    rows, width = tokens.shape
    return kernel_call(
        input_back_kernel,
        "input_back",
        (1,),
        [whole(o) for o in operands],
        [
            fixed_out((rows, KV_WIDTH)),
            fixed_out((8, LANES)),
            fixed_out((rows, width)),
            fixed_out((8, width)),
        ],
        [
            shape((rows, KV_WIDTH), BF),
            shape((8, LANES), F32),
            shape((rows, width), F32),
            shape((8, width), F32),
        ],
        [pltpu.VMEM((rows, width), F32)],
        2 * rows * width * KV_WIDTH,
        table,
    )(*operands)


def layer_out_kernel(table, hidden0, hidden1, added0, added1, out):
    part = hidden0.shape[0]
    for batch, (hidden, added) in enumerate(((hidden0, added0), (hidden1, added1))):
        for j in range(hidden.shape[1] // BLOCK):
            out[span(batch, part), place(table, j)] = (
                hidden[:, span(j)] + added[:, span(j)].astype(F32)
            ).astype(BF)


def finish_layer(table, *operands):
    rows, width = operands[0].shape
    return kernel_call(
        layer_out_kernel,
        "finish_layer",
        (1,),
        [whole(o) for o in operands],
        fixed_out((2 * rows, width)),
        shape((2 * rows, width), BF),
        [],
        0,
        table,
    )(*operands)


def key_value_grad_kernel(normed, d_kv_raw, gain_grads, out0, out1):
    half = normed.shape[1] // 2
    for index, out in enumerate((out0, out1)):
        cut = span(index, half)
        out[:, :KV_WIDTH] = dot_tn(normed[:, cut], d_kv_raw[...]).astype(BF)
        rows = gain_grads[:, cut]
        rows = jnp.concatenate([rows, jnp.zeros((LANES - 8, half), F32)], axis=0)
        out[:, KV_WIDTH:] = rows.T.astype(BF)


def key_value_grad(normed, d_kv_raw, gain_grads):
    rows, width = normed.shape
    dims = (width // 2, KV_WIDTH + LANES)
    return kernel_call(
        key_value_grad_kernel,
        "key_value_grad",
        (1,),
        [whole(normed), whole(d_kv_raw), whole(gain_grads)],
        [fixed_out(dims), fixed_out(dims)],
        [shape(dims, BF), shape(dims, BF)],
        [],
        2 * rows * width * KV_WIDTH,
    )(normed, d_kv_raw, gain_grads)


def pad_heads(tile, low, keep_low):
    parts = []
    for pair in range(GROUP // 2):
        both = tile[:, span(pair, LANES)].astype(F32)
        turned = pltpu.roll(both, HEAD_SIZE, 1)
        first, second = (both, turned) if keep_low else (turned, both)
        keep = low if keep_low else jnp.logical_not(low)
        parts.append(jnp.where(keep, first, 0.0))
        parts.append(jnp.where(keep, second, 0.0))
    return jnp.concatenate(parts, axis=0).astype(BF)


def four_wide(row):
    return jnp.concatenate([row] * GROUP, axis=1)


def heads_back(stacked, rows):
    parts = []
    for pair in range(GROUP // 2):
        start = 2 * pair * rows
        both = jnp.concatenate(
            [stacked[:, start : start + rows], stacked[:, start + rows : start + 2 * rows]], axis=0
        )
        parts.append(both.T)
    return jnp.concatenate(parts, axis=1)


def key_rows(kv, cut):
    rows = kv.shape[2]
    block = kv[cut.start // rows : cut.stop // rows, 0]
    return block.reshape(cut.stop - cut.start, kv.shape[3])


def every_row(kv):
    return key_rows(kv, slice(0, kv.shape[0] * kv.shape[2]))


def ones_and_values(kv):
    values = every_row(kv)
    return jnp.where(half_lanes(values.shape[0]), 1.0, values.astype(F32)).astype(BF)


def attention_forward_kernel(kv0, kv1, query, bias0, bias1, mixed, lse, expo):
    rows = query.shape[0]
    half = bias0.shape[0]
    padded = pad_heads(query[...], half_lanes(rows), True)
    for part, (kv, bias) in enumerate(((kv0, bias0), (kv1, bias1))):
        for step in range(half // CHUNK):
            cut = span(step, CHUNK)
            weight = jnp.exp(dot_nt(key_rows(kv, cut), padded) + four_wide(bias[cut, :]))
            expo[part * half + step * CHUNK : part * half + (step + 1) * CHUNK, :] = weight.astype(BF)
    total = dot_tn(ones_and_values(kv0), expo[:half, :]) + dot_tn(
        ones_and_values(kv1), expo[half:, :]
    )
    lse[...] = jnp.log(total[0:1, :])[None]
    mixed[...] = heads_back(total[HEAD_SIZE:, :] / total[:HEAD_SIZE, :], rows).astype(BF)


def attention_forward(kv0, kv1, query, batch, bias0, bias1):
    half, rows = bias0.shape
    wide = GROUP * rows
    keys = pl.BlockSpec((half // rows, 1, rows, LANES), lambda c: (0, 0, 0, c))
    kv0, kv1 = (kv.reshape(half // rows, -1, rows, KV_WIDTH) for kv in (kv0, kv1))
    return kernel_call(
        attention_forward_kernel,
        "attention_forward",
        (KEY_VALUE_HEADS,),
        [
            keys,
            keys,
            pl.BlockSpec((rows, GROUP_WIDTH), lambda c: (batch, c)),
            whole(bias0),
            whole(bias1),
        ],
        [
            pl.BlockSpec((rows, GROUP_WIDTH), lambda c: (0, c)),
            pl.BlockSpec((1, 1, wide), lambda c: (c, 0, 0)),
        ],
        [shape((rows, Q_WIDTH), BF), shape((KEY_VALUE_HEADS, 1, wide), F32)],
        [pltpu.VMEM((2 * half, wide), BF)],
        KEY_VALUE_HEADS * 2 * half * wide * LANES * 12,
    )(kv0, kv1, query, bias0, bias1)


def attention_backward_kernel(
    kv0,
    kv1,
    query,
    mixed,
    d_mixed,
    bias0,
    bias1,
    lse,
    q_raw,
    cosine,
    sine,
    gain,
    d_q_raw,
    d_kv0,
    d_kv1,
    gain_grad,
    d_scores,
):
    rows = query.shape[0]
    half = bias0.shape[0]
    low = half_lanes(rows)
    padded = pad_heads(query[...], low, True)
    d_padded = pad_heads(d_mixed[...], low, False)
    product = d_mixed[...].astype(F32) * mixed[...].astype(F32)
    pick = (
        lax.broadcasted_iota(jnp.int32, (8, GROUP_WIDTH), 1) // HEAD_SIZE
        == lax.broadcasted_iota(jnp.int32, (8, GROUP_WIDTH), 0)
    ).astype(F32)
    balance = lax.dot_general(
        pick,
        product,
        (((1,), (1,)), ((), ())),
        precision=lax.Precision.HIGHEST,
        preferred_element_type=F32,
    )
    balance = jnp.concatenate([balance[head : head + 1, :] for head in range(GROUP)], axis=1)
    level = lse[0]
    for part, (kv, bias, d_kv) in enumerate(((kv0, bias0, d_kv0), (kv1, bias1, d_kv1))):
        for step in range(half // CHUNK):
            cut = span(step, CHUNK)
            block = key_rows(kv, cut)
            probs = jnp.exp(dot_nt(block, padded) + four_wide(bias[cut, :]) - level)
            d_probs = dot_nt(block, d_padded)
            low_scores = (probs * (d_probs - balance)).astype(BF)
            d_scores[part * half + step * CHUNK : part * half + (step + 1) * CHUNK, :] = low_scores
            d_kv[cut, :] = (
                dot_nn(low_scores, padded) + dot_nn(probs.astype(BF), d_padded)
            ).astype(BF)
    total = dot_tn(every_row(kv0), d_scores[:half, :]) + dot_tn(
        every_row(kv1), d_scores[half:, :]
    )
    d_query = heads_back(total[:HEAD_SIZE, :] * SCORE_SCALE, rows)
    grads = 0.0
    for tile_index in range(GROUP_WIDTH // LANES):
        cut = span(tile_index, LANES)
        d_tile, g_tile = head_norm_back(
            q_raw[:, cut], gain[...], cosine[...], sine[...], low, d_query[:, cut]
        )
        d_q_raw[:, cut] = d_tile.astype(BF)
        grads = grads + g_tile

    @pl.when(pl.program_id(0) == 0)
    def _():
        gain_grad[...] = jnp.zeros_like(gain_grad)

    gain_grad[...] += jnp.broadcast_to(grads, gain_grad.shape)


def attention_backward(
    kv0, kv1, query, batch, mixed, d_mixed, bias0, bias1, lse, q_raw, cosine, sine, gain
):
    half, rows = bias0.shape
    wide = GROUP * rows
    keys = pl.BlockSpec((half // rows, 1, rows, LANES), lambda c: (0, 0, 0, c))
    kv0, kv1 = (kv.reshape(half // rows, -1, rows, KV_WIDTH) for kv in (kv0, kv1))
    d_keys = pl.BlockSpec((half, LANES), lambda c: (0, c))
    heads = pl.BlockSpec((rows, GROUP_WIDTH), lambda c: (0, c))
    part = pl.BlockSpec((rows, GROUP_WIDTH), lambda c: (batch, c))
    table = pl.BlockSpec((rows, LANES), lambda c: (batch, 0))
    return kernel_call(
        attention_backward_kernel,
        "attention_backward",
        (KEY_VALUE_HEADS,),
        [
            keys,
            keys,
            part,
            heads,
            heads,
            whole(bias0),
            whole(bias1),
            pl.BlockSpec((1, 1, wide), lambda c: (c, 0, 0)),
            part,
            table,
            table,
            whole(gain),
        ],
        [heads, d_keys, d_keys, fixed_out((8, LANES))],
        [
            shape((rows, Q_WIDTH), BF),
            shape((half, KV_WIDTH), BF),
            shape((half, KV_WIDTH), BF),
            shape((8, LANES), F32),
        ],
        [pltpu.VMEM((2 * half, wide), BF)],
        KEY_VALUE_HEADS * 2 * half * wide * LANES * 28,
    )(kv0, kv1, query, mixed, d_mixed, bias0, bias1, lse, q_raw, cosine, sine, gain)


def swap_halves(values):
    half = values.shape[1] // 2
    return jnp.concatenate([values[:, half:], values[:, :half]], axis=1)


def feed_forward_kernel(count, units, *refs):
    feed0, feed1, cot0, cot1 = refs[:4]
    gate_up = refs[4 : 4 + count]
    down = refs[4 + count : 4 + 2 * count]
    act_out, d_units_out, out0, out1, d_feed0, d_feed1 = refs[4 + 2 * count :]
    first = pl.program_id(0) < pl.num_programs(0) // 2
    rows, width = feed0.shape
    half = width // 2
    size = down[0].shape[0] // 2
    feed = jnp.where(first, swap_halves(feed0[...]), feed1[...])
    cot = jnp.where(first, swap_halves(cot0[...]), cot1[...])

    def over(left, pieces):
        total = None
        for b, piece in enumerate(pieces):
            both = jnp.concatenate(
                [left[:, b * size : (b + 1) * size], left[:, half + b * size : half + (b + 1) * size]],
                axis=1,
            )
            term = dot_nn(both, piece[...])
            total = term if total is None else total + term
        return total

    both = over(feed, gate_up)
    gate_pre, up_pre = both[:, :units], both[:, units : 2 * units]
    sig = 1.0 / (1.0 + jnp.exp(-gate_pre))
    silu = gate_pre * sig
    act = (silu * up_pre).astype(BF)
    act = jnp.concatenate([act, jnp.zeros((rows, down[0].shape[1] - units), BF)], axis=1)
    act_out[...] = act
    d_act = over(cot, down)[:, :units]
    d_gate = d_act * up_pre * (sig * (1.0 + gate_pre * (1.0 - sig)))
    d_units = jnp.concatenate(
        [
            d_gate.astype(BF),
            (d_act * silu).astype(BF),
            jnp.zeros((rows, gate_up[0].shape[1] - 2 * units), BF),
        ],
        axis=1,
    )
    d_units_out[...] = d_units

    def write(target, left, pieces, swapped):
        for b, piece in enumerate(pieces):
            block = dot_nt(left, piece[...]).astype(BF)
            early, late = (half, 0) if swapped else (0, half)
            target[:, early + b * size : early + (b + 1) * size] = block[:, :size]
            target[:, late + b * size : late + (b + 1) * size] = block[:, size:]

    @pl.when(first)
    def _():
        write(d_feed0, d_units, gate_up, True)
        write(out0, act, down, True)

    @pl.when(jnp.logical_not(first))
    def _():
        write(d_feed1, d_units, gate_up, False)
        write(out1, act, down, False)


def feed_forward(feeds, cots, gate_up, down, units):
    tokens, width = feeds[0].shape
    steps = tokens // FFN_ROWS
    early = pl.BlockSpec((FFN_ROWS, width), lambda i: (jnp.minimum(i, steps - 1), 0))
    late = pl.BlockSpec((FFN_ROWS, width), lambda i: (jnp.maximum(i - steps, 0), 0))
    act_width, units_width = down[0].shape[1], gate_up[0].shape[1]
    return kernel_call(
        functools.partial(feed_forward_kernel, len(down), units),
        "feed_forward",
        (2 * steps,),
        [early, late, early, late, *[whole(w) for w in (*gate_up, *down)]],
        [
            pl.BlockSpec((FFN_ROWS, act_width), lambda i: (i, 0)),
            pl.BlockSpec((FFN_ROWS, units_width), lambda i: (i, 0)),
            early,
            late,
            early,
            late,
        ],
        [
            shape((2 * tokens, act_width), BF),
            shape((2 * tokens, units_width), BF),
            *[shape((tokens, width), BF)] * 4,
        ],
        [],
        2 * tokens * 2 * width * units * 6,
    )(*feeds, *cots, *gate_up, *down)


def weight_grad_kernel(count, columns, *refs):
    lefts = refs[: 2 * count]
    rights = refs[2 * count : -1]
    out = refs[-1]
    rows = lefts[0].shape[0]
    each = count // len(rights)
    total = None
    for index in range(count):
        left = jnp.concatenate([lefts[2 * index][...], lefts[2 * index + 1][...]], axis=1)
        right = rights[index // each]
        term = dot_tn(left, right[span(index % each, rows), columns])
        total = term if total is None else total + term
    out[...] = total.astype(BF)


def weight_grad(lefts, rights, columns, steps, stride, offset):
    rows, width = lefts[0].shape
    units = columns.stop - columns.start
    half = width // 2 // BLOCK
    mine = pl.BlockSpec((rows, BLOCK), lambda i: (0, i * stride + offset))
    other = pl.BlockSpec((rows, BLOCK), lambda i: (0, half + i * stride + offset))
    specs, operands = [], []
    for index, left in enumerate(lefts):
        specs += [other, mine] if index % 2 == 0 else [mine, other]
        operands += [left, left]
    return kernel_call(
        functools.partial(weight_grad_kernel, len(lefts), columns),
        "weight_grad",
        (steps,),
        [*specs, *[whole(r) for r in rights]],
        pl.BlockSpec((2 * BLOCK, units), lambda i: (i, 0)),
        shape((2 * BLOCK * steps, units), BF),
        [],
        2 * len(lefts) * rows * 2 * BLOCK * steps * units,
    )(*operands, *rights)


def rotary_tables(places):
    half_width = HEAD_SIZE // 2
    freqs = jnp.exp(jnp.arange(half_width, dtype=F32) * (-2.0 * math.log(10000.0) / HEAD_SIZE))
    angles = places.astype(F32)[:, None] * freqs[None, :]
    cosine, sine = jnp.cos(angles), jnp.sin(angles)
    return (
        jnp.concatenate([cosine] * 4, axis=1),
        jnp.concatenate([-sine, sine, -sine, sine], axis=1),
    )


def padded_columns(values, columns):
    return jnp.pad(values, ((0, 0), (0, columns - values.shape[1])))


def up_to(size):
    return -(-size // LANES) * LANES


def on_device(
    tokens,
    lengths,
    attention_gain,
    query_weight,
    key_value_matrix,
    per_head_gains,
    output_weight,
    feed_gain,
    gate_weight,
    up_weight,
    down_weight,
    cotangent,
):
    batches = tokens.shape[0]
    rows = tokens.shape[2]
    width = tokens.shape[3]
    dp_size = lax.axis_size("dp")
    heads_size = lax.axis_size("heads")
    seq_size = lax.axis_size("seq")
    assert seq_size == 4 and heads_size == 4 and batches == 2
    paired = dp_size == 2
    y = lax.axis_index("dp").astype(jnp.int32)
    s = lax.axis_index("seq").astype(jnp.int32)
    z = lax.axis_index("heads").astype(jnp.int32)
    x = s // 2
    core = s % 2

    def after(v, *others):
        return lax.optimization_barrier((v, others))[0]

    def beside(outs, parts):
        return lax.optimization_barrier((outs, parts))

    def swap_x(v):
        return lax.ppermute(v, "seq", [(i, i ^ 2) for i in range(4)])

    def swap_xy(v):
        return lax.ppermute(v, ("dp", "seq"), [(i, i ^ 6) for i in range(8)])

    def swap_core(v):
        return lax.ppermute(v, "seq", [(i, i ^ 1) for i in range(4)])

    def swap_y(v):
        return lax.ppermute(v, "dp", [(0, 1), (1, 0)])

    def line_scatter(v, axis):
        cut = jnp.split(v, 4, axis=axis)
        total = lax.select_n(z, *cut)
        for k in range(1, 4):
            block = lax.select_n(z, *[cut[i ^ k] for i in range(4)])
            total = total + lax.ppermute(block, "heads", [(i, i ^ k) for i in range(4)])
        return total

    def gather_near(v):
        if not paired:
            both = jnp.stack([v, swap_x(v)], axis=0)
            return [lax.all_gather(both, "dp", axis=0).reshape(-1, v.shape[-1])]
        return [v, swap_x(v), swap_y(v)]

    def gather_far(near, x_first):
        if not paired:
            return near
        return [*near, swap_y(near[1]) if x_first else swap_x(near[2])]

    def pair_gather(v, axis):
        def step(u, upper, distance):
            got = lax.ppermute(u, "heads", [(i, i ^ distance) for i in range(4)])
            return jnp.where(
                upper,
                jnp.concatenate([got, u], axis=axis),
                jnp.concatenate([u, got], axis=axis),
            )

        return step(step(v, z % 2 == 1, 1), z >= 2, 2)

    def both_cores(pieces):
        return [*pieces, *[swap_core(v) for v in pieces]]

    def unit_pieces(pieces):
        if paired:
            return pieces
        g = pieces[0].reshape(blocks, 2, -1, pieces[0].shape[-1])
        return [g.transpose(1, 0, 2, 3).reshape(pieces[0].shape)]

    def scatter_yx(g, x_last, first=(), second=()):
        def along_x(u, late):
            return u[..., 0, :, :] + after(swap_x(u[..., 1, :, :]), late)

        def along_y(u, late):
            if paired:
                return u[0] + after(swap_y(u[1]), late)
            return lax.psum_scatter(u, "dp", scatter_dimension=0)

        if x_last:
            return along_x(along_y(g, first), second)
        return along_y(along_x(g, first), second)

    blocks = 2 * dp_size
    piece = width // blocks

    if paired:
        own = (2 * y + x) * 2 + core
        places_of = jnp.array([b * 2 + c for c in range(2) for b in range(4)], jnp.int32)
        table = places_of ^ own

        def to_order(v):
            return v

        from_order = to_order
    else:
        table = jnp.arange(width // BLOCK, dtype=jnp.int32)

        def flip(v):
            u = v.reshape(v.shape[:-1] + (dp_size, 2, 2, piece // 2))
            u = jnp.where(x == 1, u[..., ::-1, :, :], u)
            return jnp.where(core == 1, u[..., ::-1, :], u)

        def to_order(v):
            return jnp.moveaxis(flip(v), -2, -4).reshape(v.shape)

        def from_order(v):
            u = v.reshape(v.shape[:-1] + (2, dp_size, 2, piece // 2))
            return flip(jnp.moveaxis(u, -4, -2).reshape(v.shape)).reshape(v.shape)

    def small_order(v, back):
        if not paired:
            return from_order(v) if back else to_order(v)
        cut = v.reshape(8, -1)
        return jnp.concatenate(
            [
                lax.select_n(own, *[cut[held(i, m, back)] for m in range(8)])
                for i in range(8)
            ]
        ).reshape(v.shape)

    def held(i, m, back):
        if back:
            source = i ^ m
            return (source % 2) * 4 + source // 2
        return ((i % 4) * 2 + i // 4) ^ m

    small = key_value_matrix.shape[0]
    per_head = per_head_gains.shape[0]
    kv_local = (
        key_value_matrix.reshape(small, 2, KEY_VALUE_HEADS, HEAD_SIZE)
        .transpose(0, 2, 1, 3)
        .reshape(small, KV_WIDTH)
    )
    gains_local = jnp.stack(
        [attention_gain, feed_gain, jnp.pad(per_head_gains, (0, small - per_head))], axis=1
    )
    kvg_local = jnp.concatenate([kv_local, padded_columns(gains_local, LANES)], axis=1)
    kvg_rows = pair_gather(kvg_local, 0)
    kvg_near = gather_near(kvg_rows)

    tokens_in = to_order(tokens[:, 0].reshape(batches * rows, width))
    cot_in = to_order(cotangent[:, 0].reshape(batches * rows, width))
    cot_held = order_columns(table, cot_in) if paired else cot_in
    projections = lax.all_gather(
        jnp.concatenate([query_weight.reshape(small, Q_WIDTH), output_weight.T], axis=0),
        "heads",
        axis=0,
    )
    q_rows = (
        projections[:, :small]
        .reshape(heads_size, query_weight.shape[0], query_weight.shape[1])
        .transpose(1, 0, 2)
        .reshape(query_weight.shape[0], Q_WIDTH)
    )
    o_rows = projections[:, small:].reshape(4 * small, Q_WIDTH)
    lined = lax.all_gather(cot_held, "heads", axis=0)
    cots_mine = [
        lined[:, span(batch, rows)].reshape(heads_size * rows, width) for batch in range(batches)
    ]

    units = gate_weight.shape[1] // 2
    act_width, units_width = up_to(units), up_to(2 * units)

    def unit_half(v, which):
        return jnp.where(which == 0, v[:, :units], v[:, units:])

    down_local = down_weight.T

    def halves(which):
        gate_up = jnp.concatenate([unit_half(gate_weight, which), unit_half(up_weight, which)], axis=1)
        return jnp.concatenate(
            [padded_columns(gate_up, units_width), padded_columns(unit_half(down_local, which), act_width)],
            axis=1,
        )

    keep = halves(core)
    take = swap_core(halves(1 - core))
    ffn_rows = jnp.concatenate([keep, take], axis=0)
    down_near = gather_near(ffn_rows[:, units_width:])
    gate_up_near = gather_near(after(ffn_rows[:, :units_width], kvg_near))
    gate_up = unit_pieces(gather_far(gate_up_near, True))
    kvg = both_cores(gather_far(after(kvg_near, down_near), True))

    head_column = jnp.concatenate([part[:, KV_WIDTH + HEAD_GAIN] for part in kvg])
    head_scale = small_order(head_column.astype(F32)[None], True)
    head_scale = head_scale.reshape(-1, small)[:, :per_head].reshape(1, -1)
    query_gain = jnp.concatenate([head_scale[:, :HEAD_SIZE]] * 2, axis=1)
    key_gain = jnp.concatenate([head_scale[:, HEAD_SIZE:]] * 2, axis=1)

    block_rows = rows * heads_size
    spots = s * block_rows + z * rows + jnp.arange(rows, dtype=jnp.int32)
    inside = jnp.arange(rows, dtype=jnp.int32)

    def key_spots(first):
        lines = jnp.arange(heads_size, dtype=jnp.int32)[:, None, None] * rows
        fronts = jnp.stack([first, first ^ 2])[None, :, None] * block_rows
        return (lines + fronts + inside[None, None, :]).reshape(-1)

    def bias_for(begin, first):
        keys = key_spots(first)[:, None]
        return jnp.where((keys <= spots[None, :]) & (keys >= begin[None, :]), 0.0, MASKED)

    begins, biases = [], []
    for batch in range(batches):
        sizes = lengths[batch, 0]
        finish = jnp.cumsum(sizes)
        begin = jnp.sum(
            jnp.where(spots[:, None] >= finish[None, :], sizes[None, :], 0), axis=1
        ).astype(jnp.int32)
        begins.append(begin)
        biases.append((bias_for(begin, s), bias_for(begin, s ^ 1)))
    cosine, sine = rotary_tables(jnp.concatenate([spots - begin for begin in begins]))

    normed, kv_raw, kv_low, gains = project_key_value(
        table, after(tokens_in, down_near), cosine, sine, key_gain, kvg
    )
    kv_got = swap_x(kv_low)
    kv_lined = []
    for batch in range(batches):
        cut = span(batch, rows)
        pair = jnp.concatenate([kv_low[cut], kv_got[cut]], axis=0)
        if batch == 0:
            pair = after(pair, gate_up_near, lined)
        kv_lined.append(lax.all_gather(pair, "heads", axis=0, tiled=True))
    down = unit_pieces(gather_far(down_near, False))
    q_near = gather_near(q_rows)
    q_full = both_cores(gather_far(after(q_near, kv_got), False))
    o_near = gather_near(after(o_rows, q_near))
    q_raw, queries = project_query(after(normed, kv_lined[0]), cosine, sine, query_gain, q_full)
    o_pieces = gather_far(after(o_near, queries), True)
    kv_lined[0] = after(kv_lined[0], queries, o_near)
    kvs = [(v, swap_core(v)) for v in kv_lined]

    feeds, mixeds, lses, hiddens = [], [], [], []
    for batch in range(batches):
        query = queries if batch == 0 else after(queries, hiddens[0])
        mixed, lse = attention_forward(*kvs[batch], query, batch, *biases[batch])
        if batch == 0:
            o_full = both_cores(after(o_pieces, mixed))
        else:
            (mixed, lse), (gate_up, down) = beside((mixed, lse), (gate_up, down))
        hidden_in, feed_rows = project_output(
            table, mixed, tokens_in, batch, gains, o_full
        )
        feeds.append(lax.all_gather(feed_rows, "heads", axis=0, tiled=True))
        mixeds.append(mixed)
        lses.append(lse)
        hiddens.append(hidden_in)

    feeds[0] = after(feeds[0], feed_rows)
    feeds = [(swap_core(v), v) for v in feeds]

    d_feeds, acts, d_units, cots = [], [], [], []
    added = []
    for batch in range(batches):
        if batch == 1:
            feeds[1] = after(feeds[1], added[0])
        cot_pair = (swap_core(cots_mine[batch]), cots_mine[batch])
        act, d_unit, out_other, out_mine, d_feed_other, d_feed_mine = feed_forward(
            feeds[batch], cot_pair, gate_up, down, units
        )
        acts.append(act)
        d_units.append(d_unit)
        cots.append(cot_pair)
        added.append(out_mine + swap_core(out_other))
        d_feed = d_feed_mine + swap_core(d_feed_other)
        if batch + 1 < batches:
            d_feed = after(d_feed, feeds[batch + 1])
        d_feeds.append(lax.psum_scatter(d_feed, "heads", scatter_dimension=0, tiled=True))

    feed_all = [f for pair in feeds for f in pair]
    cot_all = [c for pair in cots for c in pair]
    count = width // 2 // BLOCK

    def unit_order(g):
        g = g.reshape(count, 2, BLOCK, -1).transpose(1, 0, 2, 3)
        g = g.reshape(2, blocks, piece // 2, -1).transpose(1, 0, 2, 3)
        return g.reshape(dp_size, 2, piece, -1)

    cut_at = up_to(units)

    def both_grads(left, right):
        return [dot_tn(left[:, span(i, width // 2)], right).astype(BF) for i in range(2)]

    def split_rows(mine, got, along_y=True):
        if not paired:
            return mine + got, None
        size = mine.shape[0] // 4
        far = (2, 3) if along_y else (1, 3)
        near = (0, 1) if along_y else (0, 2)

        def pick(v, blocks_of):
            return jnp.concatenate([v[span(b, size)] for b in blocks_of], axis=0)

        return pick(mine, far) + pick(got, far), pick(mine, near) + pick(got, near)

    def send_parts(v, swap, *rows_of):
        parts, start = [], 0
        for size in rows_of:
            parts.append(swap(v[start : start + size]))
            start += size
        assert start == v.shape[0]
        return parts

    def halved(total):
        near = total.shape[0] // 2
        return total[near:], total[:near]

    def fold(parts, kept, *late):
        return halved(kept + after(jnp.concatenate(parts, axis=0), late))

    def fold_whole(sent):
        g = sent.reshape(dp_size, 2, -1, sent.shape[-1])
        g = lax.psum_scatter(g, "dp", scatter_dimension=0)
        return g[0] + swap_x(g[1])

    d_hiddens, d_attendeds, d_q_raws, d_lined = [], [], [], []
    feed_gain_grads, query_gain_grads = [], []
    mixed_all = jnp.concatenate(mixeds, axis=0)
    first_cut, second_cut = slice(0, cut_at), slice(cut_at, up_to(2 * units))
    if paired:
        first_far = weight_grad(feed_all, d_units, first_cut, 2, 1, 2)
        first_parts = send_parts(first_far, swap_y, 384, 640)
        second_far = weight_grad(feed_all, after(d_units, first_far), second_cut, 2, 2, 1)
        second_parts = send_parts(second_far, swap_x, 384, 640)
        d_feeds[0] = after(d_feeds[0], second_far)
    for batch in range(batches):
        d_feed = d_feeds[batch]
        if batch == 1:
            d_feed = after(d_feed, d_q_raws[0])
            if paired:
                tied = after(acts, d_q_raws[0])
                down_far = weight_grad(cot_all, tied, slice(0, act_width), 2, 2, 1)
                down_parts = send_parts(down_far, swap_x, 256, 640, 128)
                d_feed = after(d_feed, down_far, last_kv)
        back = hidden_back(table, d_feed, hiddens[batch], cot_in, batch, gains, o_full)
        if paired and batch == 0:
            back, (first_parts[0], second_parts[0]) = beside(
                back, (first_parts[0], second_parts[0])
            )
        if paired and batch == 1:
            back, down_parts[0] = beside(back, down_parts[0])
        d_hidden, d_attended, feed_grad, d_mixed = back
        d_hiddens.append(d_hidden)
        d_attendeds.append(d_attended)
        if batch == 1:
            o_grads = both_grads(jnp.concatenate(d_attendeds, axis=0), mixed_all)
            o_send, o_keep = split_rows(o_grads[0], swap_core(o_grads[1]))
            d_mixed = after(d_mixed, o_send)
            if paired:
                o_parts = send_parts(o_send, swap_y, 256, 128, 128)
        back = attention_backward(
            *kvs[batch],
            queries,
            batch,
            mixeds[batch],
            d_mixed,
            *biases[batch],
            lses[batch],
            q_raw,
            cosine,
            sine,
            query_gain,
        )
        if paired and batch == 0:
            back, (first_parts[1], second_parts[1]) = beside(
                back, (first_parts[1], second_parts[1])
            )
        if paired and batch == 1:
            back, (down_parts[1], o_parts[0]) = beside(back, (down_parts[1], o_parts[0]))
        d_q_raw, d_kv0, d_kv1, query_grad = back
        d_kv = d_kv0 + swap_core(d_kv1)
        last_kv = d_kv
        d_lined.append(lax.psum_scatter(d_kv, "heads", scatter_dimension=0, tiled=True))
        d_q_raws.append(d_q_raw)
        feed_gain_grads.append(feed_grad)
        query_gain_grads.append(query_grad)

    pairs_got = [swap_x(d_lined[0][rows:])]
    d_q_raw_all = jnp.concatenate(d_q_raws, axis=0)
    q_grads = both_grads(after(normed, last_kv), d_q_raw_all)
    if paired:
        q_grads, (down_parts[2], o_parts[1], pairs_got) = beside(
            q_grads, (down_parts[2], o_parts[1], pairs_got)
        )
    q_send, q_keep = split_rows(q_grads[0], swap_core(q_grads[1]), False)
    d_normed_q = query_back(after(d_q_raw_all, q_send), q_full)
    if paired:
        q_parts = send_parts(q_send[: 2 * LANES], swap_x, 128, 128)
        d_normed_q, (q_parts[0], o_parts[2]) = beside(d_normed_q, (q_parts[0], o_parts[2]))
        tied = after(d_units, d_normed_q)
        second_half = weight_grad(feed_all, tied, second_cut, 2, 2, 0)
        second_half, q_parts[1] = beside(second_half, q_parts[1])
        second_half = second_half + jnp.concatenate(second_parts, axis=0)
        second_last = send_parts(second_half[2 * BLOCK :], swap_y, 320, 192)
        d_lined[1] = after(d_lined[1], second_half)
        pairs_got.append(swap_x(d_lined[1][rows:]))
        q_parts += send_parts(after(q_send[2 * LANES :], pairs_got[1]), swap_x, 128, 128)
    else:
        every_unit = slice(0, units_width)
        g_gate_up = scatter_yx(
            unit_order(weight_grad(feed_all, d_units, every_unit, count, 1, 0)), True
        )
        g_down = scatter_yx(
            unit_order(weight_grad(cot_all, acts, slice(0, act_width), count, 1, 0)), False
        )
        pairs_got.append(swap_x(d_lined[1][rows:]))
    d_pair_all = jnp.concatenate(
        [pair[:rows] + got for pair, got in zip(d_lined, pairs_got)], axis=0
    )

    back = input_back(
        table,
        d_pair_all,
        kv_raw,
        cosine,
        sine,
        key_gain,
        d_normed_q,
        *d_hiddens,
        tokens_in,
        gains,
        *kvg,
    )
    if paired:
        back, (q_parts[2], second_last[0]) = beside(back, (q_parts[2], second_last[0]))
    d_kv_raw, key_grad, tokens_grad, attention_grad = back
    query_grad = query_gain_grads[0][0] + query_gain_grads[1][0]
    head_grads = jnp.concatenate(
        [query_grad[:HEAD_SIZE] + query_grad[HEAD_SIZE:], key_grad[0, :HEAD_SIZE]]
    ).reshape(-1, per_head)
    head_row = small_order(
        jnp.pad(head_grads, ((0, 0), (0, small - per_head))).reshape(1, width), False
    )
    gain_grads = jnp.concatenate(
        [
            attention_grad[0:1],
            feed_gain_grads[0][0:1] + feed_gain_grads[1][0:1],
            head_row,
            jnp.zeros((5, width), F32),
        ],
        axis=0,
    )
    kv_grads = key_value_grad(normed, d_kv_raw, gain_grads)
    if paired:
        kv_grads, second_last[1] = beside(kv_grads, second_last[1])
        o_send, o_keep = fold(o_parts, o_keep, d_kv_raw)
        kv_got = swap_core(kv_grads[1])
        kv_sums = [kv_grads[0][span(b)] + kv_got[span(b)] for b in range(4)]
        kv_parts = [swap_x(kv_sums[1]), swap_y(kv_sums[2]), swap_xy(kv_sums[3])]
        o_got = swap_x(after(o_send, kv_sums))
        tied = after(acts, kv_sums)
        half = weight_grad(cot_all, tied, slice(0, act_width), 2, 2, 0)
        half, q_parts[3] = beside(half, q_parts[3])
        q_send, q_keep = fold(q_parts, q_keep)
        q_got = swap_y(q_send)
        half = half + jnp.concatenate(down_parts, axis=0)
        tied = after(d_units, half, q_send)
        first_half = weight_grad(feed_all, tied, first_cut, 2, 1, 0)
        first_half, kv_parts = beside(first_half, kv_parts)
        g_kv = kv_sums[0] + kv_parts[0] + kv_parts[1] + kv_parts[2]
        first_half = first_half + jnp.concatenate(first_parts, axis=0)
        first_last = swap_x(after(first_half[2 * BLOCK :], g_kv))
        down_last = swap_y(after(half[2 * BLOCK :], q_send))
        g_o = o_keep + after(o_got, first_half)
        g_q = q_keep + after(q_got, first_half)
        first_last, down_last = after((first_last, down_last), g_o, g_q)
        second_got = jnp.concatenate(second_last, axis=0)
        g_gate_up = jnp.concatenate(
            [first_half[: 2 * BLOCK] + first_last, second_half[: 2 * BLOCK] + second_got], axis=1
        )
        g_down = half[: 2 * BLOCK] + down_last
    else:
        kv_send = kv_grads[0] + swap_core(kv_grads[1])
        g_o, g_q, g_kv = (fold_whole(v) for v in (o_send, q_send, kv_send))
    g_kv = line_scatter(g_kv, 0).astype(F32)
    grad_output = line_scatter(g_o, 0).astype(F32).T
    grad_query = line_scatter(g_q, 1).astype(F32)
    part_rows = g_down.shape[0] // 2
    g_ffn = jnp.concatenate([g_gate_up, g_down], axis=1)
    g_keep = g_ffn[:part_rows]
    g_take = swap_core(g_ffn[part_rows:])
    grads_ffn = []
    for start in (0, units, units_width):
        kept, got = g_keep[:, start : start + units], g_take[:, start : start + units]
        grads_ffn.append(
            jnp.where(
                core == 0,
                jnp.concatenate([kept, got], axis=1),
                jnp.concatenate([got, kept], axis=1),
            ).astype(F32)
        )
    grad_gate, grad_up, grad_down = grads_ffn
    grad_down = grad_down.T

    grad_key_value = (
        g_kv[:, :KV_WIDTH]
        .reshape(small, KEY_VALUE_HEADS, 2, HEAD_SIZE)
        .transpose(0, 2, 1, 3)
        .reshape(small, KV_WIDTH)
    )

    added = [
        lax.psum_scatter(after(v, last_kv), "heads", scatter_dimension=0, tiled=True) for v in added
    ]
    added = after(added, (g_kv, grad_output))
    layer_out = finish_layer(table, *hiddens, *added)

    return (
        from_order(layer_out).reshape(tokens.shape),
        from_order(tokens_grad).reshape(tokens.shape),
        g_kv[:, KV_WIDTH + ATTENTION_GAIN],
        grad_query,
        grad_key_value,
        g_kv[:per_head, KV_WIDTH + HEAD_GAIN],
        grad_output,
        g_kv[:, KV_WIDTH + FEED_GAIN],
        grad_gate,
        grad_up,
        grad_down,
    )


def order_kernel(table, values, out):
    for j in range(values.shape[1] // BLOCK):
        out[:, span(j)] = values[:, place(table, j)]


def order_columns(table, values):
    return kernel_call(
        order_kernel,
        "order_columns",
        (1,),
        [whole(values)],
        fixed_out(values.shape),
        shape(values.shape, values.dtype),
        [],
        0,
        table,
    )(values)


def solution(mesh):
    every = ("dp", "seq", "heads")
    token_spec = P(None, "dp", ("seq", "heads"), None)
    return jax.shard_map(
        on_device,
        mesh=mesh,
        in_specs=(
            token_spec,
            P(None, "dp", None),
            P(every),
            P(("dp", "seq"), "heads"),
            P(every, None),
            P(every),
            P(None, every),
            P(every),
            P(("dp", "seq"), "heads"),
            P(("dp", "seq"), "heads"),
            P("heads", ("dp", "seq")),
            token_spec,
        ),
        out_specs=(
            token_spec,
            token_spec,
            P(every),
            P(("dp", "seq"), "heads"),
            P(every, None),
            P(every),
            P(None, every),
            P(every),
            P(("dp", "seq"), "heads"),
            P(("dp", "seq"), "heads"),
            P("heads", ("dp", "seq")),
        ),
        check_vma=False,
    )
```

```python
import functools
import math

import jax
import jax.numpy as jnp
from jax import lax
from jax.experimental import pallas as pl
from jax.experimental.pallas import tpu as pltpu
from jax.sharding import PartitionSpec as P

QUERY_HEADS = 28
KEY_VALUE_HEADS = 7
HEAD_SIZE = 64
GROUP = QUERY_HEADS // KEY_VALUE_HEADS
GROUP_WIDTH = GROUP * HEAD_SIZE
Q_WIDTH = QUERY_HEADS * HEAD_SIZE
KV_WIDTH = 2 * KEY_VALUE_HEADS * HEAD_SIZE

EPSILON = 1e-06
SCORE_SCALE = 0.125
MASKED = -1e30
LANES = 128
CHUNK = 256
BLOCK = 256
FFN_ROWS = 256
ATTENTION_GAIN, FEED_GAIN, HEAD_GAIN = 0, 1, 2

BF = jnp.bfloat16
F32 = jnp.float32


def dot_nn(left, right):
    return lax.dot_general(left, right, (((1,), (0,)), ((), ())), preferred_element_type=F32)


def dot_nt(left, right):
    return lax.dot_general(left, right, (((1,), (1,)), ((), ())), preferred_element_type=F32)


def dot_tn(left, right):
    return lax.dot_general(left, right, (((0,), (0,)), ((), ())), preferred_element_type=F32)


def shape(dims, kind):
    return jax.ShapeDtypeStruct(dims, kind)


def whole(array):
    dims = array.shape
    return pl.BlockSpec(
        dims, lambda *unused: (0,) * len(dims), pipeline_mode=pl.Buffered(1)
    )


def fixed_out(dims):
    return pl.BlockSpec(dims, lambda *unused: (0,) * len(dims))


def kernel_call(body, name, grid, in_specs, out_specs, out_shape, scratch, flops, table=None):
    outs = out_shape if isinstance(out_shape, (list, tuple)) else [out_shape]
    moved = sum(math.prod(o.shape) * jnp.dtype(o.dtype).itemsize for o in outs)
    kwargs = dict(
        out_shape=out_shape,
        compiler_params=pltpu.CompilerParams(
            dimension_semantics=("arbitrary",) * len(grid), vmem_limit_bytes=56 * 1024 * 1024
        ),
        name=name,
    )

    def call(*operands):
        size = moved + sum(math.prod(o.shape) * o.dtype.itemsize for o in operands)
        cost = pl.CostEstimate(
            flops=flops,
            bytes_accessed=size,
            transcendentals=0,
        )
        if table is None:
            return pl.pallas_call(
                body,
                grid=grid,
                in_specs=in_specs,
                out_specs=out_specs,
                scratch_shapes=scratch,
                cost_estimate=cost,
                **kwargs,
            )(*operands)
        return pl.pallas_call(
            body,
            grid_spec=pltpu.PrefetchScalarGridSpec(
                num_scalar_prefetch=1,
                grid=grid,
                in_specs=in_specs,
                out_specs=out_specs,
                scratch_shapes=scratch,
            ),
            cost_estimate=cost,
            **kwargs,
        )(table, *operands)

    return call


def half_lanes(rows):
    return lax.broadcasted_iota(jnp.int32, (rows, LANES), 1) < HEAD_SIZE


def half_means(values, low):
    first = jnp.sum(jnp.where(low, values, 0.0), axis=1, keepdims=True) / HEAD_SIZE
    second = jnp.sum(jnp.where(low, 0.0, values), axis=1, keepdims=True) / HEAD_SIZE
    return jnp.where(low, first, second)


def turn(values):
    lane = lax.broadcasted_iota(jnp.int32, values.shape, 1)
    early = (lane & (HEAD_SIZE // 2)) == 0
    return jnp.where(
        early, pltpu.roll(values, LANES - HEAD_SIZE // 2, 1), pltpu.roll(values, HEAD_SIZE // 2, 1)
    )


def head_norm(tile, gain, cosine, sine, low):
    normed = tile * lax.rsqrt(half_means(tile * tile, low) + EPSILON) * gain
    return normed * cosine + turn(normed) * sine


def head_norm_back(tile, gain, cosine, sine, low, grad):
    grad = grad * cosine - turn(grad) * sine
    scale = lax.rsqrt(half_means(tile * tile, low) + EPSILON)
    lifted = grad * gain
    dots = half_means(tile * lifted, low)
    d_tile = scale * lifted - tile * (scale * scale * scale) * dots
    return d_tile, jnp.sum(grad * tile * scale, axis=0, keepdims=True)


def place(table, j):
    return pl.ds(pl.multiple_of(table[j] * BLOCK, BLOCK), BLOCK)


def span(j, size=BLOCK):
    return slice(j * size, (j + 1) * size)


def over_pieces(left, pieces, columns=None):
    total, start = None, 0
    for piece in pieces:
        size = piece.shape[0]
        right = piece[...] if columns is None else piece[:, columns]
        term = dot_nn(left[:, start : start + size], right)
        total = term if total is None else total + term
        start += size
    return total


def add_back(target, left, pieces, columns=None):
    start = 0
    for piece in pieces:
        size = piece.shape[0]
        right = piece[...] if columns is None else piece[:, columns]
        target[:, start : start + size] += dot_nt(left, right)
        start += size


def key_value_kernel(table, tokens, cosine, sine, gain, *refs):
    kvg = refs[:-4]
    normed, kv_raw, kv_low, gains = refs[-4:]
    rows, width = tokens.shape
    count = width // BLOCK
    columns = jnp.concatenate([part[:, KV_WIDTH:].astype(F32).T for part in kvg], axis=1)
    gains[...] = columns[:8]
    squares = 0.0
    for j in range(count):
        block = tokens[:, place(table, j)].astype(F32)
        squares = squares + jnp.sum(block * block, axis=1, keepdims=True)
    scale = lax.rsqrt(squares / width + EPSILON)
    for j in range(count):
        block = tokens[:, place(table, j)].astype(F32)
        normed[:, span(j)] = (
            block * scale * columns[ATTENTION_GAIN : ATTENTION_GAIN + 1, span(j)]
        ).astype(BF)
    raw = over_pieces(normed, kvg, slice(0, KV_WIDTH))
    kv_raw[...] = raw
    low = half_lanes(rows)
    for c in range(KEY_VALUE_HEADS):
        tile = raw[:, span(c, LANES)]
        key = head_norm(tile, gain[...], cosine[...], sine[...], low)
        kv_low[:, span(c, LANES)] = jnp.where(low, key, tile).astype(BF)


def project_key_value(table, tokens, cosine, sine, gain, kvg):
    rows, width = tokens.shape
    operands = (tokens, cosine, sine, gain, *kvg)
    return kernel_call(
        key_value_kernel,
        "project_key_value",
        (1,),
        [whole(o) for o in operands],
        [
            fixed_out((rows, width)),
            fixed_out((rows, KV_WIDTH)),
            fixed_out((rows, KV_WIDTH)),
            fixed_out((8, width)),
        ],
        [
            shape((rows, width), BF),
            shape((rows, KV_WIDTH), F32),
            shape((rows, KV_WIDTH), BF),
            shape((8, width), F32),
        ],
        [],
        2 * rows * width * KV_WIDTH,
        table,
    )(*operands)


def query_kernel(normed, cosine, sine, gain, *refs):
    q_raw, queries = refs[-2:]
    rows = normed.shape[0]
    raw = over_pieces(normed, refs[:-2])
    q_raw[...] = raw
    low = half_lanes(rows)
    for tile_index in range(GROUP_WIDTH // LANES):
        tile = raw[:, span(tile_index, LANES)]
        turned = head_norm(tile, gain[...], cosine[...], sine[...], low)
        queries[:, span(tile_index, LANES)] = (turned * SCORE_SCALE).astype(BF)


def column_parts(pieces):
    return [pl.BlockSpec((piece.shape[0], GROUP_WIDTH), lambda c, *t: (0, c)) for piece in pieces]


def project_query(normed, cosine, sine, gain, weight):
    rows, width = normed.shape
    out = pl.BlockSpec((rows, GROUP_WIDTH), lambda c: (0, c))
    return kernel_call(
        query_kernel,
        "project_query",
        (KEY_VALUE_HEADS,),
        [whole(normed), whole(cosine), whole(sine), whole(gain), *column_parts(weight)],
        [out, out],
        [shape((rows, Q_WIDTH), F32), shape((rows, Q_WIDTH), BF)],
        [],
        2 * rows * width * Q_WIDTH,
    )(normed, cosine, sine, gain, *weight)


def output_kernel(table, mixed, tokens, gains, *refs):
    hidden, feed = refs[-2:]
    width = hidden.shape[1]
    step = pl.program_id(0)

    @pl.when(step == 0)
    def _():
        for j in range(width // BLOCK):
            hidden[:, span(j)] = tokens[:, place(table, j)].astype(F32)

    add_back(hidden, mixed[...], refs[:-2])

    @pl.when(step == pl.num_programs(0) - 1)
    def _():
        values = hidden[...]
        scale = lax.rsqrt(jnp.mean(values * values, axis=1, keepdims=True) + EPSILON)
        feed[...] = (values * scale * gains[FEED_GAIN : FEED_GAIN + 1, :]).astype(BF)


def project_output(table, mixed, tokens, batch, gains, weight):
    rows = mixed.shape[0]
    width = tokens.shape[1]
    return kernel_call(
        output_kernel,
        "project_output",
        (KEY_VALUE_HEADS,),
        [
            pl.BlockSpec((rows, GROUP_WIDTH), lambda c, t: (0, c)),
            pl.BlockSpec((rows, width), lambda c, t: (batch, 0)),
            whole(gains),
            *column_parts(weight),
        ],
        [fixed_out((rows, width)), fixed_out((rows, width))],
        [shape((rows, width), F32), shape((rows, width), BF)],
        [],
        2 * rows * width * Q_WIDTH,
        table,
    )(mixed, tokens, gains, *weight)


def hidden_back_kernel(table, d_feed, hidden, cot, gains, *refs):
    d_hidden, d_attended, gain_grad, d_mixed = refs[-4:]
    width = hidden.shape[1]

    @pl.when(pl.program_id(0) == 0)
    def _():
        values = hidden[...]
        grad = d_feed[...].astype(F32)
        scale = lax.rsqrt(jnp.mean(values * values, axis=1, keepdims=True) + EPSILON)
        lifted = grad * gains[FEED_GAIN : FEED_GAIN + 1, :]
        dots = jnp.mean(values * lifted, axis=1, keepdims=True)
        d_norm = scale * lifted - values * (scale * scale * scale) * dots
        gain_grad[...] = jnp.broadcast_to(
            jnp.sum(grad * values * scale, axis=0, keepdims=True), gain_grad.shape
        )
        for j in range(width // BLOCK):
            total = cot[:, place(table, j)].astype(F32) + d_norm[:, span(j)]
            d_hidden[:, span(j)] = total
            d_attended[:, span(j)] = total.astype(BF)

    d_mixed[...] = over_pieces(d_attended, refs[:-4]).astype(BF)


def hidden_back(table, d_feed, hidden, cot, batch, gains, weight):
    rows, width = hidden.shape
    return kernel_call(
        hidden_back_kernel,
        "hidden_back",
        (KEY_VALUE_HEADS,),
        [
            whole(d_feed),
            whole(hidden),
            pl.BlockSpec((rows, width), lambda c, t: (batch, 0)),
            whole(gains),
            *column_parts(weight),
        ],
        [
            fixed_out((rows, width)),
            fixed_out((rows, width)),
            fixed_out((8, width)),
            pl.BlockSpec((rows, GROUP_WIDTH), lambda c, t: (0, c)),
        ],
        [
            shape((rows, width), F32),
            shape((rows, width), BF),
            shape((8, width), F32),
            shape((rows, Q_WIDTH), BF),
        ],
        [],
        2 * rows * width * Q_WIDTH,
        table,
    )(d_feed, hidden, cot, gains, *weight)


def query_back_kernel(d_q, *refs):
    out = refs[-1]

    @pl.when(pl.program_id(0) == 0)
    def _():
        out[...] = jnp.zeros_like(out)

    add_back(out, d_q[...], refs[:-1])


def query_back(d_q, weight):
    rows = d_q.shape[0]
    width = sum(piece.shape[0] for piece in weight)
    return kernel_call(
        query_back_kernel,
        "query_back",
        (KEY_VALUE_HEADS,),
        [pl.BlockSpec((rows, GROUP_WIDTH), lambda c: (0, c)), *column_parts(weight)],
        fixed_out((rows, width)),
        shape((rows, width), F32),
        [],
        2 * rows * width * Q_WIDTH,
    )(d_q, *weight)


def input_back_kernel(
    table,
    d_pair,
    kv_raw,
    cosine,
    sine,
    gain,
    d_normed_q,
    d_hidden0,
    d_hidden1,
    tokens,
    gains,
    *refs,
):
    kvg = refs[:-5]
    d_kv_raw, head_grad, tokens_grad, gain_grad, d_normed = refs[-5:]
    rows, width = tokens.shape
    part = d_hidden0.shape[0]
    low = half_lanes(rows)
    total = 0.0
    for c in range(KEY_VALUE_HEADS):
        grad = d_pair[:, span(c, LANES)].astype(F32)
        d_tile, g_tile = head_norm_back(
            kv_raw[:, span(c, LANES)], gain[...], cosine[...], sine[...], low, grad
        )
        total = total + g_tile
        d_kv_raw[:, span(c, LANES)] = jnp.where(low, d_tile, grad).astype(BF)
    head_grad[...] = jnp.broadcast_to(total, head_grad.shape)
    d_kv = d_kv_raw[...]
    d_normed[...] = d_normed_q[...]
    add_back(d_normed, d_kv, kvg, slice(0, KV_WIDTH))
    squares, dots = 0.0, 0.0
    for j in range(width // BLOCK):
        block = tokens[:, place(table, j)].astype(F32)
        lifted = d_normed[:, span(j)] * gains[ATTENTION_GAIN : ATTENTION_GAIN + 1, span(j)]
        squares = squares + jnp.sum(block * block, axis=1, keepdims=True)
        dots = dots + jnp.sum(block * lifted, axis=1, keepdims=True)
    scale = lax.rsqrt(squares / width + EPSILON)
    dots = dots / width * (scale * scale * scale)
    for j in range(width // BLOCK):
        block = tokens[:, place(table, j)].astype(F32)
        grad = d_normed[:, span(j)]
        lifted = grad * gains[ATTENTION_GAIN : ATTENTION_GAIN + 1, span(j)]
        d_input = scale * lifted - block * dots
        for batch, d_hidden in enumerate((d_hidden0, d_hidden1)):
            tokens_grad[span(batch, part), place(table, j)] = (
                d_hidden[:, span(j)] + d_input[span(batch, part), :]
            )
        gain_grad[:, span(j)] = jnp.broadcast_to(
            jnp.sum(grad * block * scale, axis=0, keepdims=True), (8, BLOCK)
        )


def input_back(table, *operands):
    tokens = operands[8]
    rows, width = tokens.shape
    return kernel_call(
        input_back_kernel,
        "input_back",
        (1,),
        [whole(o) for o in operands],
        [
            fixed_out((rows, KV_WIDTH)),
            fixed_out((8, LANES)),
            fixed_out((rows, width)),
            fixed_out((8, width)),
        ],
        [
            shape((rows, KV_WIDTH), BF),
            shape((8, LANES), F32),
            shape((rows, width), F32),
            shape((8, width), F32),
        ],
        [pltpu.VMEM((rows, width), F32)],
        2 * rows * width * KV_WIDTH,
        table,
    )(*operands)


def layer_out_kernel(table, hidden0, hidden1, added0, added1, out):
    part = hidden0.shape[0]
    for batch, (hidden, added) in enumerate(((hidden0, added0), (hidden1, added1))):
        for j in range(hidden.shape[1] // BLOCK):
            out[span(batch, part), place(table, j)] = (
                hidden[:, span(j)] + added[:, span(j)].astype(F32)
            ).astype(BF)


def finish_layer(table, *operands):
    rows, width = operands[0].shape
    return kernel_call(
        layer_out_kernel,
        "finish_layer",
        (1,),
        [whole(o) for o in operands],
        fixed_out((2 * rows, width)),
        shape((2 * rows, width), BF),
        [],
        0,
        table,
    )(*operands)


def key_value_grad_kernel(normed, d_kv_raw, gain_grads, out0, out1):
    half = normed.shape[1] // 2
    for index, out in enumerate((out0, out1)):
        cut = span(index, half)
        out[:, :KV_WIDTH] = dot_tn(normed[:, cut], d_kv_raw[...]).astype(BF)
        rows = gain_grads[:, cut]
        rows = jnp.concatenate([rows, jnp.zeros((LANES - 8, half), F32)], axis=0)
        out[:, KV_WIDTH:] = rows.T.astype(BF)


def key_value_grad(normed, d_kv_raw, gain_grads):
    rows, width = normed.shape
    dims = (width // 2, KV_WIDTH + LANES)
    return kernel_call(
        key_value_grad_kernel,
        "key_value_grad",
        (1,),
        [whole(normed), whole(d_kv_raw), whole(gain_grads)],
        [fixed_out(dims), fixed_out(dims)],
        [shape(dims, BF), shape(dims, BF)],
        [],
        2 * rows * width * KV_WIDTH,
    )(normed, d_kv_raw, gain_grads)


def pad_heads(tile, low, keep_low):
    parts = []
    for pair in range(GROUP // 2):
        both = tile[:, span(pair, LANES)].astype(F32)
        turned = pltpu.roll(both, HEAD_SIZE, 1)
        first, second = (both, turned) if keep_low else (turned, both)
        keep = low if keep_low else jnp.logical_not(low)
        parts.append(jnp.where(keep, first, 0.0))
        parts.append(jnp.where(keep, second, 0.0))
    return jnp.concatenate(parts, axis=0).astype(BF)


def four_wide(row):
    return jnp.concatenate([row] * GROUP, axis=1)


def heads_back(stacked, rows):
    parts = []
    for pair in range(GROUP // 2):
        start = 2 * pair * rows
        both = jnp.concatenate(
            [stacked[:, start : start + rows], stacked[:, start + rows : start + 2 * rows]], axis=0
        )
        parts.append(both.T)
    return jnp.concatenate(parts, axis=1)


def key_rows(kv, cut):
    rows = kv.shape[2]
    block = kv[cut.start // rows : cut.stop // rows, 0]
    return block.reshape(cut.stop - cut.start, kv.shape[3])


def every_row(kv):
    return key_rows(kv, slice(0, kv.shape[0] * kv.shape[2]))


def ones_and_values(kv):
    values = every_row(kv)
    return jnp.where(half_lanes(values.shape[0]), 1.0, values.astype(F32)).astype(BF)


def attention_forward_kernel(kv0, kv1, query, bias0, bias1, mixed, lse, expo):
    rows = query.shape[0]
    half = bias0.shape[0]
    padded = pad_heads(query[...], half_lanes(rows), True)
    for part, (kv, bias) in enumerate(((kv0, bias0), (kv1, bias1))):
        for step in range(half // CHUNK):
            cut = span(step, CHUNK)
            weight = jnp.exp(dot_nt(key_rows(kv, cut), padded) + four_wide(bias[cut, :]))
            expo[part * half + step * CHUNK : part * half + (step + 1) * CHUNK, :] = weight.astype(BF)
    total = dot_tn(ones_and_values(kv0), expo[:half, :]) + dot_tn(
        ones_and_values(kv1), expo[half:, :]
    )
    lse[...] = jnp.log(total[0:1, :])[None]
    mixed[...] = heads_back(total[HEAD_SIZE:, :] / total[:HEAD_SIZE, :], rows).astype(BF)


def attention_forward(kv0, kv1, query, batch, bias0, bias1):
    half, rows = bias0.shape
    wide = GROUP * rows
    keys = pl.BlockSpec((half // rows, 1, rows, LANES), lambda c: (0, 0, 0, c))
    kv0, kv1 = (kv.reshape(half // rows, -1, rows, KV_WIDTH) for kv in (kv0, kv1))
    return kernel_call(
        attention_forward_kernel,
        "attention_forward",
        (KEY_VALUE_HEADS,),
        [
            keys,
            keys,
            pl.BlockSpec((rows, GROUP_WIDTH), lambda c: (batch, c)),
            whole(bias0),
            whole(bias1),
        ],
        [
            pl.BlockSpec((rows, GROUP_WIDTH), lambda c: (0, c)),
            pl.BlockSpec((1, 1, wide), lambda c: (c, 0, 0)),
        ],
        [shape((rows, Q_WIDTH), BF), shape((KEY_VALUE_HEADS, 1, wide), F32)],
        [pltpu.VMEM((2 * half, wide), BF)],
        KEY_VALUE_HEADS * 2 * half * wide * LANES * 12,
    )(kv0, kv1, query, bias0, bias1)


def attention_backward_kernel(
    kv0,
    kv1,
    query,
    mixed,
    d_mixed,
    bias0,
    bias1,
    lse,
    q_raw,
    cosine,
    sine,
    gain,
    d_q_raw,
    d_kv0,
    d_kv1,
    gain_grad,
    d_scores,
):
    rows = query.shape[0]
    half = bias0.shape[0]
    low = half_lanes(rows)
    padded = pad_heads(query[...], low, True)
    d_padded = pad_heads(d_mixed[...], low, False)
    product = d_mixed[...].astype(F32) * mixed[...].astype(F32)
    pick = (
        lax.broadcasted_iota(jnp.int32, (8, GROUP_WIDTH), 1) // HEAD_SIZE
        == lax.broadcasted_iota(jnp.int32, (8, GROUP_WIDTH), 0)
    ).astype(F32)
    balance = lax.dot_general(
        pick,
        product,
        (((1,), (1,)), ((), ())),
        precision=lax.Precision.HIGHEST,
        preferred_element_type=F32,
    )
    balance = jnp.concatenate([balance[head : head + 1, :] for head in range(GROUP)], axis=1)
    level = lse[0]
    for part, (kv, bias, d_kv) in enumerate(((kv0, bias0, d_kv0), (kv1, bias1, d_kv1))):
        for step in range(half // CHUNK):
            cut = span(step, CHUNK)
            block = key_rows(kv, cut)
            probs = jnp.exp(dot_nt(block, padded) + four_wide(bias[cut, :]) - level)
            d_probs = dot_nt(block, d_padded)
            low_scores = (probs * (d_probs - balance)).astype(BF)
            d_scores[part * half + step * CHUNK : part * half + (step + 1) * CHUNK, :] = low_scores
            d_kv[cut, :] = (
                dot_nn(low_scores, padded) + dot_nn(probs.astype(BF), d_padded)
            ).astype(BF)
    total = dot_tn(every_row(kv0), d_scores[:half, :]) + dot_tn(
        every_row(kv1), d_scores[half:, :]
    )
    d_query = heads_back(total[:HEAD_SIZE, :] * SCORE_SCALE, rows)
    grads = 0.0
    for tile_index in range(GROUP_WIDTH // LANES):
        cut = span(tile_index, LANES)
        d_tile, g_tile = head_norm_back(
            q_raw[:, cut], gain[...], cosine[...], sine[...], low, d_query[:, cut]
        )
        d_q_raw[:, cut] = d_tile.astype(BF)
        grads = grads + g_tile

    @pl.when(pl.program_id(0) == 0)
    def _():
        gain_grad[...] = jnp.zeros_like(gain_grad)

    gain_grad[...] += jnp.broadcast_to(grads, gain_grad.shape)


def attention_backward(
    kv0, kv1, query, batch, mixed, d_mixed, bias0, bias1, lse, q_raw, cosine, sine, gain
):
    half, rows = bias0.shape
    wide = GROUP * rows
    keys = pl.BlockSpec((half // rows, 1, rows, LANES), lambda c: (0, 0, 0, c))
    kv0, kv1 = (kv.reshape(half // rows, -1, rows, KV_WIDTH) for kv in (kv0, kv1))
    d_keys = pl.BlockSpec((half, LANES), lambda c: (0, c))
    heads = pl.BlockSpec((rows, GROUP_WIDTH), lambda c: (0, c))
    part = pl.BlockSpec((rows, GROUP_WIDTH), lambda c: (batch, c))
    table = pl.BlockSpec((rows, LANES), lambda c: (batch, 0))
    return kernel_call(
        attention_backward_kernel,
        "attention_backward",
        (KEY_VALUE_HEADS,),
        [
            keys,
            keys,
            part,
            heads,
            heads,
            whole(bias0),
            whole(bias1),
            pl.BlockSpec((1, 1, wide), lambda c: (c, 0, 0)),
            part,
            table,
            table,
            whole(gain),
        ],
        [heads, d_keys, d_keys, fixed_out((8, LANES))],
        [
            shape((rows, Q_WIDTH), BF),
            shape((half, KV_WIDTH), BF),
            shape((half, KV_WIDTH), BF),
            shape((8, LANES), F32),
        ],
        [pltpu.VMEM((2 * half, wide), BF)],
        KEY_VALUE_HEADS * 2 * half * wide * LANES * 28,
    )(kv0, kv1, query, mixed, d_mixed, bias0, bias1, lse, q_raw, cosine, sine, gain)


def swap_halves(values):
    half = values.shape[1] // 2
    return jnp.concatenate([values[:, half:], values[:, :half]], axis=1)


def feed_forward_kernel(count, units, *refs):
    feed0, feed1, cot0, cot1 = refs[:4]
    gate_up = refs[4 : 4 + count]
    down = refs[4 + count : 4 + 2 * count]
    act_out, d_units_out, out0, out1, d_feed0, d_feed1 = refs[4 + 2 * count :]
    first = pl.program_id(0) < pl.num_programs(0) // 2
    rows, width = feed0.shape
    half = width // 2
    size = down[0].shape[0] // 2
    feed = jnp.where(first, swap_halves(feed0[...]), feed1[...])
    cot = jnp.where(first, swap_halves(cot0[...]), cot1[...])

    def over(left, pieces):
        total = None
        for b, piece in enumerate(pieces):
            both = jnp.concatenate(
                [left[:, b * size : (b + 1) * size], left[:, half + b * size : half + (b + 1) * size]],
                axis=1,
            )
            term = dot_nn(both, piece[...])
            total = term if total is None else total + term
        return total

    both = over(feed, gate_up)
    gate_pre, up_pre = both[:, :units], both[:, units : 2 * units]
    sig = 1.0 / (1.0 + jnp.exp(-gate_pre))
    silu = gate_pre * sig
    act = (silu * up_pre).astype(BF)
    act = jnp.concatenate([act, jnp.zeros((rows, down[0].shape[1] - units), BF)], axis=1)
    act_out[...] = act
    d_act = over(cot, down)[:, :units]
    d_gate = d_act * up_pre * (sig * (1.0 + gate_pre * (1.0 - sig)))
    d_units = jnp.concatenate(
        [
            d_gate.astype(BF),
            (d_act * silu).astype(BF),
            jnp.zeros((rows, gate_up[0].shape[1] - 2 * units), BF),
        ],
        axis=1,
    )
    d_units_out[...] = d_units

    def write(target, left, pieces, swapped):
        for b, piece in enumerate(pieces):
            block = dot_nt(left, piece[...]).astype(BF)
            early, late = (half, 0) if swapped else (0, half)
            target[:, early + b * size : early + (b + 1) * size] = block[:, :size]
            target[:, late + b * size : late + (b + 1) * size] = block[:, size:]

    @pl.when(first)
    def _():
        write(d_feed0, d_units, gate_up, True)
        write(out0, act, down, True)

    @pl.when(jnp.logical_not(first))
    def _():
        write(d_feed1, d_units, gate_up, False)
        write(out1, act, down, False)


def feed_forward(feeds, cots, gate_up, down, units):
    tokens, width = feeds[0].shape
    steps = tokens // FFN_ROWS
    early = pl.BlockSpec((FFN_ROWS, width), lambda i: (jnp.minimum(i, steps - 1), 0))
    late = pl.BlockSpec((FFN_ROWS, width), lambda i: (jnp.maximum(i - steps, 0), 0))
    act_width, units_width = down[0].shape[1], gate_up[0].shape[1]
    return kernel_call(
        functools.partial(feed_forward_kernel, len(down), units),
        "feed_forward",
        (2 * steps,),
        [early, late, early, late, *[whole(w) for w in (*gate_up, *down)]],
        [
            pl.BlockSpec((FFN_ROWS, act_width), lambda i: (i, 0)),
            pl.BlockSpec((FFN_ROWS, units_width), lambda i: (i, 0)),
            early,
            late,
            early,
            late,
        ],
        [
            shape((2 * tokens, act_width), BF),
            shape((2 * tokens, units_width), BF),
            *[shape((tokens, width), BF)] * 4,
        ],
        [],
        2 * tokens * 2 * width * units * 6,
    )(*feeds, *cots, *gate_up, *down)


def weight_grad_kernel(count, columns, *refs):
    lefts = refs[: 2 * count]
    rights = refs[2 * count : -1]
    out = refs[-1]
    rows = lefts[0].shape[0]
    each = count // len(rights)
    total = None
    for index in range(count):
        left = jnp.concatenate([lefts[2 * index][...], lefts[2 * index + 1][...]], axis=1)
        right = rights[index // each]
        term = dot_tn(left, right[span(index % each, rows), columns])
        total = term if total is None else total + term
    out[...] = total.astype(BF)


def weight_grad(lefts, rights, columns, steps, stride, offset):
    rows, width = lefts[0].shape
    units = columns.stop - columns.start
    half = width // 2 // BLOCK
    mine = pl.BlockSpec((rows, BLOCK), lambda i: (0, i * stride + offset))
    other = pl.BlockSpec((rows, BLOCK), lambda i: (0, half + i * stride + offset))
    specs, operands = [], []
    for index, left in enumerate(lefts):
        specs += [other, mine] if index % 2 == 0 else [mine, other]
        operands += [left, left]
    return kernel_call(
        functools.partial(weight_grad_kernel, len(lefts), columns),
        "weight_grad",
        (steps,),
        [*specs, *[whole(r) for r in rights]],
        pl.BlockSpec((2 * BLOCK, units), lambda i: (i, 0)),
        shape((2 * BLOCK * steps, units), BF),
        [],
        2 * len(lefts) * rows * 2 * BLOCK * steps * units,
    )(*operands, *rights)


def rotary_tables(places):
    half_width = HEAD_SIZE // 2
    freqs = jnp.exp(jnp.arange(half_width, dtype=F32) * (-2.0 * math.log(10000.0) / HEAD_SIZE))
    angles = places.astype(F32)[:, None] * freqs[None, :]
    cosine, sine = jnp.cos(angles), jnp.sin(angles)
    return (
        jnp.concatenate([cosine] * 4, axis=1),
        jnp.concatenate([-sine, sine, -sine, sine], axis=1),
    )


def padded_columns(values, columns):
    return jnp.pad(values, ((0, 0), (0, columns - values.shape[1])))


def up_to(size):
    return -(-size // LANES) * LANES


def on_device(
    tokens,
    lengths,
    attention_gain,
    query_weight,
    key_value_matrix,
    per_head_gains,
    output_weight,
    feed_gain,
    gate_weight,
    up_weight,
    down_weight,
    cotangent,
):
    batches = tokens.shape[0]
    rows = tokens.shape[2]
    width = tokens.shape[3]
    dp_size = lax.axis_size("dp")
    heads_size = lax.axis_size("heads")
    seq_size = lax.axis_size("seq")
    assert seq_size == 4 and heads_size == 4 and batches == 2
    paired = dp_size == 2
    y = lax.axis_index("dp").astype(jnp.int32)
    s = lax.axis_index("seq").astype(jnp.int32)
    z = lax.axis_index("heads").astype(jnp.int32)
    x = s // 2
    core = s % 2

    def after(v, *others):
        return lax.optimization_barrier((v, others))[0]

    def beside(outs, parts):
        return lax.optimization_barrier((outs, parts))

    def swap_x(v):
        return lax.ppermute(v, "seq", [(i, i ^ 2) for i in range(4)])

    def swap_xy(v):
        return lax.ppermute(v, ("dp", "seq"), [(i, i ^ 6) for i in range(8)])

    def swap_core(v):
        return lax.ppermute(v, "seq", [(i, i ^ 1) for i in range(4)])

    def swap_y(v):
        return lax.ppermute(v, "dp", [(0, 1), (1, 0)])

    def line_sends(v, axis):
        cut = jnp.split(v, 4, axis=axis)
        got = []
        for k in range(1, 4):
            block = lax.select_n(z, *[cut[i ^ k] for i in range(4)])
            got.append(lax.ppermute(block, "heads", [(i, i ^ k) for i in range(4)]))
        return lax.select_n(z, *cut), got

    def line_sum(own_block, got):
        return own_block + got[0] + got[1] + got[2]

    def gather_near(v):
        if not paired:
            both = jnp.stack([v, swap_x(v)], axis=0)
            return [lax.all_gather(both, "dp", axis=0).reshape(-1, v.shape[-1])]
        return [v, swap_x(v), swap_y(v)]

    def gather_far(near, x_first):
        if not paired:
            return near
        return [*near, swap_y(near[1]) if x_first else swap_x(near[2])]

    def pair_gather(v, axis):
        def step(u, upper, distance):
            got = lax.ppermute(u, "heads", [(i, i ^ distance) for i in range(4)])
            return jnp.where(
                upper,
                jnp.concatenate([got, u], axis=axis),
                jnp.concatenate([u, got], axis=axis),
            )

        return step(step(v, z % 2 == 1, 1), z >= 2, 2)

    def both_cores(pieces):
        return [*pieces, *[swap_core(v) for v in pieces]]

    def unit_pieces(pieces):
        if paired:
            return pieces
        g = pieces[0].reshape(blocks, 2, -1, pieces[0].shape[-1])
        return [g.transpose(1, 0, 2, 3).reshape(pieces[0].shape)]

    def scatter_yx(g, x_last, first=(), second=()):
        def along_x(u, late):
            return u[..., 0, :, :] + after(swap_x(u[..., 1, :, :]), late)

        def along_y(u, late):
            if paired:
                return u[0] + after(swap_y(u[1]), late)
            return lax.psum_scatter(u, "dp", scatter_dimension=0)

        if x_last:
            return along_x(along_y(g, first), second)
        return along_y(along_x(g, first), second)

    blocks = 2 * dp_size
    piece = width // blocks

    if paired:
        own = (2 * y + x) * 2 + core
        places_of = jnp.array([b * 2 + c for c in range(2) for b in range(4)], jnp.int32)
        table = places_of ^ own

        def to_order(v):
            return v

        from_order = to_order
    else:
        table = jnp.arange(width // BLOCK, dtype=jnp.int32)

        def flip(v):
            u = v.reshape(v.shape[:-1] + (dp_size, 2, 2, piece // 2))
            u = jnp.where(x == 1, u[..., ::-1, :, :], u)
            return jnp.where(core == 1, u[..., ::-1, :], u)

        def to_order(v):
            return jnp.moveaxis(flip(v), -2, -4).reshape(v.shape)

        def from_order(v):
            u = v.reshape(v.shape[:-1] + (2, dp_size, 2, piece // 2))
            return flip(jnp.moveaxis(u, -4, -2).reshape(v.shape)).reshape(v.shape)

    def small_order(v, back):
        if not paired:
            return from_order(v) if back else to_order(v)
        cut = v.reshape(8, -1)
        return jnp.concatenate(
            [
                lax.select_n(own, *[cut[held(i, m, back)] for m in range(8)])
                for i in range(8)
            ]
        ).reshape(v.shape)

    def held(i, m, back):
        if back:
            source = i ^ m
            return (source % 2) * 4 + source // 2
        return ((i % 4) * 2 + i // 4) ^ m

    small = key_value_matrix.shape[0]
    per_head = per_head_gains.shape[0]
    kv_local = (
        key_value_matrix.reshape(small, 2, KEY_VALUE_HEADS, HEAD_SIZE)
        .transpose(0, 2, 1, 3)
        .reshape(small, KV_WIDTH)
    )
    gains_local = jnp.stack(
        [attention_gain, feed_gain, jnp.pad(per_head_gains, (0, small - per_head))], axis=1
    )
    kvg_local = jnp.concatenate([kv_local, padded_columns(gains_local, LANES)], axis=1)
    kvg_rows = pair_gather(kvg_local, 0)
    kvg_near = gather_near(kvg_rows)

    tokens_in = to_order(tokens[:, 0].reshape(batches * rows, width))
    cot_in = to_order(cotangent[:, 0].reshape(batches * rows, width))
    cot_held = order_columns(table, cot_in) if paired else cot_in
    projections = lax.all_gather(
        jnp.concatenate([query_weight.reshape(small, Q_WIDTH), output_weight.T], axis=0),
        "heads",
        axis=0,
    )
    q_rows = (
        projections[:, :small]
        .reshape(heads_size, query_weight.shape[0], query_weight.shape[1])
        .transpose(1, 0, 2)
        .reshape(query_weight.shape[0], Q_WIDTH)
    )
    o_rows = projections[:, small:].reshape(4 * small, Q_WIDTH)
    lined = lax.all_gather(cot_held, "heads", axis=0)
    cots_mine = [
        lined[:, span(batch, rows)].reshape(heads_size * rows, width) for batch in range(batches)
    ]

    units = gate_weight.shape[1] // 2
    act_width, units_width = up_to(units), up_to(2 * units)

    def unit_half(v, which):
        return jnp.where(which == 0, v[:, :units], v[:, units:])

    down_local = down_weight.T

    def halves(which):
        gate_up = jnp.concatenate([unit_half(gate_weight, which), unit_half(up_weight, which)], axis=1)
        return jnp.concatenate(
            [padded_columns(gate_up, units_width), padded_columns(unit_half(down_local, which), act_width)],
            axis=1,
        )

    keep = halves(core)
    take = swap_core(halves(1 - core))
    ffn_rows = jnp.concatenate([keep, take], axis=0)
    down_near = gather_near(ffn_rows[:, units_width:])
    gate_up_near = gather_near(after(ffn_rows[:, :units_width], kvg_near))
    gate_up = unit_pieces(gather_far(gate_up_near, True))
    kvg = both_cores(gather_far(after(kvg_near, down_near), True))

    head_column = jnp.concatenate([part[:, KV_WIDTH + HEAD_GAIN] for part in kvg])
    head_scale = small_order(head_column.astype(F32)[None], True)
    head_scale = head_scale.reshape(-1, small)[:, :per_head].reshape(1, -1)
    query_gain = jnp.concatenate([head_scale[:, :HEAD_SIZE]] * 2, axis=1)
    key_gain = jnp.concatenate([head_scale[:, HEAD_SIZE:]] * 2, axis=1)

    block_rows = rows * heads_size
    spots = s * block_rows + z * rows + jnp.arange(rows, dtype=jnp.int32)
    inside = jnp.arange(rows, dtype=jnp.int32)

    def key_spots(first):
        lines = jnp.arange(heads_size, dtype=jnp.int32)[:, None, None] * rows
        fronts = jnp.stack([first, first ^ 2])[None, :, None] * block_rows
        return (lines + fronts + inside[None, None, :]).reshape(-1)

    def bias_for(begin, first):
        keys = key_spots(first)[:, None]
        return jnp.where((keys <= spots[None, :]) & (keys >= begin[None, :]), 0.0, MASKED)

    begins, biases = [], []
    for batch in range(batches):
        sizes = lengths[batch, 0]
        finish = jnp.cumsum(sizes)
        begin = jnp.sum(
            jnp.where(spots[:, None] >= finish[None, :], sizes[None, :], 0), axis=1
        ).astype(jnp.int32)
        begins.append(begin)
        biases.append((bias_for(begin, s), bias_for(begin, s ^ 1)))
    cosine, sine = rotary_tables(jnp.concatenate([spots - begin for begin in begins]))

    normed, kv_raw, kv_low, gains = project_key_value(
        table, after(tokens_in, down_near), cosine, sine, key_gain, kvg
    )
    kv_got = swap_x(kv_low)
    kv_lined = []
    for batch in range(batches):
        cut = span(batch, rows)
        pair = jnp.concatenate([kv_low[cut], kv_got[cut]], axis=0)
        if batch == 0:
            pair = after(pair, gate_up_near, lined)
        kv_lined.append(lax.all_gather(pair, "heads", axis=0, tiled=True))
    down = unit_pieces(gather_far(down_near, False))
    q_near = gather_near(q_rows)
    q_full = both_cores(gather_far(after(q_near, kv_got), False))
    o_near = gather_near(after(o_rows, q_near))
    q_raw, queries = project_query(after(normed, kv_lined[0]), cosine, sine, query_gain, q_full)
    o_pieces = gather_far(after(o_near, queries), True)
    kv_lined[0] = after(kv_lined[0], queries, o_near)
    kvs = [(v, swap_core(v)) for v in kv_lined]

    feeds, mixeds, lses, hiddens = [], [], [], []
    for batch in range(batches):
        query = queries if batch == 0 else after(queries, hiddens[0])
        mixed, lse = attention_forward(*kvs[batch], query, batch, *biases[batch])
        if batch == 0:
            o_full = both_cores(after(o_pieces, mixed))
        else:
            (mixed, lse), (gate_up, down) = beside((mixed, lse), (gate_up, down))
        hidden_in, feed_rows = project_output(
            table, mixed, tokens_in, batch, gains, o_full
        )
        feeds.append(lax.all_gather(feed_rows, "heads", axis=0, tiled=True))
        mixeds.append(mixed)
        lses.append(lse)
        hiddens.append(hidden_in)

    feeds[0] = after(feeds[0], feed_rows)
    feeds = [(swap_core(v), v) for v in feeds]

    d_feeds, acts, d_units, cots = [], [], [], []
    added = []
    for batch in range(batches):
        if batch == 1:
            feeds[1] = after(feeds[1], added[0])
        cot_pair = (swap_core(cots_mine[batch]), cots_mine[batch])
        act, d_unit, out_other, out_mine, d_feed_other, d_feed_mine = feed_forward(
            feeds[batch], cot_pair, gate_up, down, units
        )
        acts.append(act)
        d_units.append(d_unit)
        cots.append(cot_pair)
        added.append(out_mine + swap_core(out_other))
        d_feed = d_feed_mine + swap_core(d_feed_other)
        if batch + 1 < batches:
            d_feed = after(d_feed, feeds[batch + 1])
        d_feeds.append(lax.psum_scatter(d_feed, "heads", scatter_dimension=0, tiled=True))

    feed_all = [f for pair in feeds for f in pair]
    cot_all = [c for pair in cots for c in pair]
    count = width // 2 // BLOCK

    def unit_order(g):
        g = g.reshape(count, 2, BLOCK, -1).transpose(1, 0, 2, 3)
        g = g.reshape(2, blocks, piece // 2, -1).transpose(1, 0, 2, 3)
        return g.reshape(dp_size, 2, piece, -1)

    cut_at = up_to(units)

    def both_grads(left, right):
        return [dot_tn(left[:, span(i, width // 2)], right).astype(BF) for i in range(2)]

    def split_rows(mine, got, along_y=True):
        if not paired:
            return mine + got, None
        size = mine.shape[0] // 4
        far = (2, 3) if along_y else (1, 3)
        near = (0, 1) if along_y else (0, 2)

        def pick(v, blocks_of):
            return jnp.concatenate([v[span(b, size)] for b in blocks_of], axis=0)

        return pick(mine, far) + pick(got, far), pick(mine, near) + pick(got, near)

    def send_parts(v, swap, *rows_of):
        parts, start = [], 0
        for size in rows_of:
            parts.append(swap(v[start : start + size]))
            start += size
        assert start == v.shape[0]
        return parts

    def halved(total):
        near = total.shape[0] // 2
        return total[near:], total[:near]

    def fold(parts, kept, *late):
        return halved(kept + after(jnp.concatenate(parts, axis=0), late))

    def fold_whole(sent):
        g = sent.reshape(dp_size, 2, -1, sent.shape[-1])
        g = lax.psum_scatter(g, "dp", scatter_dimension=0)
        return g[0] + swap_x(g[1])

    d_hiddens, d_attendeds, d_q_raws, d_lined = [], [], [], []
    feed_gain_grads, query_gain_grads = [], []
    mixed_all = jnp.concatenate(mixeds, axis=0)
    first_cut, second_cut = slice(0, cut_at), slice(cut_at, up_to(2 * units))
    if paired:
        first_far = weight_grad(feed_all, d_units, first_cut, 2, 1, 2)
        first_parts = send_parts(first_far, swap_y, 384, 640)
        second_far = weight_grad(feed_all, after(d_units, first_far), second_cut, 2, 2, 1)
        second_parts = send_parts(second_far, swap_x, 384, 640)
        d_feeds[0] = after(d_feeds[0], second_far)
    for batch in range(batches):
        d_feed = d_feeds[batch]
        if batch == 1:
            d_feed = after(d_feed, d_q_raws[0])
            if paired:
                tied = after(acts, d_q_raws[0])
                down_far = weight_grad(cot_all, tied, slice(0, act_width), 2, 2, 1)
                down_parts = send_parts(down_far, swap_x, 256, 640, 128)
                d_feed = after(d_feed, down_far, last_kv)
        back = hidden_back(table, d_feed, hiddens[batch], cot_in, batch, gains, o_full)
        if paired and batch == 0:
            back, (first_parts[0], second_parts[0]) = beside(
                back, (first_parts[0], second_parts[0])
            )
        if paired and batch == 1:
            back, down_parts[0] = beside(back, down_parts[0])
        d_hidden, d_attended, feed_grad, d_mixed = back
        d_hiddens.append(d_hidden)
        d_attendeds.append(d_attended)
        if batch == 1:
            o_grads = both_grads(jnp.concatenate(d_attendeds, axis=0), mixed_all)
            o_send, o_keep = split_rows(o_grads[0], swap_core(o_grads[1]))
            d_mixed = after(d_mixed, o_send)
            if paired:
                o_parts = send_parts(o_send, swap_y, 256, 128, 128)
        back = attention_backward(
            *kvs[batch],
            queries,
            batch,
            mixeds[batch],
            d_mixed,
            *biases[batch],
            lses[batch],
            q_raw,
            cosine,
            sine,
            query_gain,
        )
        if paired and batch == 0:
            back, (first_parts[1], second_parts[1]) = beside(
                back, (first_parts[1], second_parts[1])
            )
        if paired and batch == 1:
            back, (down_parts[1], o_parts[0]) = beside(back, (down_parts[1], o_parts[0]))
        d_q_raw, d_kv0, d_kv1, query_grad = back
        d_kv = d_kv0 + swap_core(d_kv1)
        last_kv = d_kv
        d_lined.append(lax.psum_scatter(d_kv, "heads", scatter_dimension=0, tiled=True))
        d_q_raws.append(d_q_raw)
        feed_gain_grads.append(feed_grad)
        query_gain_grads.append(query_grad)

    pairs_got = [swap_x(d_lined[0][rows:])]
    d_q_raw_all = jnp.concatenate(d_q_raws, axis=0)
    q_grads = both_grads(after(normed, last_kv), d_q_raw_all)
    if paired:
        q_grads, (down_parts[2], o_parts[1], pairs_got) = beside(
            q_grads, (down_parts[2], o_parts[1], pairs_got)
        )
    q_send, q_keep = split_rows(q_grads[0], swap_core(q_grads[1]), False)
    d_normed_q = query_back(after(d_q_raw_all, q_send), q_full)
    if paired:
        q_parts = send_parts(q_send[: 2 * LANES], swap_x, 128, 128)
        d_normed_q, (q_parts[0], o_parts[2]) = beside(d_normed_q, (q_parts[0], o_parts[2]))
        tied = after(d_units, d_normed_q)
        second_half = weight_grad(feed_all, tied, second_cut, 2, 2, 0)
        second_half, q_parts[1] = beside(second_half, q_parts[1])
        second_half = second_half + jnp.concatenate(second_parts, axis=0)
        second_last = send_parts(second_half[2 * BLOCK :], swap_y, 320, 192)
        d_lined[1] = after(d_lined[1], second_half)
        pairs_got.append(swap_x(d_lined[1][rows:]))
        q_parts += send_parts(after(q_send[2 * LANES :], pairs_got[1]), swap_x, 128, 128)
    else:
        every_unit = slice(0, units_width)
        g_gate_up = scatter_yx(
            unit_order(weight_grad(feed_all, d_units, every_unit, count, 1, 0)), True
        )
        g_down = scatter_yx(
            unit_order(weight_grad(cot_all, acts, slice(0, act_width), count, 1, 0)), False
        )
        pairs_got.append(swap_x(d_lined[1][rows:]))
    d_pair_all = jnp.concatenate(
        [pair[:rows] + got for pair, got in zip(d_lined, pairs_got)], axis=0
    )

    back = input_back(
        table,
        d_pair_all,
        kv_raw,
        cosine,
        sine,
        key_gain,
        d_normed_q,
        *d_hiddens,
        tokens_in,
        gains,
        *kvg,
    )
    if paired:
        back, (q_parts[2], second_last[0]) = beside(back, (q_parts[2], second_last[0]))
    d_kv_raw, key_grad, tokens_grad, attention_grad = back
    query_grad = query_gain_grads[0][0] + query_gain_grads[1][0]
    head_grads = jnp.concatenate(
        [query_grad[:HEAD_SIZE] + query_grad[HEAD_SIZE:], key_grad[0, :HEAD_SIZE]]
    ).reshape(-1, per_head)
    head_row = small_order(
        jnp.pad(head_grads, ((0, 0), (0, small - per_head))).reshape(1, width), False
    )
    gain_grads = jnp.concatenate(
        [
            attention_grad[0:1],
            feed_gain_grads[0][0:1] + feed_gain_grads[1][0:1],
            head_row,
            jnp.zeros((5, width), F32),
        ],
        axis=0,
    )
    kv_grads = key_value_grad(normed, d_kv_raw, gain_grads)
    if paired:
        kv_grads, second_last[1] = beside(kv_grads, second_last[1])
        o_send, o_keep = fold(o_parts, o_keep, d_kv_raw)
        kv_got = swap_core(kv_grads[1])
        kv_sums = [kv_grads[0][span(b)] + kv_got[span(b)] for b in range(4)]
        kv_parts = [swap_x(kv_sums[1]), swap_y(kv_sums[2]), swap_xy(kv_sums[3])]
        o_got = swap_x(after(o_send, kv_sums))
        tied = after(acts, kv_sums)
        half = weight_grad(cot_all, tied, slice(0, act_width), 2, 2, 0)
        half, q_parts[3] = beside(half, q_parts[3])
        q_send, q_keep = fold(q_parts, q_keep)
        q_got = swap_y(q_send)
        half = half + jnp.concatenate(down_parts, axis=0)
        tied = after(d_units, half, q_send)
        first_half = weight_grad(feed_all, tied, first_cut, 2, 1, 0)
        first_half, kv_parts = beside(first_half, kv_parts)
        g_kv = kv_sums[0] + kv_parts[0] + kv_parts[1] + kv_parts[2]
        first_half = first_half + jnp.concatenate(first_parts, axis=0)
        first_last = swap_x(after(first_half[2 * BLOCK :], g_kv))
        down_last = swap_y(after(half[2 * BLOCK :], q_send))
        kv_own, kv_got = line_sends(g_kv, 0)
        g_o = o_keep + after(o_got, first_half, kv_got)
        g_q = q_keep + after(q_got, first_half)
        o_own, o_got = line_sends(g_o, 0)
        q_own, q_got = line_sends(g_q, 1)
        o_got, q_got[:2] = beside(o_got, q_got[:2])
        o_final = line_sum(o_own, o_got)
        first_last, down_last = after((first_last, down_last), o_final)
        second_got = jnp.concatenate(second_last, axis=0)
        g_gate_up = jnp.concatenate(
            [first_half[: 2 * BLOCK] + first_last, second_half[: 2 * BLOCK] + second_got], axis=1
        )
        g_down = half[: 2 * BLOCK] + down_last
    else:
        kv_send = kv_grads[0] + swap_core(kv_grads[1])
        g_o, g_q, g_kv = (fold_whole(v) for v in (o_send, q_send, kv_send))
        kv_own, kv_got = line_sends(g_kv, 0)
        q_own, q_got = line_sends(g_q, 1)
        o_final = line_sum(*line_sends(g_o, 0))
    g_kv = line_sum(kv_own, kv_got).astype(F32)
    grad_output = o_final.astype(F32).T
    grad_query = line_sum(q_own, q_got).astype(F32)
    part_rows = g_down.shape[0] // 2
    g_ffn = jnp.concatenate([g_gate_up, g_down], axis=1)
    g_keep = g_ffn[:part_rows]
    g_take = swap_core(g_ffn[part_rows:])
    grads_ffn = []
    for start in (0, units, units_width):
        kept, got = g_keep[:, start : start + units], g_take[:, start : start + units]
        grads_ffn.append(
            jnp.where(
                core == 0,
                jnp.concatenate([kept, got], axis=1),
                jnp.concatenate([got, kept], axis=1),
            ).astype(F32)
        )
    grad_gate, grad_up, grad_down = grads_ffn
    grad_down = grad_down.T

    grad_key_value = (
        g_kv[:, :KV_WIDTH]
        .reshape(small, KEY_VALUE_HEADS, 2, HEAD_SIZE)
        .transpose(0, 2, 1, 3)
        .reshape(small, KV_WIDTH)
    )

    added = [
        lax.psum_scatter(after(v, last_kv), "heads", scatter_dimension=0, tiled=True) for v in added
    ]
    added = after(added, g_o, g_q)
    layer_out = finish_layer(table, *hiddens, *added)

    return (
        from_order(layer_out).reshape(tokens.shape),
        from_order(tokens_grad).reshape(tokens.shape),
        g_kv[:, KV_WIDTH + ATTENTION_GAIN],
        grad_query,
        grad_key_value,
        g_kv[:per_head, KV_WIDTH + HEAD_GAIN],
        grad_output,
        g_kv[:, KV_WIDTH + FEED_GAIN],
        grad_gate,
        grad_up,
        grad_down,
    )


def order_kernel(table, values, out):
    for j in range(values.shape[1] // BLOCK):
        out[:, span(j)] = values[:, place(table, j)]


def order_columns(table, values):
    return kernel_call(
        order_kernel,
        "order_columns",
        (1,),
        [whole(values)],
        fixed_out(values.shape),
        shape(values.shape, values.dtype),
        [],
        0,
        table,
    )(values)


def solution(mesh):
    every = ("dp", "seq", "heads")
    token_spec = P(None, "dp", ("seq", "heads"), None)
    return jax.shard_map(
        on_device,
        mesh=mesh,
        in_specs=(
            token_spec,
            P(None, "dp", None),
            P(every),
            P(("dp", "seq"), "heads"),
            P(every, None),
            P(every),
            P(None, every),
            P(every),
            P(("dp", "seq"), "heads"),
            P(("dp", "seq"), "heads"),
            P("heads", ("dp", "seq")),
            token_spec,
        ),
        out_specs=(
            token_spec,
            token_spec,
            P(every),
            P(("dp", "seq"), "heads"),
            P(every, None),
            P(every),
            P(None, every),
            P(every),
            P(("dp", "seq"), "heads"),
            P(("dp", "seq"), "heads"),
            P("heads", ("dp", "seq")),
        ),
        check_vma=False,
    )
```

```python
import functools
import math

import jax
import jax.numpy as jnp
from jax import lax
from jax.experimental import pallas as pl
from jax.experimental.pallas import tpu as pltpu
from jax.sharding import PartitionSpec as P

QUERY_HEADS = 28
KEY_VALUE_HEADS = 7
HEAD_SIZE = 64
GROUP = QUERY_HEADS // KEY_VALUE_HEADS
GROUP_WIDTH = GROUP * HEAD_SIZE
Q_WIDTH = QUERY_HEADS * HEAD_SIZE
KV_WIDTH = 2 * KEY_VALUE_HEADS * HEAD_SIZE

EPSILON = 1e-06
SCORE_SCALE = 0.125
MASKED = -1e30
LANES = 128
CHUNK = 256
BLOCK = 256
FFN_ROWS = 256
ATTENTION_GAIN, FEED_GAIN, HEAD_GAIN = 0, 1, 2

BF = jnp.bfloat16
F32 = jnp.float32


def dot_nn(left, right):
    return lax.dot_general(left, right, (((1,), (0,)), ((), ())), preferred_element_type=F32)


def dot_nt(left, right):
    return lax.dot_general(left, right, (((1,), (1,)), ((), ())), preferred_element_type=F32)


def dot_tn(left, right):
    return lax.dot_general(left, right, (((0,), (0,)), ((), ())), preferred_element_type=F32)


def shape(dims, kind):
    return jax.ShapeDtypeStruct(dims, kind)


def whole(array):
    dims = array.shape
    return pl.BlockSpec(
        dims, lambda *unused: (0,) * len(dims), pipeline_mode=pl.Buffered(1)
    )


def fixed_out(dims):
    return pl.BlockSpec(dims, lambda *unused: (0,) * len(dims))


def kernel_call(body, name, grid, in_specs, out_specs, out_shape, scratch, flops, table=None):
    outs = out_shape if isinstance(out_shape, (list, tuple)) else [out_shape]
    moved = sum(math.prod(o.shape) * jnp.dtype(o.dtype).itemsize for o in outs)
    kwargs = dict(
        out_shape=out_shape,
        compiler_params=pltpu.CompilerParams(
            dimension_semantics=("arbitrary",) * len(grid), vmem_limit_bytes=56 * 1024 * 1024
        ),
        name=name,
    )

    def call(*operands):
        size = moved + sum(math.prod(o.shape) * o.dtype.itemsize for o in operands)
        cost = pl.CostEstimate(
            flops=flops,
            bytes_accessed=size,
            transcendentals=0,
        )
        if table is None:
            return pl.pallas_call(
                body,
                grid=grid,
                in_specs=in_specs,
                out_specs=out_specs,
                scratch_shapes=scratch,
                cost_estimate=cost,
                **kwargs,
            )(*operands)
        return pl.pallas_call(
            body,
            grid_spec=pltpu.PrefetchScalarGridSpec(
                num_scalar_prefetch=1,
                grid=grid,
                in_specs=in_specs,
                out_specs=out_specs,
                scratch_shapes=scratch,
            ),
            cost_estimate=cost,
            **kwargs,
        )(table, *operands)

    return call


def half_lanes(rows):
    return lax.broadcasted_iota(jnp.int32, (rows, LANES), 1) < HEAD_SIZE


def half_means(values, low):
    first = jnp.sum(jnp.where(low, values, 0.0), axis=1, keepdims=True) / HEAD_SIZE
    second = jnp.sum(jnp.where(low, 0.0, values), axis=1, keepdims=True) / HEAD_SIZE
    return jnp.where(low, first, second)


def turn(values):
    lane = lax.broadcasted_iota(jnp.int32, values.shape, 1)
    early = (lane & (HEAD_SIZE // 2)) == 0
    return jnp.where(
        early, pltpu.roll(values, LANES - HEAD_SIZE // 2, 1), pltpu.roll(values, HEAD_SIZE // 2, 1)
    )


def head_norm(tile, gain, cosine, sine, low):
    normed = tile * lax.rsqrt(half_means(tile * tile, low) + EPSILON) * gain
    return normed * cosine + turn(normed) * sine


def head_norm_back(tile, gain, cosine, sine, low, grad):
    grad = grad * cosine - turn(grad) * sine
    scale = lax.rsqrt(half_means(tile * tile, low) + EPSILON)
    lifted = grad * gain
    dots = half_means(tile * lifted, low)
    d_tile = scale * lifted - tile * (scale * scale * scale) * dots
    return d_tile, jnp.sum(grad * tile * scale, axis=0, keepdims=True)


def place(table, j):
    return pl.ds(pl.multiple_of(table[j] * BLOCK, BLOCK), BLOCK)


def span(j, size=BLOCK):
    return slice(j * size, (j + 1) * size)


def over_pieces(left, pieces, columns=None):
    total, start = None, 0
    for piece in pieces:
        size = piece.shape[0]
        right = piece[...] if columns is None else piece[:, columns]
        term = dot_nn(left[:, start : start + size], right)
        total = term if total is None else total + term
        start += size
    return total


def add_back(target, left, pieces, columns=None):
    start = 0
    for piece in pieces:
        size = piece.shape[0]
        right = piece[...] if columns is None else piece[:, columns]
        target[:, start : start + size] += dot_nt(left, right)
        start += size


def key_value_kernel(table, tokens, cosine, sine, gain, *refs):
    kvg = refs[:-4]
    normed, kv_raw, kv_low, gains = refs[-4:]
    rows, width = tokens.shape
    count = width // BLOCK
    columns = jnp.concatenate([part[:, KV_WIDTH:].astype(F32).T for part in kvg], axis=1)
    gains[...] = columns[:8]
    squares = 0.0
    for j in range(count):
        block = tokens[:, place(table, j)].astype(F32)
        squares = squares + jnp.sum(block * block, axis=1, keepdims=True)
    scale = lax.rsqrt(squares / width + EPSILON)
    for j in range(count):
        block = tokens[:, place(table, j)].astype(F32)
        normed[:, span(j)] = (
            block * scale * columns[ATTENTION_GAIN : ATTENTION_GAIN + 1, span(j)]
        ).astype(BF)
    raw = over_pieces(normed, kvg, slice(0, KV_WIDTH))
    kv_raw[...] = raw
    low = half_lanes(rows)
    for c in range(KEY_VALUE_HEADS):
        tile = raw[:, span(c, LANES)]
        key = head_norm(tile, gain[...], cosine[...], sine[...], low)
        kv_low[:, span(c, LANES)] = jnp.where(low, key, tile).astype(BF)


def project_key_value(table, tokens, cosine, sine, gain, kvg):
    rows, width = tokens.shape
    operands = (tokens, cosine, sine, gain, *kvg)
    return kernel_call(
        key_value_kernel,
        "project_key_value",
        (1,),
        [whole(o) for o in operands],
        [
            fixed_out((rows, width)),
            fixed_out((rows, KV_WIDTH)),
            fixed_out((rows, KV_WIDTH)),
            fixed_out((8, width)),
        ],
        [
            shape((rows, width), BF),
            shape((rows, KV_WIDTH), F32),
            shape((rows, KV_WIDTH), BF),
            shape((8, width), F32),
        ],
        [],
        2 * rows * width * KV_WIDTH,
        table,
    )(*operands)


def query_kernel(normed, cosine, sine, gain, *refs):
    q_raw, queries = refs[-2:]
    rows = normed.shape[0]
    raw = over_pieces(normed, refs[:-2])
    q_raw[...] = raw
    low = half_lanes(rows)
    for tile_index in range(GROUP_WIDTH // LANES):
        tile = raw[:, span(tile_index, LANES)]
        turned = head_norm(tile, gain[...], cosine[...], sine[...], low)
        queries[:, span(tile_index, LANES)] = (turned * SCORE_SCALE).astype(BF)


def column_parts(pieces):
    return [pl.BlockSpec((piece.shape[0], GROUP_WIDTH), lambda c, *t: (0, c)) for piece in pieces]


def project_query(normed, cosine, sine, gain, weight):
    rows, width = normed.shape
    out = pl.BlockSpec((rows, GROUP_WIDTH), lambda c: (0, c))
    return kernel_call(
        query_kernel,
        "project_query",
        (KEY_VALUE_HEADS,),
        [whole(normed), whole(cosine), whole(sine), whole(gain), *column_parts(weight)],
        [out, out],
        [shape((rows, Q_WIDTH), F32), shape((rows, Q_WIDTH), BF)],
        [],
        2 * rows * width * Q_WIDTH,
    )(normed, cosine, sine, gain, *weight)


def output_kernel(table, mixed, tokens, gains, *refs):
    hidden, feed = refs[-2:]
    width = hidden.shape[1]
    step = pl.program_id(0)

    @pl.when(step == 0)
    def _():
        for j in range(width // BLOCK):
            hidden[:, span(j)] = tokens[:, place(table, j)].astype(F32)

    add_back(hidden, mixed[...], refs[:-2])

    @pl.when(step == pl.num_programs(0) - 1)
    def _():
        values = hidden[...]
        scale = lax.rsqrt(jnp.mean(values * values, axis=1, keepdims=True) + EPSILON)
        feed[...] = (values * scale * gains[FEED_GAIN : FEED_GAIN + 1, :]).astype(BF)


def project_output(table, mixed, tokens, batch, gains, weight):
    rows = mixed.shape[0]
    width = tokens.shape[1]
    return kernel_call(
        output_kernel,
        "project_output",
        (KEY_VALUE_HEADS,),
        [
            pl.BlockSpec((rows, GROUP_WIDTH), lambda c, t: (0, c)),
            pl.BlockSpec((rows, width), lambda c, t: (batch, 0)),
            whole(gains),
            *column_parts(weight),
        ],
        [fixed_out((rows, width)), fixed_out((rows, width))],
        [shape((rows, width), F32), shape((rows, width), BF)],
        [],
        2 * rows * width * Q_WIDTH,
        table,
    )(mixed, tokens, gains, *weight)


def hidden_back_kernel(table, d_feed, hidden, cot, gains, *refs):
    d_hidden, d_attended, gain_grad, d_mixed = refs[-4:]
    width = hidden.shape[1]

    @pl.when(pl.program_id(0) == 0)
    def _():
        values = hidden[...]
        grad = d_feed[...].astype(F32)
        scale = lax.rsqrt(jnp.mean(values * values, axis=1, keepdims=True) + EPSILON)
        lifted = grad * gains[FEED_GAIN : FEED_GAIN + 1, :]
        dots = jnp.mean(values * lifted, axis=1, keepdims=True)
        d_norm = scale * lifted - values * (scale * scale * scale) * dots
        gain_grad[...] = jnp.broadcast_to(
            jnp.sum(grad * values * scale, axis=0, keepdims=True), gain_grad.shape
        )
        for j in range(width // BLOCK):
            total = cot[:, place(table, j)].astype(F32) + d_norm[:, span(j)]
            d_hidden[:, span(j)] = total
            d_attended[:, span(j)] = total.astype(BF)

    d_mixed[...] = over_pieces(d_attended, refs[:-4]).astype(BF)


def hidden_back(table, d_feed, hidden, cot, batch, gains, weight):
    rows, width = hidden.shape
    return kernel_call(
        hidden_back_kernel,
        "hidden_back",
        (KEY_VALUE_HEADS,),
        [
            whole(d_feed),
            whole(hidden),
            pl.BlockSpec((rows, width), lambda c, t: (batch, 0)),
            whole(gains),
            *column_parts(weight),
        ],
        [
            fixed_out((rows, width)),
            fixed_out((rows, width)),
            fixed_out((8, width)),
            pl.BlockSpec((rows, GROUP_WIDTH), lambda c, t: (0, c)),
        ],
        [
            shape((rows, width), F32),
            shape((rows, width), BF),
            shape((8, width), F32),
            shape((rows, Q_WIDTH), BF),
        ],
        [],
        2 * rows * width * Q_WIDTH,
        table,
    )(d_feed, hidden, cot, gains, *weight)


def query_back_kernel(d_q, *refs):
    out = refs[-1]

    @pl.when(pl.program_id(0) == 0)
    def _():
        out[...] = jnp.zeros_like(out)

    add_back(out, d_q[...], refs[:-1])


def query_back(d_q, weight):
    rows = d_q.shape[0]
    width = sum(piece.shape[0] for piece in weight)
    return kernel_call(
        query_back_kernel,
        "query_back",
        (KEY_VALUE_HEADS,),
        [pl.BlockSpec((rows, GROUP_WIDTH), lambda c: (0, c)), *column_parts(weight)],
        fixed_out((rows, width)),
        shape((rows, width), F32),
        [],
        2 * rows * width * Q_WIDTH,
    )(d_q, *weight)


def input_back_kernel(
    table,
    d_pair,
    kv_raw,
    cosine,
    sine,
    gain,
    d_normed_q,
    d_hidden0,
    d_hidden1,
    tokens,
    gains,
    *refs,
):
    kvg = refs[:-5]
    d_kv_raw, head_grad, tokens_grad, gain_grad, d_normed = refs[-5:]
    rows, width = tokens.shape
    part = d_hidden0.shape[0]
    low = half_lanes(rows)
    total = 0.0
    for c in range(KEY_VALUE_HEADS):
        grad = d_pair[:, span(c, LANES)].astype(F32)
        d_tile, g_tile = head_norm_back(
            kv_raw[:, span(c, LANES)], gain[...], cosine[...], sine[...], low, grad
        )
        total = total + g_tile
        d_kv_raw[:, span(c, LANES)] = jnp.where(low, d_tile, grad).astype(BF)
    head_grad[...] = jnp.broadcast_to(total, head_grad.shape)
    d_kv = d_kv_raw[...]
    d_normed[...] = d_normed_q[...]
    add_back(d_normed, d_kv, kvg, slice(0, KV_WIDTH))
    squares, dots = 0.0, 0.0
    for j in range(width // BLOCK):
        block = tokens[:, place(table, j)].astype(F32)
        lifted = d_normed[:, span(j)] * gains[ATTENTION_GAIN : ATTENTION_GAIN + 1, span(j)]
        squares = squares + jnp.sum(block * block, axis=1, keepdims=True)
        dots = dots + jnp.sum(block * lifted, axis=1, keepdims=True)
    scale = lax.rsqrt(squares / width + EPSILON)
    dots = dots / width * (scale * scale * scale)
    for j in range(width // BLOCK):
        block = tokens[:, place(table, j)].astype(F32)
        grad = d_normed[:, span(j)]
        lifted = grad * gains[ATTENTION_GAIN : ATTENTION_GAIN + 1, span(j)]
        d_input = scale * lifted - block * dots
        for batch, d_hidden in enumerate((d_hidden0, d_hidden1)):
            tokens_grad[span(batch, part), place(table, j)] = (
                d_hidden[:, span(j)] + d_input[span(batch, part), :]
            )
        gain_grad[:, span(j)] = jnp.broadcast_to(
            jnp.sum(grad * block * scale, axis=0, keepdims=True), (8, BLOCK)
        )


def input_back(table, *operands):
    tokens = operands[8]
    rows, width = tokens.shape
    return kernel_call(
        input_back_kernel,
        "input_back",
        (1,),
        [whole(o) for o in operands],
        [
            fixed_out((rows, KV_WIDTH)),
            fixed_out((8, LANES)),
            fixed_out((rows, width)),
            fixed_out((8, width)),
        ],
        [
            shape((rows, KV_WIDTH), BF),
            shape((8, LANES), F32),
            shape((rows, width), F32),
            shape((8, width), F32),
        ],
        [pltpu.VMEM((rows, width), F32)],
        2 * rows * width * KV_WIDTH,
        table,
    )(*operands)


def layer_out_kernel(table, hidden0, hidden1, added0, added1, out):
    part = hidden0.shape[0]
    for batch, (hidden, added) in enumerate(((hidden0, added0), (hidden1, added1))):
        for j in range(hidden.shape[1] // BLOCK):
            out[span(batch, part), place(table, j)] = (
                hidden[:, span(j)] + added[:, span(j)].astype(F32)
            ).astype(BF)


def finish_layer(table, *operands):
    rows, width = operands[0].shape
    return kernel_call(
        layer_out_kernel,
        "finish_layer",
        (1,),
        [whole(o) for o in operands],
        fixed_out((2 * rows, width)),
        shape((2 * rows, width), BF),
        [],
        0,
        table,
    )(*operands)


def key_value_grad_kernel(normed, d_kv_raw, gain_grads, out0, out1):
    half = normed.shape[1] // 2
    for index, out in enumerate((out0, out1)):
        cut = span(index, half)
        out[:, :KV_WIDTH] = dot_tn(normed[:, cut], d_kv_raw[...]).astype(BF)
        rows = gain_grads[:, cut]
        rows = jnp.concatenate([rows, jnp.zeros((LANES - 8, half), F32)], axis=0)
        out[:, KV_WIDTH:] = rows.T.astype(BF)


def key_value_grad(normed, d_kv_raw, gain_grads):
    rows, width = normed.shape
    dims = (width // 2, KV_WIDTH + LANES)
    return kernel_call(
        key_value_grad_kernel,
        "key_value_grad",
        (1,),
        [whole(normed), whole(d_kv_raw), whole(gain_grads)],
        [fixed_out(dims), fixed_out(dims)],
        [shape(dims, BF), shape(dims, BF)],
        [],
        2 * rows * width * KV_WIDTH,
    )(normed, d_kv_raw, gain_grads)


def pad_heads(tile, low, keep_low):
    parts = []
    for pair in range(GROUP // 2):
        both = tile[:, span(pair, LANES)].astype(F32)
        turned = pltpu.roll(both, HEAD_SIZE, 1)
        first, second = (both, turned) if keep_low else (turned, both)
        keep = low if keep_low else jnp.logical_not(low)
        parts.append(jnp.where(keep, first, 0.0))
        parts.append(jnp.where(keep, second, 0.0))
    return jnp.concatenate(parts, axis=0).astype(BF)


def four_wide(row):
    return jnp.concatenate([row] * GROUP, axis=1)


def heads_back(stacked, rows):
    parts = []
    for pair in range(GROUP // 2):
        start = 2 * pair * rows
        both = jnp.concatenate(
            [stacked[:, start : start + rows], stacked[:, start + rows : start + 2 * rows]], axis=0
        )
        parts.append(both.T)
    return jnp.concatenate(parts, axis=1)


def key_rows(kv, cut):
    rows = kv.shape[2]
    block = kv[cut.start // rows : cut.stop // rows, 0]
    return block.reshape(cut.stop - cut.start, kv.shape[3])


def every_row(kv):
    return key_rows(kv, slice(0, kv.shape[0] * kv.shape[2]))


def ones_and_values(kv):
    values = every_row(kv)
    return jnp.where(half_lanes(values.shape[0]), 1.0, values.astype(F32)).astype(BF)


def attention_forward_kernel(kv0, kv1, query, bias0, bias1, mixed, lse, expo):
    rows = query.shape[0]
    half = bias0.shape[0]
    padded = pad_heads(query[...], half_lanes(rows), True)
    for part, (kv, bias) in enumerate(((kv0, bias0), (kv1, bias1))):
        for step in range(half // CHUNK):
            cut = span(step, CHUNK)
            weight = jnp.exp(dot_nt(key_rows(kv, cut), padded) + four_wide(bias[cut, :]))
            expo[part * half + step * CHUNK : part * half + (step + 1) * CHUNK, :] = weight.astype(BF)
    total = dot_tn(ones_and_values(kv0), expo[:half, :]) + dot_tn(
        ones_and_values(kv1), expo[half:, :]
    )
    lse[...] = jnp.log(total[0:1, :])[None]
    mixed[...] = heads_back(total[HEAD_SIZE:, :] / total[:HEAD_SIZE, :], rows).astype(BF)


def attention_forward(kv0, kv1, query, batch, bias0, bias1):
    half, rows = bias0.shape
    wide = GROUP * rows
    keys = pl.BlockSpec((half // rows, 1, rows, LANES), lambda c: (0, 0, 0, c))
    kv0, kv1 = (kv.reshape(half // rows, -1, rows, KV_WIDTH) for kv in (kv0, kv1))
    return kernel_call(
        attention_forward_kernel,
        "attention_forward",
        (KEY_VALUE_HEADS,),
        [
            keys,
            keys,
            pl.BlockSpec((rows, GROUP_WIDTH), lambda c: (batch, c)),
            whole(bias0),
            whole(bias1),
        ],
        [
            pl.BlockSpec((rows, GROUP_WIDTH), lambda c: (0, c)),
            pl.BlockSpec((1, 1, wide), lambda c: (c, 0, 0)),
        ],
        [shape((rows, Q_WIDTH), BF), shape((KEY_VALUE_HEADS, 1, wide), F32)],
        [pltpu.VMEM((2 * half, wide), BF)],
        KEY_VALUE_HEADS * 2 * half * wide * LANES * 12,
    )(kv0, kv1, query, bias0, bias1)


def attention_backward_kernel(
    kv0,
    kv1,
    query,
    mixed,
    d_mixed,
    bias0,
    bias1,
    lse,
    q_raw,
    cosine,
    sine,
    gain,
    d_q_raw,
    d_kv0,
    d_kv1,
    gain_grad,
    d_scores,
):
    rows = query.shape[0]
    half = bias0.shape[0]
    low = half_lanes(rows)
    padded = pad_heads(query[...], low, True)
    d_padded = pad_heads(d_mixed[...], low, False)
    product = d_mixed[...].astype(F32) * mixed[...].astype(F32)
    pick = (
        lax.broadcasted_iota(jnp.int32, (8, GROUP_WIDTH), 1) // HEAD_SIZE
        == lax.broadcasted_iota(jnp.int32, (8, GROUP_WIDTH), 0)
    ).astype(F32)
    balance = lax.dot_general(
        pick,
        product,
        (((1,), (1,)), ((), ())),
        precision=lax.Precision.HIGHEST,
        preferred_element_type=F32,
    )
    balance = jnp.concatenate([balance[head : head + 1, :] for head in range(GROUP)], axis=1)
    level = lse[0]
    for part, (kv, bias, d_kv) in enumerate(((kv0, bias0, d_kv0), (kv1, bias1, d_kv1))):
        for step in range(half // CHUNK):
            cut = span(step, CHUNK)
            block = key_rows(kv, cut)
            probs = jnp.exp(dot_nt(block, padded) + four_wide(bias[cut, :]) - level)
            d_probs = dot_nt(block, d_padded)
            low_scores = (probs * (d_probs - balance)).astype(BF)
            d_scores[part * half + step * CHUNK : part * half + (step + 1) * CHUNK, :] = low_scores
            d_kv[cut, :] = (
                dot_nn(low_scores, padded) + dot_nn(probs.astype(BF), d_padded)
            ).astype(BF)
    total = dot_tn(every_row(kv0), d_scores[:half, :]) + dot_tn(
        every_row(kv1), d_scores[half:, :]
    )
    d_query = heads_back(total[:HEAD_SIZE, :] * SCORE_SCALE, rows)
    grads = 0.0
    for tile_index in range(GROUP_WIDTH // LANES):
        cut = span(tile_index, LANES)
        d_tile, g_tile = head_norm_back(
            q_raw[:, cut], gain[...], cosine[...], sine[...], low, d_query[:, cut]
        )
        d_q_raw[:, cut] = d_tile.astype(BF)
        grads = grads + g_tile

    @pl.when(pl.program_id(0) == 0)
    def _():
        gain_grad[...] = jnp.zeros_like(gain_grad)

    gain_grad[...] += jnp.broadcast_to(grads, gain_grad.shape)


def attention_backward(
    kv0, kv1, query, batch, mixed, d_mixed, bias0, bias1, lse, q_raw, cosine, sine, gain
):
    half, rows = bias0.shape
    wide = GROUP * rows
    keys = pl.BlockSpec((half // rows, 1, rows, LANES), lambda c: (0, 0, 0, c))
    kv0, kv1 = (kv.reshape(half // rows, -1, rows, KV_WIDTH) for kv in (kv0, kv1))
    d_keys = pl.BlockSpec((half, LANES), lambda c: (0, c))
    heads = pl.BlockSpec((rows, GROUP_WIDTH), lambda c: (0, c))
    part = pl.BlockSpec((rows, GROUP_WIDTH), lambda c: (batch, c))
    table = pl.BlockSpec((rows, LANES), lambda c: (batch, 0))
    return kernel_call(
        attention_backward_kernel,
        "attention_backward",
        (KEY_VALUE_HEADS,),
        [
            keys,
            keys,
            part,
            heads,
            heads,
            whole(bias0),
            whole(bias1),
            pl.BlockSpec((1, 1, wide), lambda c: (c, 0, 0)),
            part,
            table,
            table,
            whole(gain),
        ],
        [heads, d_keys, d_keys, fixed_out((8, LANES))],
        [
            shape((rows, Q_WIDTH), BF),
            shape((half, KV_WIDTH), BF),
            shape((half, KV_WIDTH), BF),
            shape((8, LANES), F32),
        ],
        [pltpu.VMEM((2 * half, wide), BF)],
        KEY_VALUE_HEADS * 2 * half * wide * LANES * 28,
    )(kv0, kv1, query, mixed, d_mixed, bias0, bias1, lse, q_raw, cosine, sine, gain)


def swap_halves(values):
    half = values.shape[1] // 2
    return jnp.concatenate([values[:, half:], values[:, :half]], axis=1)


def feed_forward_kernel(count, units, *refs):
    feed0, feed1, cot0, cot1 = refs[:4]
    gate_up = refs[4 : 4 + count]
    down = refs[4 + count : 4 + 2 * count]
    act_out, d_units_out, out0, out1, d_feed0, d_feed1 = refs[4 + 2 * count :]
    first = pl.program_id(0) < pl.num_programs(0) // 2
    rows, width = feed0.shape
    half = width // 2
    size = down[0].shape[0] // 2
    feed = jnp.where(first, swap_halves(feed0[...]), feed1[...])
    cot = jnp.where(first, swap_halves(cot0[...]), cot1[...])

    def over(left, pieces):
        total = None
        for b, piece in enumerate(pieces):
            both = jnp.concatenate(
                [left[:, b * size : (b + 1) * size], left[:, half + b * size : half + (b + 1) * size]],
                axis=1,
            )
            term = dot_nn(both, piece[...])
            total = term if total is None else total + term
        return total

    both = over(feed, gate_up)
    gate_pre, up_pre = both[:, :units], both[:, units : 2 * units]
    sig = 1.0 / (1.0 + jnp.exp(-gate_pre))
    silu = gate_pre * sig
    act = (silu * up_pre).astype(BF)
    act = jnp.concatenate([act, jnp.zeros((rows, down[0].shape[1] - units), BF)], axis=1)
    act_out[...] = act
    d_act = over(cot, down)[:, :units]
    d_gate = d_act * up_pre * (sig * (1.0 + gate_pre * (1.0 - sig)))
    d_units = jnp.concatenate(
        [
            d_gate.astype(BF),
            (d_act * silu).astype(BF),
            jnp.zeros((rows, gate_up[0].shape[1] - 2 * units), BF),
        ],
        axis=1,
    )
    d_units_out[...] = d_units

    def write(target, left, pieces, swapped):
        for b, piece in enumerate(pieces):
            block = dot_nt(left, piece[...]).astype(BF)
            early, late = (half, 0) if swapped else (0, half)
            target[:, early + b * size : early + (b + 1) * size] = block[:, :size]
            target[:, late + b * size : late + (b + 1) * size] = block[:, size:]

    @pl.when(first)
    def _():
        write(d_feed0, d_units, gate_up, True)
        write(out0, act, down, True)

    @pl.when(jnp.logical_not(first))
    def _():
        write(d_feed1, d_units, gate_up, False)
        write(out1, act, down, False)


def feed_forward(feeds, cots, gate_up, down, units):
    tokens, width = feeds[0].shape
    steps = tokens // FFN_ROWS
    early = pl.BlockSpec((FFN_ROWS, width), lambda i: (jnp.minimum(i, steps - 1), 0))
    late = pl.BlockSpec((FFN_ROWS, width), lambda i: (jnp.maximum(i - steps, 0), 0))
    act_width, units_width = down[0].shape[1], gate_up[0].shape[1]
    return kernel_call(
        functools.partial(feed_forward_kernel, len(down), units),
        "feed_forward",
        (2 * steps,),
        [early, late, early, late, *[whole(w) for w in (*gate_up, *down)]],
        [
            pl.BlockSpec((FFN_ROWS, act_width), lambda i: (i, 0)),
            pl.BlockSpec((FFN_ROWS, units_width), lambda i: (i, 0)),
            early,
            late,
            early,
            late,
        ],
        [
            shape((2 * tokens, act_width), BF),
            shape((2 * tokens, units_width), BF),
            *[shape((tokens, width), BF)] * 4,
        ],
        [],
        2 * tokens * 2 * width * units * 6,
    )(*feeds, *cots, *gate_up, *down)


def weight_grad_kernel(count, columns, *refs):
    lefts = refs[: 2 * count]
    rights = refs[2 * count : -1]
    out = refs[-1]
    rows = lefts[0].shape[0]
    each = count // len(rights)
    total = None
    for index in range(count):
        left = jnp.concatenate([lefts[2 * index][...], lefts[2 * index + 1][...]], axis=1)
        right = rights[index // each]
        term = dot_tn(left, right[span(index % each, rows), columns])
        total = term if total is None else total + term
    out[...] = total.astype(BF)


def weight_grad(lefts, rights, columns, steps, stride, offset):
    rows, width = lefts[0].shape
    units = columns.stop - columns.start
    half = width // 2 // BLOCK
    mine = pl.BlockSpec((rows, BLOCK), lambda i: (0, i * stride + offset))
    other = pl.BlockSpec((rows, BLOCK), lambda i: (0, half + i * stride + offset))
    specs, operands = [], []
    for index, left in enumerate(lefts):
        specs += [other, mine] if index % 2 == 0 else [mine, other]
        operands += [left, left]
    return kernel_call(
        functools.partial(weight_grad_kernel, len(lefts), columns),
        "weight_grad",
        (steps,),
        [*specs, *[whole(r) for r in rights]],
        pl.BlockSpec((2 * BLOCK, units), lambda i: (i, 0)),
        shape((2 * BLOCK * steps, units), BF),
        [],
        2 * len(lefts) * rows * 2 * BLOCK * steps * units,
    )(*operands, *rights)


def rotary_tables(places):
    half_width = HEAD_SIZE // 2
    freqs = jnp.exp(jnp.arange(half_width, dtype=F32) * (-2.0 * math.log(10000.0) / HEAD_SIZE))
    angles = places.astype(F32)[:, None] * freqs[None, :]
    cosine, sine = jnp.cos(angles), jnp.sin(angles)
    return (
        jnp.concatenate([cosine] * 4, axis=1),
        jnp.concatenate([-sine, sine, -sine, sine], axis=1),
    )


def padded_columns(values, columns):
    return jnp.pad(values, ((0, 0), (0, columns - values.shape[1])))


def up_to(size):
    return -(-size // LANES) * LANES


def on_device(
    tokens,
    lengths,
    attention_gain,
    query_weight,
    key_value_matrix,
    per_head_gains,
    output_weight,
    feed_gain,
    gate_weight,
    up_weight,
    down_weight,
    cotangent,
):
    batches = tokens.shape[0]
    rows = tokens.shape[2]
    width = tokens.shape[3]
    dp_size = lax.axis_size("dp")
    heads_size = lax.axis_size("heads")
    seq_size = lax.axis_size("seq")
    assert seq_size == 4 and heads_size == 4 and batches == 2
    paired = dp_size == 2
    y = lax.axis_index("dp").astype(jnp.int32)
    s = lax.axis_index("seq").astype(jnp.int32)
    z = lax.axis_index("heads").astype(jnp.int32)
    x = s // 2
    core = s % 2

    def after(v, *others):
        return lax.optimization_barrier((v, others))[0]

    def beside(outs, parts):
        return lax.optimization_barrier((outs, parts))

    def swap_x(v):
        return lax.ppermute(v, "seq", [(i, i ^ 2) for i in range(4)])

    def swap_xy(v):
        return lax.ppermute(v, ("dp", "seq"), [(i, i ^ 6) for i in range(8)])

    def swap_core(v):
        return lax.ppermute(v, "seq", [(i, i ^ 1) for i in range(4)])

    def swap_y(v):
        return lax.ppermute(v, "dp", [(0, 1), (1, 0)])

    def line_sends(v, axis):
        cut = jnp.split(v, 4, axis=axis)
        got = []
        for k in range(1, 4):
            block = lax.select_n(z, *[cut[i ^ k] for i in range(4)])
            got.append(lax.ppermute(block, "heads", [(i, i ^ k) for i in range(4)]))
        return lax.select_n(z, *cut), got

    def line_sum(own_block, got):
        return own_block + got[0] + got[1] + got[2]

    def gather_near(v):
        if not paired:
            both = jnp.stack([v, swap_x(v)], axis=0)
            return [lax.all_gather(both, "dp", axis=0).reshape(-1, v.shape[-1])]
        return [v, swap_x(v), swap_y(v)]

    def gather_far(near, x_first):
        if not paired:
            return near
        return [*near, swap_y(near[1]) if x_first else swap_x(near[2])]

    def pair_gather(v, axis):
        def step(u, upper, distance):
            got = lax.ppermute(u, "heads", [(i, i ^ distance) for i in range(4)])
            return jnp.where(
                upper,
                jnp.concatenate([got, u], axis=axis),
                jnp.concatenate([u, got], axis=axis),
            )

        return step(step(v, z % 2 == 1, 1), z >= 2, 2)

    def both_cores(pieces):
        return [*pieces, *[swap_core(v) for v in pieces]]

    def unit_pieces(pieces):
        if paired:
            return pieces
        g = pieces[0].reshape(blocks, 2, -1, pieces[0].shape[-1])
        return [g.transpose(1, 0, 2, 3).reshape(pieces[0].shape)]

    def scatter_yx(g, x_last, first=(), second=()):
        def along_x(u, late):
            return u[..., 0, :, :] + after(swap_x(u[..., 1, :, :]), late)

        def along_y(u, late):
            if paired:
                return u[0] + after(swap_y(u[1]), late)
            return lax.psum_scatter(u, "dp", scatter_dimension=0)

        if x_last:
            return along_x(along_y(g, first), second)
        return along_y(along_x(g, first), second)

    blocks = 2 * dp_size
    piece = width // blocks

    if paired:
        own = (2 * y + x) * 2 + core
        places_of = jnp.array([b * 2 + c for c in range(2) for b in range(4)], jnp.int32)
        table = places_of ^ own

        def to_order(v):
            return v

        from_order = to_order
    else:
        table = jnp.arange(width // BLOCK, dtype=jnp.int32)

        def flip(v):
            u = v.reshape(v.shape[:-1] + (dp_size, 2, 2, piece // 2))
            u = jnp.where(x == 1, u[..., ::-1, :, :], u)
            return jnp.where(core == 1, u[..., ::-1, :], u)

        def to_order(v):
            return jnp.moveaxis(flip(v), -2, -4).reshape(v.shape)

        def from_order(v):
            u = v.reshape(v.shape[:-1] + (2, dp_size, 2, piece // 2))
            return flip(jnp.moveaxis(u, -4, -2).reshape(v.shape)).reshape(v.shape)

    def small_order(v, back):
        if not paired:
            return from_order(v) if back else to_order(v)
        cut = v.reshape(8, -1)
        return jnp.concatenate(
            [
                lax.select_n(own, *[cut[held(i, m, back)] for m in range(8)])
                for i in range(8)
            ]
        ).reshape(v.shape)

    def held(i, m, back):
        if back:
            source = i ^ m
            return (source % 2) * 4 + source // 2
        return ((i % 4) * 2 + i // 4) ^ m

    small = key_value_matrix.shape[0]
    per_head = per_head_gains.shape[0]
    kv_local = (
        key_value_matrix.reshape(small, 2, KEY_VALUE_HEADS, HEAD_SIZE)
        .transpose(0, 2, 1, 3)
        .reshape(small, KV_WIDTH)
    )
    gains_local = jnp.stack(
        [attention_gain, feed_gain, jnp.pad(per_head_gains, (0, small - per_head))], axis=1
    )
    kvg_local = jnp.concatenate([kv_local, padded_columns(gains_local, LANES)], axis=1)
    kvg_rows = pair_gather(kvg_local, 0)
    kvg_near = gather_near(kvg_rows)

    tokens_in = to_order(tokens[:, 0].reshape(batches * rows, width))
    cot_in = to_order(cotangent[:, 0].reshape(batches * rows, width))
    cot_held = order_columns(table, cot_in) if paired else cot_in
    projections = lax.all_gather(
        jnp.concatenate([query_weight.reshape(small, Q_WIDTH), output_weight.T], axis=0),
        "heads",
        axis=0,
    )
    q_rows = (
        projections[:, :small]
        .reshape(heads_size, query_weight.shape[0], query_weight.shape[1])
        .transpose(1, 0, 2)
        .reshape(query_weight.shape[0], Q_WIDTH)
    )
    o_rows = projections[:, small:].reshape(4 * small, Q_WIDTH)
    lined = lax.all_gather(cot_held, "heads", axis=0)
    cots_mine = [
        lined[:, span(batch, rows)].reshape(heads_size * rows, width) for batch in range(batches)
    ]

    units = gate_weight.shape[1] // 2
    act_width, units_width = up_to(units), up_to(2 * units)

    def unit_half(v, which):
        return jnp.where(which == 0, v[:, :units], v[:, units:])

    down_local = down_weight.T

    def halves(which):
        gate_up = jnp.concatenate([unit_half(gate_weight, which), unit_half(up_weight, which)], axis=1)
        return jnp.concatenate(
            [padded_columns(gate_up, units_width), padded_columns(unit_half(down_local, which), act_width)],
            axis=1,
        )

    keep = halves(core)
    take = swap_core(halves(1 - core))
    ffn_rows = jnp.concatenate([keep, take], axis=0)
    down_near = gather_near(ffn_rows[:, units_width:])
    gate_up_near = gather_near(after(ffn_rows[:, :units_width], kvg_near))
    gate_up = unit_pieces(gather_far(gate_up_near, True))
    kvg = both_cores(gather_far(after(kvg_near, down_near), True))

    head_column = jnp.concatenate([part[:, KV_WIDTH + HEAD_GAIN] for part in kvg])
    head_scale = small_order(head_column.astype(F32)[None], True)
    head_scale = head_scale.reshape(-1, small)[:, :per_head].reshape(1, -1)
    query_gain = jnp.concatenate([head_scale[:, :HEAD_SIZE]] * 2, axis=1)
    key_gain = jnp.concatenate([head_scale[:, HEAD_SIZE:]] * 2, axis=1)

    block_rows = rows * heads_size
    spots = s * block_rows + z * rows + jnp.arange(rows, dtype=jnp.int32)
    inside = jnp.arange(rows, dtype=jnp.int32)

    def key_spots(first):
        lines = jnp.arange(heads_size, dtype=jnp.int32)[:, None, None] * rows
        fronts = jnp.stack([first, first ^ 2])[None, :, None] * block_rows
        return (lines + fronts + inside[None, None, :]).reshape(-1)

    def bias_for(begin, first):
        keys = key_spots(first)[:, None]
        return jnp.where((keys <= spots[None, :]) & (keys >= begin[None, :]), 0.0, MASKED)

    begins, biases = [], []
    for batch in range(batches):
        sizes = lengths[batch, 0]
        finish = jnp.cumsum(sizes)
        begin = jnp.sum(
            jnp.where(spots[:, None] >= finish[None, :], sizes[None, :], 0), axis=1
        ).astype(jnp.int32)
        begins.append(begin)
        biases.append((bias_for(begin, s), bias_for(begin, s ^ 1)))
    cosine, sine = rotary_tables(jnp.concatenate([spots - begin for begin in begins]))

    normed, kv_raw, kv_low, gains = project_key_value(
        table, after(tokens_in, down_near), cosine, sine, key_gain, kvg
    )
    kv_got = swap_x(kv_low)
    kv_lined = []
    for batch in range(batches):
        cut = span(batch, rows)
        pair = jnp.concatenate([kv_low[cut], kv_got[cut]], axis=0)
        if batch == 0:
            pair = after(pair, gate_up_near, lined)
        kv_lined.append(lax.all_gather(pair, "heads", axis=0, tiled=True))
    down = unit_pieces(gather_far(down_near, False))
    q_near = gather_near(q_rows)
    q_full = both_cores(gather_far(after(q_near, kv_got), False))
    o_near = gather_near(after(o_rows, q_near))
    q_raw, queries = project_query(after(normed, kv_lined[0]), cosine, sine, query_gain, q_full)
    o_pieces = gather_far(after(o_near, queries), True)
    kv_lined[0] = after(kv_lined[0], queries, o_near)
    kvs = [(v, swap_core(v)) for v in kv_lined]

    feeds, mixeds, lses, hiddens = [], [], [], []
    for batch in range(batches):
        query = queries if batch == 0 else after(queries, hiddens[0])
        mixed, lse = attention_forward(*kvs[batch], query, batch, *biases[batch])
        if batch == 0:
            o_full = both_cores(after(o_pieces, mixed))
        else:
            (mixed, lse), (gate_up, down) = beside((mixed, lse), (gate_up, down))
        hidden_in, feed_rows = project_output(
            table, mixed, tokens_in, batch, gains, o_full
        )
        feeds.append(lax.all_gather(feed_rows, "heads", axis=0, tiled=True))
        mixeds.append(mixed)
        lses.append(lse)
        hiddens.append(hidden_in)

    feeds[0] = after(feeds[0], feed_rows)
    feeds = [(swap_core(v), v) for v in feeds]

    d_feeds, acts, d_units, cots = [], [], [], []
    added = []
    for batch in range(batches):
        if batch == 1:
            feeds[1] = after(feeds[1], added[0])
        cot_pair = (swap_core(cots_mine[batch]), cots_mine[batch])
        act, d_unit, out_other, out_mine, d_feed_other, d_feed_mine = feed_forward(
            feeds[batch], cot_pair, gate_up, down, units
        )
        acts.append(act)
        d_units.append(d_unit)
        cots.append(cot_pair)
        added.append(out_mine + swap_core(out_other))
        d_feed = d_feed_mine + swap_core(d_feed_other)
        if batch + 1 < batches:
            d_feed = after(d_feed, feeds[batch + 1])
        d_feeds.append(lax.psum_scatter(d_feed, "heads", scatter_dimension=0, tiled=True))

    feed_all = [f for pair in feeds for f in pair]
    cot_all = [c for pair in cots for c in pair]
    count = width // 2 // BLOCK

    def unit_order(g):
        g = g.reshape(count, 2, BLOCK, -1).transpose(1, 0, 2, 3)
        g = g.reshape(2, blocks, piece // 2, -1).transpose(1, 0, 2, 3)
        return g.reshape(dp_size, 2, piece, -1)

    cut_at = up_to(units)

    def both_grads(left, right):
        return [dot_tn(left[:, span(i, width // 2)], right).astype(BF) for i in range(2)]

    def split_rows(mine, got, along_y=True):
        if not paired:
            return mine + got, None
        size = mine.shape[0] // 4
        far = (2, 3) if along_y else (1, 3)
        near = (0, 1) if along_y else (0, 2)

        def pick(v, blocks_of):
            return jnp.concatenate([v[span(b, size)] for b in blocks_of], axis=0)

        return pick(mine, far) + pick(got, far), pick(mine, near) + pick(got, near)

    def send_parts(v, swap, *rows_of):
        parts, start = [], 0
        for size in rows_of:
            parts.append(swap(v[start : start + size]))
            start += size
        assert start == v.shape[0]
        return parts

    def halved(total):
        near = total.shape[0] // 2
        return total[near:], total[:near]

    def fold(parts, kept, *late):
        return halved(kept + after(jnp.concatenate(parts, axis=0), late))

    def fold_whole(sent):
        g = sent.reshape(dp_size, 2, -1, sent.shape[-1])
        g = lax.psum_scatter(g, "dp", scatter_dimension=0)
        return g[0] + swap_x(g[1])

    d_hiddens, d_attendeds, d_q_raws, d_lined = [], [], [], []
    feed_gain_grads, query_gain_grads = [], []
    mixed_all = jnp.concatenate(mixeds, axis=0)
    first_cut, second_cut = slice(0, cut_at), slice(cut_at, up_to(2 * units))
    if paired:
        first_far = weight_grad(feed_all, d_units, first_cut, 2, 1, 2)
        first_parts = send_parts(first_far, swap_y, 384, 640)
        second_far = weight_grad(feed_all, after(d_units, first_far), second_cut, 2, 2, 1)
        second_parts = send_parts(second_far, swap_x, 384, 640)
        d_feeds[0] = after(d_feeds[0], second_far)
    for batch in range(batches):
        d_feed = d_feeds[batch]
        if batch == 1:
            d_feed = after(d_feed, d_q_raws[0])
            if paired:
                tied = after(acts, d_q_raws[0])
                down_far = weight_grad(cot_all, tied, slice(0, act_width), 2, 2, 1)
                down_parts = send_parts(down_far, swap_x, 256, 640, 128)
                d_feed = after(d_feed, down_far, last_kv)
        back = hidden_back(table, d_feed, hiddens[batch], cot_in, batch, gains, o_full)
        if paired and batch == 0:
            back, (first_parts[0], second_parts[0]) = beside(
                back, (first_parts[0], second_parts[0])
            )
        if paired and batch == 1:
            back, down_parts[0] = beside(back, down_parts[0])
        d_hidden, d_attended, feed_grad, d_mixed = back
        d_hiddens.append(d_hidden)
        d_attendeds.append(d_attended)
        if batch == 1:
            o_grads = both_grads(jnp.concatenate(d_attendeds, axis=0), mixed_all)
            o_send, o_keep = split_rows(o_grads[0], swap_core(o_grads[1]))
            d_mixed = after(d_mixed, o_send)
            if paired:
                o_parts = send_parts(o_send, swap_y, 256, 128, 128)
        back = attention_backward(
            *kvs[batch],
            queries,
            batch,
            mixeds[batch],
            d_mixed,
            *biases[batch],
            lses[batch],
            q_raw,
            cosine,
            sine,
            query_gain,
        )
        if paired and batch == 0:
            back, (first_parts[1], second_parts[1]) = beside(
                back, (first_parts[1], second_parts[1])
            )
        if paired and batch == 1:
            back, (down_parts[1], o_parts[0]) = beside(back, (down_parts[1], o_parts[0]))
        d_q_raw, d_kv0, d_kv1, query_grad = back
        d_kv = d_kv0 + swap_core(d_kv1)
        last_kv = d_kv
        d_lined.append(lax.psum_scatter(d_kv, "heads", scatter_dimension=0, tiled=True))
        d_q_raws.append(d_q_raw)
        feed_gain_grads.append(feed_grad)
        query_gain_grads.append(query_grad)

    pairs_got = [swap_x(d_lined[0][rows:])]
    d_q_raw_all = jnp.concatenate(d_q_raws, axis=0)
    q_grads = both_grads(after(normed, last_kv), d_q_raw_all)
    if paired:
        q_grads, (down_parts[2], o_parts[1], pairs_got) = beside(
            q_grads, (down_parts[2], o_parts[1], pairs_got)
        )
    q_send, q_keep = split_rows(q_grads[0], swap_core(q_grads[1]), False)
    d_normed_q = query_back(after(d_q_raw_all, q_send), q_full)
    if paired:
        q_parts = send_parts(q_send[: 2 * LANES], swap_x, 128, 128)
        d_normed_q, (q_parts[0], o_parts[2]) = beside(d_normed_q, (q_parts[0], o_parts[2]))
        tied = after(d_units, d_normed_q)
        second_half = weight_grad(feed_all, tied, second_cut, 2, 2, 0)
        second_half, q_parts[1] = beside(second_half, q_parts[1])
        second_half = second_half + jnp.concatenate(second_parts, axis=0)
        second_last = send_parts(second_half[2 * BLOCK :], swap_y, 320, 192)
        d_lined[1] = after(d_lined[1], second_half)
        pairs_got.append(swap_x(d_lined[1][rows:]))
        q_parts += send_parts(after(q_send[2 * LANES :], pairs_got[1]), swap_x, 128, 128)
    else:
        every_unit = slice(0, units_width)
        g_gate_up = scatter_yx(
            unit_order(weight_grad(feed_all, d_units, every_unit, count, 1, 0)), True
        )
        g_down = scatter_yx(
            unit_order(weight_grad(cot_all, acts, slice(0, act_width), count, 1, 0)), False
        )
        pairs_got.append(swap_x(d_lined[1][rows:]))
    d_pair_all = jnp.concatenate(
        [pair[:rows] + got for pair, got in zip(d_lined, pairs_got)], axis=0
    )

    back = input_back(
        table,
        d_pair_all,
        kv_raw,
        cosine,
        sine,
        key_gain,
        d_normed_q,
        *d_hiddens,
        tokens_in,
        gains,
        *kvg,
    )
    if paired:
        back, (q_parts[2], second_last[0]) = beside(back, (q_parts[2], second_last[0]))
    d_kv_raw, key_grad, tokens_grad, attention_grad = back
    query_grad = query_gain_grads[0][0] + query_gain_grads[1][0]
    head_grads = jnp.concatenate(
        [query_grad[:HEAD_SIZE] + query_grad[HEAD_SIZE:], key_grad[0, :HEAD_SIZE]]
    ).reshape(-1, per_head)
    head_row = small_order(
        jnp.pad(head_grads, ((0, 0), (0, small - per_head))).reshape(1, width), False
    )
    gain_grads = jnp.concatenate(
        [
            attention_grad[0:1],
            feed_gain_grads[0][0:1] + feed_gain_grads[1][0:1],
            head_row,
            jnp.zeros((5, width), F32),
        ],
        axis=0,
    )
    kv_grads = key_value_grad(normed, d_kv_raw, gain_grads)
    if paired:
        kv_grads, second_last[1] = beside(kv_grads, second_last[1])
        o_send, o_keep = fold(o_parts, o_keep, d_kv_raw)
        kv_got = swap_core(kv_grads[1])
        kv_sums = [kv_grads[0][span(b)] + kv_got[span(b)] for b in range(4)]
        kv_parts = [swap_x(kv_sums[1]), swap_y(kv_sums[2]), swap_xy(kv_sums[3])]
        o_got = swap_x(after(o_send, kv_sums))
        tied = after(acts, kv_sums)
        half = weight_grad(cot_all, tied, slice(0, act_width), 2, 2, 0)
        half, q_parts[3] = beside(half, q_parts[3])
        q_send, q_keep = fold(q_parts, q_keep)
        q_got = swap_y(q_send)
        half = half + jnp.concatenate(down_parts, axis=0)
        tied = after(d_units, half, q_send)
        first_half = weight_grad(feed_all, tied, first_cut, 2, 1, 0)
        first_half, kv_parts = beside(first_half, kv_parts)
        g_kv = kv_sums[0] + kv_parts[0] + kv_parts[1] + kv_parts[2]
        first_half = first_half + jnp.concatenate(first_parts, axis=0)
        first_last = swap_x(after(first_half[2 * BLOCK :], g_kv))
        down_last = swap_y(after(half[2 * BLOCK :], q_send))
        kv_own, kv_got = line_sends(g_kv, 0)
        g_o = o_keep + after(o_got, first_half, kv_got)
        g_q = q_keep + after(q_got, first_half)
        o_own, o_got = line_sends(g_o, 0)
        q_own, q_got = line_sends(g_q, 1)
        o_got, q_got = beside(o_got, q_got)
        o_final = line_sum(o_own, o_got)
        first_last, down_last = after((first_last, down_last), o_final)
        second_got = jnp.concatenate(second_last, axis=0)
        g_gate_up = jnp.concatenate(
            [first_half[: 2 * BLOCK] + first_last, second_half[: 2 * BLOCK] + second_got], axis=1
        )
        g_down = half[: 2 * BLOCK] + down_last
    else:
        kv_send = kv_grads[0] + swap_core(kv_grads[1])
        g_o, g_q, g_kv = (fold_whole(v) for v in (o_send, q_send, kv_send))
        kv_own, kv_got = line_sends(g_kv, 0)
        q_own, q_got = line_sends(g_q, 1)
        o_final = line_sum(*line_sends(g_o, 0))
    g_kv = line_sum(kv_own, kv_got).astype(F32)
    grad_output = o_final.astype(F32).T
    grad_query = line_sum(q_own, q_got).astype(F32)
    part_rows = g_down.shape[0] // 2
    g_ffn = jnp.concatenate([g_gate_up, g_down], axis=1)
    g_keep = g_ffn[:part_rows]
    g_take = swap_core(g_ffn[part_rows:])
    grads_ffn = []
    for start in (0, units, units_width):
        kept, got = g_keep[:, start : start + units], g_take[:, start : start + units]
        grads_ffn.append(
            jnp.where(
                core == 0,
                jnp.concatenate([kept, got], axis=1),
                jnp.concatenate([got, kept], axis=1),
            ).astype(F32)
        )
    grad_gate, grad_up, grad_down = grads_ffn
    grad_down = grad_down.T

    grad_key_value = (
        g_kv[:, :KV_WIDTH]
        .reshape(small, KEY_VALUE_HEADS, 2, HEAD_SIZE)
        .transpose(0, 2, 1, 3)
        .reshape(small, KV_WIDTH)
    )

    added = [
        lax.psum_scatter(after(v, last_kv), "heads", scatter_dimension=0, tiled=True) for v in added
    ]
    added = after(added, g_o, g_q)
    layer_out = finish_layer(table, *hiddens, *added)

    return (
        from_order(layer_out).reshape(tokens.shape),
        from_order(tokens_grad).reshape(tokens.shape),
        g_kv[:, KV_WIDTH + ATTENTION_GAIN],
        grad_query,
        grad_key_value,
        g_kv[:per_head, KV_WIDTH + HEAD_GAIN],
        grad_output,
        g_kv[:, KV_WIDTH + FEED_GAIN],
        grad_gate,
        grad_up,
        grad_down,
    )


def order_kernel(table, values, out):
    for j in range(values.shape[1] // BLOCK):
        out[:, span(j)] = values[:, place(table, j)]


def order_columns(table, values):
    return kernel_call(
        order_kernel,
        "order_columns",
        (1,),
        [whole(values)],
        fixed_out(values.shape),
        shape(values.shape, values.dtype),
        [],
        0,
        table,
    )(values)


def solution(mesh):
    every = ("dp", "seq", "heads")
    token_spec = P(None, "dp", ("seq", "heads"), None)
    return jax.shard_map(
        on_device,
        mesh=mesh,
        in_specs=(
            token_spec,
            P(None, "dp", None),
            P(every),
            P(("dp", "seq"), "heads"),
            P(every, None),
            P(every),
            P(None, every),
            P(every),
            P(("dp", "seq"), "heads"),
            P(("dp", "seq"), "heads"),
            P("heads", ("dp", "seq")),
            token_spec,
        ),
        out_specs=(
            token_spec,
            token_spec,
            P(every),
            P(("dp", "seq"), "heads"),
            P(every, None),
            P(every),
            P(None, every),
            P(every),
            P(("dp", "seq"), "heads"),
            P(("dp", "seq"), "heads"),
            P("heads", ("dp", "seq")),
        ),
        check_vma=False,
    )
```
